32 devices in a mesh: seq: 8 (over y, x, core), head: 4 (over z).
Axes of the slice: x: 2, y: 2, z: 4, core: 2. Of those that a mesh axis runs over, the one named last changes fastest.
Arguments:
- grad_out: bfloat16 [2048, 8192], P('seq', 'head'), may hold values from -6 to 6
- out_weight: bfloat16 [16384, 8192], P('head', 'seq'), may hold values from -0.046875 to 0.046875
- ssm_input: bfloat16 [2048, 16384], P('seq', 'head'), may hold values from -6 to 6
- step_size: float32 [2048, 128], P('seq', 'head'), may hold values from 0.02 to 0.2
- log_decay: float32 [2048, 128], P('seq', 'head'), may hold values from -1 to 0, as said below
- b_in: bfloat16 [2048, 256], P('seq'), may hold values from -1.5 to 1.5
- c_in: bfloat16 [2048, 256], P('seq'), may hold values from -1.5 to 1.5
- skip: float32 [128], P('head'), may hold values from 0.5 to 1.5
Outputs:
- grad_input: bfloat16 [2048, 16384], P('seq', 'head')
- grad_step: float32 [2048, 128], P('seq', 'head')
- grad_decay: float32 [2048, 128], P('seq', 'head')
- grad_b: float32 [2048, 256], P('seq')
- grad_c: float32 [2048, 256], P('seq')
The draws below stay inside these ranges and needn't reach their ends.
Inputs may be any that keep to these rules, and one draw needn't show every extreme that they name: `log_decay`: every entry is negative.
All inputs are finite; a program needn't handle non-finite values.
Results may differ from the reference program's by a relative error of at most 0.0049.
Values may be sent and summed in bfloat16 or wider, within the bound.
No kernel may reach another device: no remote copies, remote signals or barrier semaphores. Data moves between devices by JAX's collectives and lax.ppermute only.
A program may use at most 128 MiB of HBM per device.

```python
import math
import jax
import jax.numpy as jnp
from jax import lax

D = 8192
SPACE_HEADS = 128
HEAD_DIM = 128
STATE = 256
TOK_DEV = 256
SEQUENCE_TOKENS = 2048
INNER = 16384


def draw_log_decay(key, part):
    random_subkeys = [jax.random.fold_in(key, 11 + draw_index) for draw_index in range(6)]
    slow_share = 0.5
    is_slow = jax.random.uniform(random_subkeys[0], (SPACE_HEADS,)) < slow_share
    fast_rate = jax.random.uniform(random_subkeys[1], (SPACE_HEADS,), minval=1.0 / 50.0, maxval=1.0 / 30.0)
    baseline_rate = jnp.where(is_slow, 0.35 / SEQUENCE_TOKENS, fast_rate)
    block_count = SEQUENCE_TOKENS // TOK_DEV
    block_multiplier = jnp.exp(jax.random.uniform(random_subkeys[2], (block_count, SPACE_HEADS), minval=math.log(0.6), maxval=math.log(1.6)))
    block_multiplier = jnp.repeat(block_multiplier, TOK_DEV, axis=0)
    jaggedness_level = jax.random.uniform(random_subkeys[3], (SEQUENCE_TOKENS, SPACE_HEADS), minval=0.5, maxval=1.5)
    token_positions = jax.random.randint(random_subkeys[4], (3, SPACE_HEADS), 0, SEQUENCE_TOKENS)
    row_indices = lax.broadcasted_iota(jnp.int32, (SEQUENCE_TOKENS, 3, SPACE_HEADS), 0)
    surge_events = jnp.any(row_indices == token_positions[None], axis=1).astype(jnp.float32)
    surge_length = jax.random.uniform(random_subkeys[5], (SEQUENCE_TOKENS, SPACE_HEADS), minval=0.22, maxval=0.69)
    return -(baseline_rate[None, :] * block_multiplier * jaggedness_level + surge_events * surge_length)


def block_scale(own_key, extent, pieces, least, high):
    level, own = 1.0, jax.random.fold_in(own_key, 6)
    for axis_at, shards_of in pieces:
        steps = jnp.exp(jax.random.uniform(jax.random.fold_in(own, axis_at), (shards_of,), jnp.float32, least / len(pieces), high / len(pieces)))
        level = level * jnp.repeat(steps, extent[axis_at] // shards_of).reshape([-1 if axis == axis_at else 1 for axis in range(len(extent))])
    return level


def bell_draw(own_key, shape, spread, most, split=(), dtype=jnp.bfloat16):
    array = jax.random.normal(own_key, shape, jnp.float32) * spread
    if len(split) > 0:
        array = block_scale(own_key, shape, split, -0.22, 0.18) * array
    return jnp.clip(array, min=-most, max=most).astype(dtype)


def setup_inputs(seed: int = 0) -> dict:
    key_of = jax.random.split(jax.random.key(seed), 9)
    return {
        "grad_out": bell_draw(key_of[0], (SEQUENCE_TOKENS, D), 1.0, 6.0, ((0, 8), (1, 4))),
        "out_weight": bell_draw(key_of[1], (INNER, D), INNER ** -0.5, 0.046875, ((0, 4), (1, 8))),
        "ssm_input": bell_draw(key_of[2], (SEQUENCE_TOKENS, INNER), 1.0, 6.0, ((0, 8), (1, 4))),
        "step_size": jnp.clip(jnp.exp(math.log(0.2) - 2.3025851 * jax.random.uniform(key_of[3], (SEQUENCE_TOKENS, SPACE_HEADS), jnp.float32) ** block_scale(key_of[3], (SEQUENCE_TOKENS, SPACE_HEADS), ((0, 8), (1, 4)), -0.2, 0.2)), 0.02, 0.2),
        "log_decay": draw_log_decay(jax.random.fold_in(key_of[8], 71), 0),
        "b_in": bell_draw(key_of[5], (SEQUENCE_TOKENS, STATE), 0.25, 1.5, ((0, 8),)),
        "c_in": bell_draw(key_of[6], (SEQUENCE_TOKENS, STATE), 0.25, 1.5, ((0, 8),)),
        "skip": jnp.clip(0.5 + 1.0 * jax.random.uniform(key_of[7], (SPACE_HEADS,), jnp.float32) ** block_scale(key_of[7], (SPACE_HEADS,), ((0, 4),), -0.2, 0.2), 0.5, 1.5),
    }


HIGH = lax.Precision.HIGHEST

def inner_terms(inputs, strides, running, b_rows, c_rows, skips):
    span = inputs.shape[0]
    row_pos = lax.broadcasted_iota(jnp.int32, (span, span), 0)
    col_pos = lax.broadcasted_iota(jnp.int32, (span, span), 1)
    causal = row_pos >= col_pos
    running_t = running.T
    gaps = running_t[:, :, None] - running_t[:, None, :]
    weights = jnp.exp(jnp.where(causal[None], gaps, -jnp.inf)) * strides.T[:, None, :]
    intersection = jnp.dot(c_rows, b_rows.T, precision=HIGH)
    mixed_sum = jnp.einsum('hts,shp->thp', weights * intersection[None], inputs, precision=HIGH)
    return mixed_sum + skips[None, :, None] * inputs

def carried(c_rows, running, carried_state):
    readout = jnp.einsum('tn,hpn->thp', c_rows, carried_state, precision=HIGH)
    return readout * jnp.exp(running)[:, :, None]

def closing(inputs, strides, b_rows, running, carried_state):
    block_end = running[-1]
    input_scale = strides * jnp.exp(block_end[None, :] - running)
    fresh = jnp.einsum('thp,tn->hpn', inputs * input_scale[:, :, None], b_rows, precision=HIGH)
    return jnp.exp(block_end)[:, None, None] * carried_state + fresh

def block_forward(inputs, strides, decays, b_rows, c_rows, skips, carried_state):
    running = jnp.cumsum(decays, axis=0)
    outputs = inner_terms(inputs, strides, running, b_rows, c_rows, skips) + carried(c_rows, running, carried_state)
    return (outputs, closing(inputs, strides, b_rows, running, carried_state))

def reference(grad_out, out_weight, ssm_input, step_size, log_decay, b_in, c_in, skip):
    summed = lax.dot_general(grad_out, out_weight, (((1,), (1,)), ((), ())), preferred_element_type=jnp.float32)
    grad_y = summed.astype(jnp.bfloat16)
    block_count = SEQUENCE_TOKENS // TOK_DEV

    def by_blocks(values):
        return values.reshape((block_count, TOK_DEV) + values.shape[1:])

    def forward(inputs, strides, decays, b_rows, c_rows):

        def advance(carried_state, block_inputs):
            outputs, ending = block_forward(block_inputs[0], block_inputs[1], block_inputs[2], block_inputs[3], block_inputs[4], skip, carried_state)
            return (ending, outputs)
        initial = jnp.zeros((SPACE_HEADS, HEAD_DIM, STATE), jnp.float32)
        _, outputs = lax.scan(jax.checkpoint(advance), initial, (by_blocks(inputs), by_blocks(strides), by_blocks(decays), by_blocks(b_rows), by_blocks(c_rows)))
        return outputs.reshape(SEQUENCE_TOKENS, SPACE_HEADS, HEAD_DIM)
    inputs = ssm_input.astype(jnp.float32).reshape(SEQUENCE_TOKENS, SPACE_HEADS, HEAD_DIM)
    _, pull_back = jax.vjp(forward, inputs, step_size, log_decay, b_in.astype(jnp.float32), c_in.astype(jnp.float32))
    gradients = pull_back(grad_y.astype(jnp.float32).reshape(SEQUENCE_TOKENS, SPACE_HEADS, HEAD_DIM))
    grad_input = gradients[0].reshape(SEQUENCE_TOKENS, INNER).astype(jnp.bfloat16)
    return (grad_input, gradients[1], gradients[2], gradients[3], gradients[4])
```

```python
import jax
import jax.numpy as jnp
from jax import lax
from jax.experimental import pallas as pl
from jax.experimental.pallas import tpu as pltpu
from jax.sharding import PartitionSpec as P

BF16 = jnp.bfloat16
F32 = jnp.float32
HIGH = lax.Precision.HIGHEST
CHUNKS = 2
NN = (((1,), (0,)), ((), ()))
NT = (((1,), (1,)), ((), ()))
TN = (((0,), (0,)), ((), ()))


def mm(a, b, dims):
    return lax.dot_general(a, b, dims, preferred_element_type=F32)


def halves(a):
    high = a.astype(BF16)
    return high, (a - high.astype(F32)).astype(BF16)


def mm_left(a, b, dims):
    high, low = halves(a)
    return mm(high, b, dims) + mm(low, b, dims)


def mm_right(a, b, dims):
    high, low = halves(b)
    return mm(a, high, dims) + mm(a, low, dims)


def pick(table, head):
    lanes = lax.broadcasted_iota(jnp.int32, table.shape, 1)
    return jnp.sum(jnp.where(lanes == head, table, 0.0), axis=1, keepdims=True)


def place(ref, column, head):
    lanes = lax.broadcasted_iota(jnp.int32, ref.shape, 1)
    ref[...] = jnp.where(lanes == head, column, ref[...])


def states_kernel(v_ref, scale_ref, rows_ref, out_ref):
    head = pl.program_id(0)
    scaled = v_ref[...].astype(F32) * pick(scale_ref[...], head)
    out_ref[0] = mm_left(scaled, rows_ref[...], TN)


def span_states(values, scale, rows):
    span, heads = scale.shape
    width = values.shape[1] // heads
    states = rows.shape[1]
    return pl.pallas_call(
        states_kernel,
        grid=(heads,),
        in_specs=[
            pl.BlockSpec((span, width), lambda h: (0, h)),
            pl.BlockSpec((span, heads), lambda h: (0, 0)),
            pl.BlockSpec((span, states), lambda h: (0, 0)),
        ],
        out_specs=pl.BlockSpec((1, width, states), lambda h: (h, 0, 0)),
        out_shape=jax.ShapeDtypeStruct((heads, width, states), F32),
        compiler_params=pltpu.CompilerParams(vmem_limit_bytes=32 << 20),
        cost_estimate=pl.CostEstimate(
            flops=4 * span * heads * width * states,
            bytes_accessed=heads * width * (2 * span + 4 * states),
            transcendentals=0,
        ),
    )(values, scale, rows)


def inner_kernel(
    x_ref, y_ref, b_ref, c_ref, run_ref, run_t_ref, step_ref, skip_ref, state_ref,
    partial_ref, grad_b_ref, grad_c_ref, col_ref, carry_ref, row_ref,
    cross, mix, grad_c_acc,
):
    head = pl.program_id(0)
    span = x_ref.shape[0]

    @pl.when(head == 0)
    def _():
        cross[...] = mm(b_ref[...], c_ref[...], NT)
        mix[...] = jnp.zeros_like(mix)
        grad_c_acc[...] = jnp.zeros_like(grad_c_acc)
        col_ref[...] = jnp.zeros_like(col_ref)
        carry_ref[...] = jnp.zeros_like(carry_ref)

    x = x_ref[...]
    y = y_ref[...]
    run_col = pick(run_ref[...], head)
    step_col = pick(step_ref[...], head)
    run_row = run_t_ref[pl.ds(head, 1), :]
    source = lax.broadcasted_iota(jnp.int32, (span, span), 0)
    target = lax.broadcasted_iota(jnp.int32, (span, span), 1)
    decay = jnp.exp(jnp.where(source <= target, run_row - run_col, -jnp.inf))
    weights = decay * cross[...]
    pairs = mm(x, y, NT)
    mix[...] += decay * pairs * step_col
    terms = weights * pairs
    place(col_ref, jnp.sum(terms, axis=1, keepdims=True), head)
    row_ref[pl.ds(head, 1), :] = jnp.sum(terms * step_col, axis=0, keepdims=True)
    inner = mm_left(weights, y, NN)
    partial_ref[...] = step_col * inner + skip_ref[pl.ds(head, 1), :] * y.astype(F32)
    readout = mm_right(y, state_ref[0], NN) * jnp.exp(run_col)
    grad_c_acc[...] += readout
    place(
        carry_ref,
        jnp.sum(readout * c_ref[...].astype(F32), axis=1, keepdims=True),
        head,
    )

    @pl.when(head == pl.num_programs(0) - 1)
    def _():
        high, low = halves(mix[...])
        grad_b_ref[...] = mm(high, c_ref[...], NN) + mm(low, c_ref[...], NN)
        grad_c_ref[...] = (
            grad_c_acc[...] + mm(high, b_ref[...], TN) + mm(low, b_ref[...], TN)
        )


def inner_part(x, y, b, c, running, running_t, steps, skip_rows, incoming):
    span, heads = steps.shape
    width = x.shape[1] // heads
    states = b.shape[1]
    whole = lambda *shape: pl.BlockSpec(shape, lambda h: (0,) * len(shape))
    block = pl.BlockSpec((span, width), lambda h: (0, h))
    return pl.pallas_call(
        inner_kernel,
        grid=(heads,),
        in_specs=[
            block,
            block,
            whole(span, states),
            whole(span, states),
            whole(span, heads),
            whole(heads, span),
            whole(span, heads),
            whole(heads, width),
            pl.BlockSpec((1, width, states), lambda h: (h, 0, 0)),
        ],
        out_specs=[
            block,
            whole(span, states),
            whole(span, states),
            whole(span, heads),
            whole(span, heads),
            whole(heads, span),
        ],
        out_shape=[
            jax.ShapeDtypeStruct((span, heads * width), F32),
            jax.ShapeDtypeStruct((span, states), F32),
            jax.ShapeDtypeStruct((span, states), F32),
            jax.ShapeDtypeStruct((span, heads), F32),
            jax.ShapeDtypeStruct((span, heads), F32),
            jax.ShapeDtypeStruct((heads, span), F32),
        ],
        scratch_shapes=[
            pltpu.VMEM((span, span), F32),
            pltpu.VMEM((span, span), F32),
            pltpu.VMEM((span, states), F32),
        ],
        compiler_params=pltpu.CompilerParams(vmem_limit_bytes=32 << 20),
        cost_estimate=pl.CostEstimate(
            flops=10 * span * heads * width * states,
            bytes_accessed=8 * span * heads * width + 4 * heads * width * states,
            transcendentals=heads * span * span,
        ),
    )(x, y, b, c, running, running_t, steps, skip_rows, incoming)


def outer_kernel(
    x_ref, part_ref, b_ref, state_ref, grad_state_ref, tail_ref, step_ref, run_ref,
    col_ref, carry_ref, row_ref, grad_b_in_ref,
    grad_x_ref, grad_b_ref, grad_step_ref, grad_decay_ref,
    overlap, late,
):
    head = pl.program_id(0)

    @pl.when(head == 0)
    def _():
        grad_b_ref[...] = grad_b_in_ref[...]
        late[...] = jnp.zeros_like(late)
        overlap[...] = jnp.zeros_like(overlap)

    tail_col = pick(tail_ref[...], head)
    step_col = pick(step_ref[...], head)
    grad_state = grad_state_ref[0]
    b = b_ref[...]
    spread = mm_right(x_ref[...], grad_state, NN) * tail_col
    grad_b_ref[...] += spread * step_col
    place(late, jnp.sum(spread * b.astype(F32), axis=1, keepdims=True), head)
    outer = mm_right(b, grad_state, NT)
    grad_x_ref[...] = (part_ref[...] + (step_col * tail_col) * outer).astype(BF16)
    shared = jnp.sum(grad_state * state_ref[0], axis=0, keepdims=True)
    place(overlap, jnp.sum(shared, axis=1, keepdims=True), head)

    @pl.when(head == pl.num_programs(0) - 1)
    def _():
        span = step_ref.shape[0]
        steps = step_ref[...]
        grad_step = col_ref[...] + late[...]
        grad_step_ref[...] = grad_step
        change = carry_ref[...] + row_ref[...].T - steps * grad_step
        end = jnp.exp(run_ref[span - 1 : span, :]) * overlap[...]
        end += jnp.sum(steps * late[...], axis=0, keepdims=True)
        from_here = lax.broadcasted_iota(jnp.int32, (span, span), 0) <= (
            lax.broadcasted_iota(jnp.int32, (span, span), 1)
        )
        grad_decay_ref[...] = end + lax.dot_general(
            from_here.astype(F32), change, NN, precision=HIGH, preferred_element_type=F32
        )


def outer_part(x, part, b, state, grad_state, tail, steps, running, cols, carries, rows, grad_b):
    span, heads = steps.shape
    width = x.shape[1] // heads
    states = b.shape[1]
    whole = lambda *shape: pl.BlockSpec(shape, lambda h: (0,) * len(shape))
    block = pl.BlockSpec((span, width), lambda h: (0, h))
    per_head = pl.BlockSpec((1, width, states), lambda h: (h, 0, 0))
    table = whole(span, heads)
    return pl.pallas_call(
        outer_kernel,
        grid=(heads,),
        in_specs=[
            block, block, whole(span, states), per_head, per_head, table, table, table,
            table, table, whole(heads, span), whole(span, states),
        ],
        out_specs=[block, whole(span, states), table, table],
        out_shape=[
            jax.ShapeDtypeStruct((span, heads * width), BF16),
            jax.ShapeDtypeStruct((span, states), F32),
            jax.ShapeDtypeStruct((span, heads), F32),
            jax.ShapeDtypeStruct((span, heads), F32),
        ],
        scratch_shapes=[pltpu.VMEM((1, heads), F32), pltpu.VMEM((span, heads), F32)],
        compiler_params=pltpu.CompilerParams(vmem_limit_bytes=32 << 20),
        cost_estimate=pl.CostEstimate(
            flops=4 * span * heads * width * states,
            bytes_accessed=8 * span * heads * width + 8 * heads * width * states,
            transcendentals=0,
        ),
    )(x, part, b, state, grad_state, tail, steps, running, cols, carries, rows, grad_b)


def across(value, hop, chips):
    pairs = [(2 * i + core, 2 * (i ^ hop) + core) for i in range(chips) for core in range(2)]
    return lax.ppermute(value, "seq", pairs)


def other_core(value, chips):
    return lax.ppermute(value, "seq", [(i, i ^ 1) for i in range(2 * chips)])


def sum_over_heads(value):
    count = lax.axis_size("head")
    here = lax.axis_index("head")
    shares = value.reshape((count, value.shape[0] // count) + value.shape[1:])
    shift = lambda hop: [(i, (i + hop) % count) for i in range(count)]
    share = lambda hop: lax.dynamic_index_in_dim(shares, (here + hop) % count, 0, False)
    total = share(0)
    for hop in range(1, count):
        total = total + lax.ppermute(share(hop), "head", shift(hop))
    parts = [total] + [lax.ppermute(total, "head", shift(hop)) for hop in range(1, count)]
    stacked = jnp.stack(parts)
    ordered = [
        lax.dynamic_index_in_dim(stacked, (here - i) % count, 0, False) for i in range(count)
    ]
    return jnp.concatenate(ordered, axis=0)


def project(grad_out, out_weight, chips, chip, core):
    span = grad_out.shape[0]
    width = out_weight.shape[1]
    half = out_weight.shape[0] // 2
    weights = jnp.concatenate([out_weight, other_core(out_weight, chips)], axis=1)
    lanes = [weights[:half], weights[half:]]
    bits = [1 << i for i in range(chips.bit_length() - 1)]
    orders = [bits, bits[::-1]]
    rows = span // CHUNKS
    done = []
    for chunk in range(CHUNKS):
        full = lax.all_gather(
            grad_out[chunk * rows : (chunk + 1) * rows], "head", axis=1, tiled=True
        )
        blocks = []
        for hop in range(chips):
            first = 2 * (chip ^ hop)
            block = jnp.concatenate(
                [
                    lax.dynamic_slice_in_dim(full, (first + core) * width, width, 1),
                    lax.dynamic_slice_in_dim(full, (first + 1 - core) * width, width, 1),
                ],
                axis=1,
            )
            blocks.append(across(block, hop, chips) if hop else block)
        pieces = []
        for lane, order in zip(lanes, orders):
            hops = [0]
            for bit in order[::-1]:
                hops = hops + [hop | bit for hop in hops]
            middle = chips // 2

            def partial(which):
                left = jnp.concatenate([blocks[hop] for hop in which], axis=0)
                return mm(left, lane, NT)

            send = partial(hops[middle:]).astype(BF16)
            keep = partial(hops[:middle])
            for bit in order:
                keep = keep + across(send, bit, chips).astype(F32)
                size = keep.shape[0] // 2
                if size >= rows:
                    send = keep[size:].astype(BF16)
                    keep = keep[:size]
            pieces.append(keep.astype(BF16))
        done.append(jnp.concatenate(pieces, axis=1))
    return jnp.concatenate(done, axis=0)


def exchange(states, ends, chips, chip, core, reverse):
    half = states.shape[0] // 2
    mine = lax.dynamic_slice_in_dim(states, core * half, half, 0)
    theirs = other_core(
        lax.dynamic_slice_in_dim(states, (1 - core) * half, half, 0), chips
    )
    ends = lax.dynamic_slice_in_dim(ends, core * half, half, 1)
    by_chip = ends.reshape(chips, 2, half)
    own_ends = lax.dynamic_index_in_dim(by_chip, chip, 0, False)
    scale = lambda logs, value: jnp.exp(logs)[:, None, None] * value
    near_first = (core == 0) != reverse
    first = jnp.where(near_first, mine, theirs)
    second = jnp.where(near_first, theirs, mine)
    first_end, second_end = (own_ends[1], own_ends[0]) if reverse else (own_ends[0], own_ends[1])
    both = (scale(second_end, first) + second).astype(BF16)
    chip_ends = by_chip[:, 0] + by_chip[:, 1]
    index = jnp.arange(chips)[:, None]
    total = jnp.zeros_like(first)
    for hop in range(1, chips):
        source = chip ^ hop
        before = source > chip if reverse else source < chip
        low = jnp.minimum(chip, source)
        high = jnp.maximum(chip, source)
        between = jnp.sum(jnp.where((index > low) & (index < high), chip_ends, 0.0), axis=0)
        pairs = [
            (2 * (i ^ hop) + c, 2 * i + c)
            for i in range(chips)
            for c in range(2)
            if ((i ^ hop) > i) == reverse
        ]
        arrived = lax.ppermute(both, "seq", pairs).astype(F32)
        total = total + scale(jnp.where(before, between, -jnp.inf), arrived)
    after = scale(first_end, total) + first
    for_mine = jnp.where(near_first, total, after)
    for_theirs = jnp.where(near_first, after, total)
    arrived = other_core(for_theirs, chips)
    return jnp.where(
        core == 0,
        jnp.concatenate([for_mine, arrived], axis=0),
        jnp.concatenate([arrived, for_mine], axis=0),
    )


def local(grad_out, out_weight, ssm_input, step_size, log_decay, b_in, c_in, skip):
    place_on_seq = lax.axis_index("seq")
    chips = lax.axis_size("seq") // 2
    chip, core = place_on_seq // 2, place_on_seq % 2
    span, heads = step_size.shape
    width = ssm_input.shape[1] // heads
    upto = jnp.tril(jnp.ones((span, span), F32))
    running = jnp.dot(upto, log_decay, precision=HIGH)
    running_t = running.T
    tail = jnp.exp(running[-1:] - running)
    ends = lax.all_gather(running[-1], "seq")
    skip_rows = jnp.broadcast_to(skip[:, None], (heads, width))

    own_states = span_states(ssm_input, step_size * tail, b_in)
    incoming = exchange(own_states, ends, chips, chip, core, False)

    grad_y = project(grad_out, out_weight, chips, chip, core)
    own_grads = span_states(grad_y, jnp.exp(running), c_in)
    outgoing = exchange(own_grads, ends, chips, chip, core, True)
    part, grad_b, grad_c, cols, carries, rows = inner_part(
        ssm_input, grad_y, b_in, c_in, running, running_t, step_size, skip_rows, incoming
    )
    grad_c = sum_over_heads(grad_c)
    grad_input, grad_b, grad_step, grad_decay = outer_part(
        ssm_input, part, b_in, incoming, outgoing, tail, step_size, running,
        cols, carries, rows, grad_b,
    )
    grad_b = sum_over_heads(grad_b)
    return (grad_input, grad_step, grad_decay, grad_b, grad_c)


def solution(mesh):
    in_specs = (
        P("seq", "head"),
        P("head", "seq"),
        P("seq", "head"),
        P("seq", "head"),
        P("seq", "head"),
        P("seq", None),
        P("seq", None),
        P("head"),
    )
    out_specs = (
        P("seq", "head"),
        P("seq", "head"),
        P("seq", "head"),
        P("seq", None),
        P("seq", None),
    )
    return jax.shard_map(local, mesh=mesh, in_specs=in_specs, out_specs=out_specs, check_vma=False)
```

```python
import jax
import jax.numpy as jnp
from jax import lax
from jax.experimental import pallas as pl
from jax.experimental.pallas import tpu as pltpu
from jax.sharding import PartitionSpec as P

BF16 = jnp.bfloat16
F32 = jnp.float32
HIGH = lax.Precision.HIGHEST
CHUNK_ROWS = 64
GROUP = 8
NN = (((1,), (0,)), ((), ()))
NT = (((1,), (1,)), ((), ()))
TN = (((0,), (0,)), ((), ()))
PARAMS = pltpu.CompilerParams(vmem_limit_bytes=48 << 20)


def mm(a, b, dims):
    return lax.dot_general(a, b, dims, preferred_element_type=F32)


def halves(a):
    high = a.astype(BF16)
    return high, (a - high.astype(F32)).astype(BF16)


def mm_left(a, b, dims):
    high, low = halves(a)
    return mm(high, b, dims) + mm(low, b, dims)


def mm_right(a, b):
    width = b.shape[1]
    both = mm(a, jnp.concatenate(halves(b), axis=1), NN)
    return both[:, :width] + both[:, width:]


def mm_wide(a, b):
    b = b.astype(BF16)
    return mm(jnp.concatenate(halves(a), axis=1), jnp.concatenate([b, b], axis=1), NT)


def whole(*shape):
    return pl.BlockSpec(shape, lambda i, at: (0,) * len(shape))


def cost(flops, size, exps=0):
    return pl.CostEstimate(flops=flops, bytes_accessed=size, transcendentals=exps)


def states_kernel(at_ref, v_ref, scale_ref, rows_ref, out_ref):
    del at_ref
    group = scale_ref.shape[2]
    width = v_ref.shape[1] // group
    for j in range(group):
        scaled = v_ref[:, j * width : (j + 1) * width].astype(F32) * scale_ref[0, :, j : j + 1]
        out_ref[j] = mm_right(rows_ref[...], scaled)


def span_states(values, scale, rows_t, at, count):
    groups, span, group = scale.shape
    width = values.shape[1] // (groups * group)
    states = rows_t.shape[0]
    return pl.pallas_call(
        states_kernel,
        grid_spec=pltpu.PrefetchScalarGridSpec(
            num_scalar_prefetch=1,
            grid=(count,),
            in_specs=[
                pl.BlockSpec((span, group * width), lambda i, at: (0, at[0] + i)),
                pl.BlockSpec((1, span, group), lambda i, at: (at[0] + i, 0, 0)),
                whole(states, span),
            ],
            out_specs=pl.BlockSpec((group, states, width), lambda i, at: (i, 0, 0)),
        ),
        out_shape=jax.ShapeDtypeStruct((count * group, states, width), F32),
        compiler_params=PARAMS,
        cost_estimate=cost(
            4 * span * count * group * width * states,
            count * group * width * (2 * span + 4 * states),
        ),
    )(at, values, scale, rows_t)


def inner_kernel(
    at_ref, x_ref, y_ref, b_ref, c_ref, run_ref, run_t_ref, step_ref, skip_ref, state_ref,
    partial_ref, grad_b_ref, grad_c_ref, col_ref, carry_ref,
    cross, mix, grad_c_acc, rows,
):
    del at_ref
    index = pl.program_id(0)
    group = step_ref.shape[2]
    span = x_ref.shape[0]
    width = x_ref.shape[1] // group

    @pl.when(index == 0)
    def _():
        cross[...] = mm(b_ref[...], c_ref[...], NT)
        mix[...] = jnp.zeros_like(mix)
        grad_c_acc[...] = jnp.zeros_like(grad_c_acc)

    source = lax.broadcasted_iota(jnp.int32, (span, span), 0)
    target = lax.broadcasted_iota(jnp.int32, (span, span), 1)
    causal = source <= target
    for j in range(group):
        columns = slice(j * width, (j + 1) * width)
        x = x_ref[:, columns]
        y = y_ref[:, columns]
        run_col = run_ref[0, :, j : j + 1]
        step_col = step_ref[0, :, j : j + 1]
        run_row = run_t_ref[0, j : j + 1, :]
        decay = jnp.exp(jnp.where(causal, run_row - run_col, -jnp.inf))
        weights = decay * cross[...]
        pairs = mm(x, y, NT)
        mix[...] += decay * pairs * step_col
        terms = weights * pairs
        col_ref[0, :, j : j + 1] = jnp.sum(terms, axis=1, keepdims=True)
        rows[j : j + 1, :] = jnp.sum(terms * step_col, axis=0, keepdims=True)
        inner = mm_left(weights, y, NN)
        y_wide = y.astype(F32)
        partial_ref[:, columns] = step_col * inner + skip_ref[0, j : j + 1, :] * y_wide
        state = state_ref[j]
        scaled = y_wide * jnp.exp(run_col)
        grad_c_acc[...] += mm_wide(scaled, state)
        carry_ref[0, :, j : j + 1] = jnp.sum(
            scaled * mm_right(c_ref[...], state), axis=1, keepdims=True
        )
    carry_ref[0] += rows[...].T

    @pl.when(index == pl.num_programs(0) - 1)
    def _():
        high, low = halves(mix[...])
        grad_b_ref[...] = mm(high, c_ref[...], NN) + mm(low, c_ref[...], NN)
        grad_c_ref[...] = (
            grad_c_acc[...] + mm(high, b_ref[...], TN) + mm(low, b_ref[...], TN)
        )


def inner_part(x, y, b, c, running, running_t, steps, skip_rows, incoming):
    groups, span, group = steps.shape
    heads = groups * group
    width = x.shape[1] // heads
    states = b.shape[1]
    block = pl.BlockSpec((span, group * width), lambda i, at: (0, i))
    table = pl.BlockSpec((1, span, group), lambda i, at: (i, 0, 0))
    return pl.pallas_call(
        inner_kernel,
        grid_spec=pltpu.PrefetchScalarGridSpec(
            num_scalar_prefetch=1,
            grid=(groups,),
            in_specs=[
                block,
                block,
                whole(span, states),
                whole(span, states),
                table,
                pl.BlockSpec((1, group, span), lambda i, at: (i, 0, 0)),
                table,
                pl.BlockSpec((1, group, width), lambda i, at: (i, 0, 0)),
                pl.BlockSpec((group, states, width), lambda i, at: (i, 0, 0)),
            ],
            out_specs=[block, whole(span, states), whole(span, states), table, table],
            scratch_shapes=[
                pltpu.VMEM((span, span), F32),
                pltpu.VMEM((span, span), F32),
                pltpu.VMEM((span, states), F32),
                pltpu.VMEM((group, span), F32),
            ],
        ),
        out_shape=[
            jax.ShapeDtypeStruct((span, heads * width), F32),
            jax.ShapeDtypeStruct((span, states), F32),
            jax.ShapeDtypeStruct((span, states), F32),
            jax.ShapeDtypeStruct((groups, span, group), F32),
            jax.ShapeDtypeStruct((groups, span, group), F32),
        ],
        compiler_params=PARAMS,
        cost_estimate=cost(
            14 * span * heads * width * states,
            8 * span * heads * width + 4 * heads * width * states,
            heads * span * span,
        ),
    )(jnp.zeros((1,), jnp.int32), x, y, b, c, running, running_t, steps, skip_rows, incoming)


def outer_kernel(
    at_ref, x_ref, part_ref, b_ref, state_ref, grad_state_ref, run_ref, step_ref,
    col_ref, carry_ref, grad_b_in_ref, *rest,
):
    del at_ref
    grad_x_ref, grad_b_ref, grad_step_ref, grad_decay_ref, late, overlap = rest[-6:]
    group = step_ref.shape[2]
    span = x_ref.shape[0]
    width = x_ref.shape[1] // group

    @pl.when(pl.program_id(0) == 0)
    def _():
        grad_b_ref[...] = grad_b_in_ref[...]

    running = run_ref[0]
    end = running[span - 1 : span, :]
    tails = jnp.exp(end - running)
    steps = step_ref[0]
    for j in range(group):
        columns = slice(j * width, (j + 1) * width)
        tail_col = tails[:, j : j + 1]
        step_col = steps[:, j : j + 1]
        grad_state = grad_state_ref[j]
        x = x_ref[:, columns].astype(F32)
        outer = mm_right(b_ref[...], grad_state) * tail_col
        late[:, j : j + 1] = jnp.sum(x * outer, axis=1, keepdims=True)
        grad_x_ref[:, columns] = (part_ref[:, columns] + step_col * outer).astype(BF16)
        grad_b_ref[...] += mm_wide(x * (step_col * tail_col), grad_state)
        shared = jnp.sum(grad_state * state_ref[j], axis=0, keepdims=True)
        overlap[:, j : j + 1] = jnp.sum(shared, axis=1, keepdims=True)

    grad_step = col_ref[0] + late[...]
    grad_step_ref[0] = grad_step
    change = carry_ref[0] - steps * grad_step
    last = jnp.exp(end) * overlap[...] + jnp.sum(steps * late[...], axis=0, keepdims=True)
    source = lax.broadcasted_iota(jnp.int32, (span, span), 0)
    target = lax.broadcasted_iota(jnp.int32, (span, span), 1)
    from_here = (source <= target).astype(BF16)
    high, low = halves(change)
    lowest = (change - high.astype(F32) - low.astype(F32)).astype(BF16)
    grad_decay_ref[0] = last + (
        mm(from_here, high, NN) + mm(from_here, low, NN) + mm(from_here, lowest, NN)
    )


def outer_part(x, part, b, state, grad_state, running, steps, cols, carries, grad_b, at, before):
    groups, span, group = steps.shape
    heads = groups * group
    count = grad_state.shape[0] // group
    width = x.shape[1] // heads
    states = b.shape[1]
    block = pl.BlockSpec((span, group * width), lambda i, at: (0, at[0] + i))
    table = pl.BlockSpec((1, span, group), lambda i, at: (at[0] + i, 0, 0))
    held = [] if before is None else list(before)
    return pl.pallas_call(
        outer_kernel,
        grid_spec=pltpu.PrefetchScalarGridSpec(
            num_scalar_prefetch=1,
            grid=(count,),
            in_specs=[
                block,
                block,
                whole(span, states),
                pl.BlockSpec((group, states, width), lambda i, at: (at[0] + i, 0, 0)),
                pl.BlockSpec((group, states, width), lambda i, at: (i, 0, 0)),
                table,
                table,
                table,
                table,
                whole(span, states),
            ]
            + [pl.BlockSpec(memory_space=pl.ANY)] * len(held),
            out_specs=[block, whole(span, states), table, table],
            scratch_shapes=[pltpu.VMEM((span, group), F32), pltpu.VMEM((1, group), F32)],
        ),
        out_shape=[
            jax.ShapeDtypeStruct((span, heads * width), BF16),
            jax.ShapeDtypeStruct((span, states), F32),
            jax.ShapeDtypeStruct((groups, span, group), F32),
            jax.ShapeDtypeStruct((groups, span, group), F32),
        ],
        input_output_aliases={11: 0, 12: 2, 13: 3} if held else {},
        compiler_params=PARAMS,
        cost_estimate=cost(
            8 * span * count * group * width * states,
            count * group * width * (8 * span + 8 * states),
        ),
    )(at, x, part, b, state, grad_state, running, steps, cols, carries, grad_b, *held)


def project_kernel(hops, at_ref, *refs):
    count = len(hops)
    pieces, (own_ref, other_ref, send_ref, keep_ref, left) = refs[:count], refs[count:]
    rows = pieces[0].shape[0]
    depth = own_ref.shape[1]

    @pl.when(pl.program_id(0) == 0)
    def _():
        first = pl.multiple_of(at_ref[0] * depth, depth)
        second = pl.multiple_of((1 - at_ref[0]) * depth, depth)
        for place, hop in enumerate(hops):
            left[pl.ds(place * rows, rows), :depth] = pieces[hop][:, pl.ds(first, depth)]
            left[pl.ds(place * rows, rows), depth:] = pieces[hop][:, pl.ds(second, depth)]

    total = mm(left[:, :depth], own_ref[...], NT) + mm(left[:, depth:], other_ref[...], NT)
    middle = rows * (count // 2)
    keep_ref[...] = total[:middle]
    send_ref[...] = total[middle:].astype(BF16)


def partial_sums(pieces, hops, own, other, lane, core):
    rows, both = pieces[0].shape
    depth = own.shape[1]
    half = own.shape[0] // 2
    tile = min(512, half)
    steps = half // tile
    middle = rows * (len(hops) // 2)
    weight = pl.BlockSpec((tile, depth), lambda i, at: (lane * steps + i, 0))
    return pl.pallas_call(
        lambda *refs: project_kernel(hops, *refs),
        grid_spec=pltpu.PrefetchScalarGridSpec(
            num_scalar_prefetch=1,
            grid=(steps,),
            in_specs=[whole(rows, both)] * len(hops) + [weight, weight],
            out_specs=[pl.BlockSpec((middle, tile), lambda i, at: (0, i))] * 2,
            scratch_shapes=[pltpu.VMEM((rows * len(hops), both), BF16)],
        ),
        out_shape=[
            jax.ShapeDtypeStruct((middle, half), BF16),
            jax.ShapeDtypeStruct((middle, half), F32),
        ],
        compiler_params=PARAMS,
        cost_estimate=cost(
            2 * rows * len(hops) * both * half, 2 * both * half + 6 * middle * half
        ),
    )(core, *pieces, own, other)


def across(value, hop, chips):
    pairs = [(2 * i + core, 2 * (i ^ hop) + core) for i in range(chips) for core in range(2)]
    return lax.ppermute(value, "seq", pairs)


def other_core(value, chips):
    return lax.ppermute(value, "seq", [(i, i ^ 1) for i in range(2 * chips)])


def orders(chips):
    bits = [1 << i for i in range(chips.bit_length() - 1)]
    return [bits, bits[::-1]]


def sum_over_heads(value):
    count = lax.axis_size("head")
    here = lax.axis_index("head")
    shares = value.reshape((count, value.shape[0] // count) + value.shape[1:])
    shift = lambda hop: [(i, (i + hop) % count) for i in range(count)]
    share = lambda hop: lax.dynamic_index_in_dim(shares, (here + hop) % count, 0, False)
    total = share(0)
    for hop in range(1, count):
        total = total + lax.ppermute(share(hop), "head", shift(hop))
    parts = [total] + [lax.ppermute(total, "head", shift(hop)) for hop in range(1, count)]
    stacked = jnp.stack(parts)
    ordered = [
        lax.dynamic_index_in_dim(stacked, (here - i) % count, 0, False) for i in range(count)
    ]
    return jnp.concatenate(ordered, axis=0)


def project(grad_out, out_weight, chips, chip, core, after):
    span = grad_out.shape[0]
    both = 2 * out_weight.shape[1]
    other = other_core(out_weight, chips)
    core_at = core.astype(jnp.int32).reshape(1)
    rows = min(CHUNK_ROWS, span)
    done = []
    for start in range(0, span, rows):
        full = lax.all_gather(grad_out[start : start + rows], "head", axis=1, tiled=True)
        base = chip if start == 0 else chip + after
        blocks = []
        for hop in range(chips):
            block = lax.dynamic_slice_in_dim(full, (base ^ hop) * both, both, 1)
            blocks.append(across(block, hop, chips) if hop else block)
        pieces = []
        for lane, order in enumerate(orders(chips)):
            hops = [0]
            for bit in order[::-1]:
                hops = hops + [hop | bit for hop in hops]
            send, keep = partial_sums(blocks, hops, out_weight, other, lane, core_at)
            for bit in order:
                keep = keep + across(send, bit, chips).astype(F32)
                size = keep.shape[0] // 2
                if size >= rows:
                    send = keep[size:].astype(BF16)
                    keep = keep[:size]
            pieces.append(keep.astype(BF16))
        done.append(jnp.concatenate(pieces, axis=1))
    return jnp.concatenate(done, axis=0)


def exchange(mine, to_other, ends, chips, chip, core, reverse):
    half = mine.shape[0]
    theirs = other_core(to_other, chips)
    ends = lax.dynamic_slice_in_dim(ends, core * half, half, 1)
    by_chip = ends.reshape(chips, 2, half)
    own_ends = lax.dynamic_index_in_dim(by_chip, chip, 0, False)
    chip_ends = by_chip[:, 0] + by_chip[:, 1]
    index = jnp.arange(chips)[:, None]
    scale = lambda logs, value: jnp.exp(logs)[:, None, None] * value.astype(F32)

    def carry(source, target):
        before = source > target if reverse else source < target
        inside = (index > jnp.minimum(source, target)) & (index < jnp.maximum(source, target))
        between = jnp.sum(jnp.where(inside, chip_ends, 0.0), axis=0)
        return jnp.where(before, between, -jnp.inf)

    near_first = (core == 0) != reverse
    first = jnp.where(near_first, mine, theirs)
    second = jnp.where(near_first, theirs, mine)
    first_end, second_end = (own_ends[1], own_ends[0]) if reverse else (own_ends[0], own_ends[1])
    chip_state = scale(second_end, first) + second
    totals = []
    for lane, order in enumerate(orders(chips)):
        heads = slice(lane * (half // 2), (lane + 1) * (half // 2))
        items = {0: chip_state[heads].astype(BF16)}
        for bit in order[:-1]:
            items.update({o | bit: across(item, bit, chips) for o, item in items.items()})
        bit = order[-1]
        gather = lambda target: sum(
            scale(carry(chip ^ o, target)[heads], item) for o, item in items.items()
        )
        arrived = across(gather(chip ^ bit).astype(BF16), bit, chips)
        totals.append(gather(chip) + arrived.astype(F32))
    total = jnp.concatenate(totals, axis=0)
    after = scale(first_end, total) + first
    for_mine = jnp.where(near_first, total, after)
    for_theirs = jnp.where(near_first, after, total)
    return for_mine, other_core(for_theirs, chips)


def local(grad_out, out_weight, ssm_input, step_size, log_decay, b_in, c_in, skip):
    place_on_seq = lax.axis_index("seq")
    chips = lax.axis_size("seq") // 2
    chip, core = place_on_seq // 2, place_on_seq % 2
    span, heads = step_size.shape
    width = ssm_input.shape[1] // heads
    group = min(GROUP, heads // 2)
    groups = heads // group
    by_group = lambda t: t.reshape(span, groups, group).transpose(1, 0, 2)
    flat = lambda t: t.transpose(1, 0, 2).reshape(span, heads)
    mine_at = (core * (groups // 2)).astype(jnp.int32).reshape(1)
    other_at = ((1 - core) * (groups // 2)).astype(jnp.int32).reshape(1)

    upto = jnp.tril(jnp.ones((span, span), F32))
    running = jnp.dot(upto, log_decay, precision=HIGH)
    ends = lax.all_gather(running[-1], "seq")
    tail = jnp.exp(running[-1:] - running)
    running_g = by_group(running)
    running_t = running.T.reshape(groups, group, span)
    steps_g = by_group(step_size)
    skip_rows = jnp.broadcast_to(skip.reshape(groups, group, 1), (groups, group, width))

    def states(values, scale, rows, reverse):
        rows_t = rows.T
        to_other = span_states(values, scale, rows_t, other_at, groups // 2)
        mine = span_states(values, scale, rows_t, mine_at, groups // 2)
        return exchange(mine, to_other, ends, chips, chip, core, reverse)

    for_mine, for_other = states(ssm_input, by_group(step_size * tail), b_in, False)
    incoming = jnp.where(
        core == 0,
        jnp.concatenate([for_mine, for_other], axis=0),
        jnp.concatenate([for_other, for_mine], axis=0),
    )
    corner = incoming[0, 0, 0]
    after = (corner != corner).astype(chip.dtype)

    grad_y = project(grad_out, out_weight, chips, chip, core, after)
    out_mine, out_other = states(grad_y, by_group(jnp.exp(running)), c_in, True)
    part, grad_b, grad_c, cols, carries = inner_part(
        ssm_input, grad_y, b_in, c_in, running_g, running_t, steps_g, skip_rows, incoming
    )
    grad_c = sum_over_heads(grad_c)
    shared = (running_g, steps_g, cols, carries)
    grad_x, grad_b, grad_step, grad_decay = outer_part(
        ssm_input, part, b_in, incoming, out_mine, *shared, grad_b, mine_at, None
    )
    grad_x, grad_b, grad_step, grad_decay = outer_part(
        ssm_input, part, b_in, incoming, out_other, *shared, grad_b, other_at,
        (grad_x, grad_step, grad_decay),
    )
    grad_b = sum_over_heads(grad_b)
    return (grad_x, flat(grad_step), flat(grad_decay), grad_b, grad_c)


def solution(mesh):
    in_specs = (
        P("seq", "head"),
        P("head", "seq"),
        P("seq", "head"),
        P("seq", "head"),
        P("seq", "head"),
        P("seq", None),
        P("seq", None),
        P("head"),
    )
    out_specs = (
        P("seq", "head"),
        P("seq", "head"),
        P("seq", "head"),
        P("seq", None),
        P("seq", None),
    )
    return jax.shard_map(local, mesh=mesh, in_specs=in_specs, out_specs=out_specs, check_vma=False)
```

```python
import jax
import jax.numpy as jnp
from jax import lax
from jax.experimental import pallas as pl
from jax.experimental.pallas import tpu as pltpu
from jax.sharding import PartitionSpec as P

BF16 = jnp.bfloat16
F32 = jnp.float32
HIGH = lax.Precision.HIGHEST
CHUNKS = 2
GROUP = 8
NN = (((1,), (0,)), ((), ()))
NT = (((1,), (1,)), ((), ()))
TN = (((0,), (0,)), ((), ()))
PARAMS = pltpu.CompilerParams(vmem_limit_bytes=48 << 20)


def mm(a, b, dims):
    return lax.dot_general(a, b, dims, preferred_element_type=F32)


def halves(a):
    high = a.astype(BF16)
    return high, (a - high.astype(F32)).astype(BF16)


def mm_left(a, b, dims):
    high, low = halves(a)
    return mm(high, b, dims) + mm(low, b, dims)


def mm_right(a, b):
    width = b.shape[1]
    both = mm(a, jnp.concatenate(halves(b), axis=1), NN)
    return both[:, :width] + both[:, width:]


def mm_wide(a, b):
    b = b.astype(BF16)
    return mm(jnp.concatenate(halves(a), axis=1), jnp.concatenate([b, b], axis=1), NT)


def whole(*shape):
    return pl.BlockSpec(shape, lambda i, at: (0,) * len(shape))


def tie(value, *before):
    return lax.optimization_barrier((value, *before))[0]


def cost(flops, size, exps=0):
    return pl.CostEstimate(flops=flops, bytes_accessed=size, transcendentals=exps)


def states_kernel(at_ref, v_ref, scale_ref, rows_ref, out_ref):
    del at_ref
    group = scale_ref.shape[2]
    width = v_ref.shape[1] // group
    for j in range(group):
        scaled = v_ref[:, j * width : (j + 1) * width].astype(F32) * scale_ref[0, :, j : j + 1]
        out_ref[j] = mm_right(rows_ref[...], scaled)


def span_states(values, scale, rows_t, at, count):
    groups, span, group = scale.shape
    width = values.shape[1] // (groups * group)
    states = rows_t.shape[0]
    return pl.pallas_call(
        states_kernel,
        grid_spec=pltpu.PrefetchScalarGridSpec(
            num_scalar_prefetch=1,
            grid=(count,),
            in_specs=[
                pl.BlockSpec((span, group * width), lambda i, at: (0, at[0] + i)),
                pl.BlockSpec((1, span, group), lambda i, at: (at[0] + i, 0, 0)),
                whole(states, span),
            ],
            out_specs=pl.BlockSpec((group, states, width), lambda i, at: (i, 0, 0)),
        ),
        out_shape=jax.ShapeDtypeStruct((count * group, states, width), F32),
        compiler_params=PARAMS,
        cost_estimate=cost(
            4 * span * count * group * width * states,
            count * group * width * (2 * span + 4 * states),
        ),
    )(at, values, scale, rows_t)


def inner_kernel(
    first, last, at_ref, x_ref, y_ref, b_ref, c_ref, run_ref, run_t_ref, step_ref, skip_ref,
    state_ref, *rest,
):
    del at_ref
    held = rest[: 0 if first else 5]
    partial_ref, col_ref, carry_ref, mix_ref, grad_c_ref, cross, rows = rest[len(held) :]
    index = pl.program_id(0)
    group = step_ref.shape[2]
    span = x_ref.shape[0]
    width = x_ref.shape[1] // group

    @pl.when(index == 0)
    def _():
        cross[...] = mm(b_ref[...], c_ref[...], NT)
        mix_ref[...] = jnp.zeros_like(mix_ref) if first else held[3][...]
        grad_c_ref[...] = jnp.zeros_like(grad_c_ref) if first else held[4][...]

    source = lax.broadcasted_iota(jnp.int32, (span, span), 0)
    target = lax.broadcasted_iota(jnp.int32, (span, span), 1)
    causal = source <= target
    for j in range(group):
        columns = slice(j * width, (j + 1) * width)
        x = x_ref[:, columns]
        y = y_ref[:, columns]
        run_col = run_ref[0, :, j : j + 1]
        step_col = step_ref[0, :, j : j + 1]
        run_row = run_t_ref[0, j : j + 1, :]
        decay = jnp.exp(jnp.where(causal, run_row - run_col, -jnp.inf))
        weights = decay * cross[...]
        pairs = mm(x, y, NT)
        mix_ref[...] += decay * pairs * step_col
        terms = weights * pairs
        col_ref[0, :, j : j + 1] = jnp.sum(terms, axis=1, keepdims=True)
        rows[j : j + 1, :] = jnp.sum(terms * step_col, axis=0, keepdims=True)
        inner = mm_left(weights, y, NN)
        y_wide = y.astype(F32)
        partial_ref[:, columns] = step_col * inner + skip_ref[0, j : j + 1, :] * y_wide
        state = state_ref[j]
        scaled = y_wide * jnp.exp(run_col)
        grad_c_ref[...] += mm_wide(scaled, state)
        carry_ref[0, :, j : j + 1] = jnp.sum(
            scaled * mm_right(c_ref[...], state), axis=1, keepdims=True
        )
    carry_ref[0] += rows[...].T

    if last:

        @pl.when(index == pl.num_programs(0) - 1)
        def _():
            high, low = halves(mix_ref[...])
            mix_ref[...] = mm(high, c_ref[...], NN) + mm(low, c_ref[...], NN)
            grad_c_ref[...] += mm(high, b_ref[...], TN) + mm(low, b_ref[...], TN)


def inner_part(x, y, b, c, running, running_t, steps, skip_rows, incoming, at, count, held, last):
    groups, span, group = steps.shape
    heads = groups * group
    width = x.shape[1] // heads
    states = b.shape[1]
    block = pl.BlockSpec((span, group * width), lambda i, at: (0, at[0] + i))
    table = pl.BlockSpec((1, span, group), lambda i, at: (at[0] + i, 0, 0))
    any_place = pl.BlockSpec(memory_space=pl.ANY)
    return pl.pallas_call(
        lambda *refs: inner_kernel(not held, last, *refs),
        grid_spec=pltpu.PrefetchScalarGridSpec(
            num_scalar_prefetch=1,
            grid=(count,),
            in_specs=[
                block,
                block,
                whole(span, states),
                whole(span, states),
                table,
                pl.BlockSpec((1, group, span), lambda i, at: (at[0] + i, 0, 0)),
                table,
                pl.BlockSpec((1, group, width), lambda i, at: (at[0] + i, 0, 0)),
                pl.BlockSpec((group, states, width), lambda i, at: (at[0] + i, 0, 0)),
            ]
            + ([any_place] * 3 + [whole(span, states)] * 2 if held else []),
            out_specs=[block, table, table, whole(span, states), whole(span, states)],
            scratch_shapes=[pltpu.VMEM((span, span), F32), pltpu.VMEM((group, span), F32)],
        ),
        out_shape=[
            jax.ShapeDtypeStruct((span, heads * width), F32),
            jax.ShapeDtypeStruct((groups, span, group), F32),
            jax.ShapeDtypeStruct((groups, span, group), F32),
            jax.ShapeDtypeStruct((span, states), F32),
            jax.ShapeDtypeStruct((span, states), F32),
        ],
        input_output_aliases={10: 0, 11: 1, 12: 2} if held else {},
        compiler_params=PARAMS,
        cost_estimate=cost(
            14 * span * count * group * width * states,
            count * group * width * (8 * span + 4 * states),
            count * group * span * span,
        ),
    )(
        jnp.full((1,), at, jnp.int32), x, y, b, c, running, running_t, steps, skip_rows,
        incoming, *held,
    )


def outer_kernel(
    at_ref, x_ref, part_ref, b_ref, state_ref, grad_state_ref, run_ref, step_ref,
    col_ref, carry_ref, grad_b_in_ref, *rest,
):
    del at_ref
    grad_x_ref, grad_b_ref, grad_step_ref, grad_decay_ref, late, overlap = rest[-6:]
    group = step_ref.shape[2]
    span = x_ref.shape[0]
    width = x_ref.shape[1] // group

    @pl.when(pl.program_id(0) == 0)
    def _():
        grad_b_ref[...] = grad_b_in_ref[...]

    running = run_ref[0]
    end = running[span - 1 : span, :]
    tails = jnp.exp(end - running)
    steps = step_ref[0]
    for j in range(group):
        columns = slice(j * width, (j + 1) * width)
        tail_col = tails[:, j : j + 1]
        step_col = steps[:, j : j + 1]
        grad_state = grad_state_ref[j]
        x = x_ref[:, columns].astype(F32)
        outer = mm_right(b_ref[...], grad_state) * tail_col
        late[:, j : j + 1] = jnp.sum(x * outer, axis=1, keepdims=True)
        grad_x_ref[:, columns] = (part_ref[:, columns] + step_col * outer).astype(BF16)
        grad_b_ref[...] += mm_wide(x * (step_col * tail_col), grad_state)
        shared = jnp.sum(grad_state * state_ref[j], axis=0, keepdims=True)
        overlap[:, j : j + 1] = jnp.sum(shared, axis=1, keepdims=True)

    grad_step = col_ref[0] + late[...]
    grad_step_ref[0] = grad_step
    change = carry_ref[0] - steps * grad_step
    last = jnp.exp(end) * overlap[...] + jnp.sum(steps * late[...], axis=0, keepdims=True)
    source = lax.broadcasted_iota(jnp.int32, (span, span), 0)
    target = lax.broadcasted_iota(jnp.int32, (span, span), 1)
    from_here = (source <= target).astype(BF16)
    high, low = halves(change)
    lowest = (change - high.astype(F32) - low.astype(F32)).astype(BF16)
    grad_decay_ref[0] = last + (
        mm(from_here, high, NN) + mm(from_here, low, NN) + mm(from_here, lowest, NN)
    )


def outer_part(x, part, b, state, grad_state, running, steps, cols, carries, grad_b, at, before):
    groups, span, group = steps.shape
    heads = groups * group
    count = grad_state.shape[0] // group
    width = x.shape[1] // heads
    states = b.shape[1]
    block = pl.BlockSpec((span, group * width), lambda i, at: (0, at[0] + i))
    table = pl.BlockSpec((1, span, group), lambda i, at: (at[0] + i, 0, 0))
    held = [] if before is None else list(before)
    return pl.pallas_call(
        outer_kernel,
        grid_spec=pltpu.PrefetchScalarGridSpec(
            num_scalar_prefetch=1,
            grid=(count,),
            in_specs=[
                block,
                block,
                whole(span, states),
                pl.BlockSpec((group, states, width), lambda i, at: (at[0] + i, 0, 0)),
                pl.BlockSpec((group, states, width), lambda i, at: (i, 0, 0)),
                table,
                table,
                table,
                table,
                whole(span, states),
            ]
            + [pl.BlockSpec(memory_space=pl.ANY)] * len(held),
            out_specs=[block, whole(span, states), table, table],
            scratch_shapes=[pltpu.VMEM((span, group), F32), pltpu.VMEM((1, group), F32)],
        ),
        out_shape=[
            jax.ShapeDtypeStruct((span, heads * width), BF16),
            jax.ShapeDtypeStruct((span, states), F32),
            jax.ShapeDtypeStruct((groups, span, group), F32),
            jax.ShapeDtypeStruct((groups, span, group), F32),
        ],
        input_output_aliases={11: 0, 12: 2, 13: 3} if held else {},
        compiler_params=PARAMS,
        cost_estimate=cost(
            8 * span * count * group * width * states,
            count * group * width * (8 * span + 8 * states),
        ),
    )(at, x, part, b, state, grad_state, running, steps, cols, carries, grad_b, *held)


def project_kernel(hops, at_ref, *refs):
    count = len(hops)
    pieces, (own_ref, other_ref, send_ref, keep_ref, left) = refs[:count], refs[count:]
    rows = pieces[0].shape[0]
    depth = own_ref.shape[1]

    @pl.when(pl.program_id(0) == 0)
    def _():
        first = pl.multiple_of(at_ref[0] * depth, depth)
        second = pl.multiple_of((1 - at_ref[0]) * depth, depth)
        for place, hop in enumerate(hops):
            left[pl.ds(place * rows, rows), :depth] = pieces[hop][:, pl.ds(first, depth)]
            left[pl.ds(place * rows, rows), depth:] = pieces[hop][:, pl.ds(second, depth)]

    total = mm(left[:, :depth], own_ref[...], NT) + mm(left[:, depth:], other_ref[...], NT)
    middle = rows * (count // 2)
    keep_ref[...] = total[:middle]
    send_ref[...] = total[middle:].astype(BF16)


def partial_sums(pieces, hops, own, other, lane, core):
    rows, both = pieces[0].shape
    depth = own.shape[1]
    half = own.shape[0] // 2
    tile = min(512, half)
    steps = half // tile
    middle = rows * (len(hops) // 2)
    weight = pl.BlockSpec((tile, depth), lambda i, at: (lane * steps + i, 0))
    return pl.pallas_call(
        lambda *refs: project_kernel(hops, *refs),
        grid_spec=pltpu.PrefetchScalarGridSpec(
            num_scalar_prefetch=1,
            grid=(steps,),
            in_specs=[whole(rows, both)] * len(hops) + [weight, weight],
            out_specs=[pl.BlockSpec((middle, tile), lambda i, at: (0, i))] * 2,
            scratch_shapes=[pltpu.VMEM((rows * len(hops), both), BF16)],
        ),
        out_shape=[
            jax.ShapeDtypeStruct((middle, half), BF16),
            jax.ShapeDtypeStruct((middle, half), F32),
        ],
        compiler_params=PARAMS,
        cost_estimate=cost(
            2 * rows * len(hops) * both * half, 2 * both * half + 6 * middle * half
        ),
    )(core, *pieces, own, other)


def finish_kernel(count, *refs):
    keeps, arrived, out_ref = refs[: 2 * count], refs[2 * count : -1], refs[-1]
    steps = pl.num_programs(0) // 2
    rows = keeps[0].shape[0]
    for lane in range(2):

        @pl.when(pl.program_id(0) // steps == lane)
        def _():
            for chunk in range(count):
                at = lane * count + chunk
                total = keeps[at][...] + arrived[at][...].astype(F32)
                out_ref[chunk * rows : (chunk + 1) * rows, :] = total.astype(BF16)


def finish(keeps, arrived):
    count = len(keeps) // 2
    rows, half = keeps[0].shape
    tile = min(1024, half)
    steps = half // tile
    place = [lambda i: (0, jnp.minimum(i, steps - 1)), lambda i: (0, jnp.maximum(i - steps, 0))]
    specs = [pl.BlockSpec((rows, tile), place[lane]) for lane in range(2) for _ in range(count)]
    return pl.pallas_call(
        lambda *refs: finish_kernel(count, *refs),
        grid=(2 * steps,),
        in_specs=specs + specs,
        out_specs=pl.BlockSpec((rows * count, tile), lambda i: (0, i)),
        out_shape=jax.ShapeDtypeStruct((rows * count, 2 * half), BF16),
        compiler_params=PARAMS,
        cost_estimate=cost(4 * rows * count * half, 16 * rows * count * half),
    )(*keeps, *arrived)


def across(value, hop, chips):
    pairs = [(2 * i + core, 2 * (i ^ hop) + core) for i in range(chips) for core in range(2)]
    return lax.ppermute(value, "seq", pairs)


def other_core(value, chips):
    return lax.ppermute(value, "seq", [(i, i ^ 1) for i in range(2 * chips)])


def orders(chips):
    bits = [1 << i for i in range(chips.bit_length() - 1)]
    return [bits, bits[::-1]]


def sum_over_heads(value):
    count = lax.axis_size("head")
    here = lax.axis_index("head")
    shares = value.reshape((count, value.shape[0] // count) + value.shape[1:])
    shift = lambda hop: [(i, (i + hop) % count) for i in range(count)]
    share = lambda hop: lax.dynamic_index_in_dim(shares, (here + hop) % count, 0, False)
    total = share(0)
    for hop in range(1, count):
        total = total + lax.ppermute(share(hop), "head", shift(hop))
    parts = [total] + [lax.ppermute(total, "head", shift(hop)) for hop in range(1, count)]
    stacked = jnp.stack(parts)
    ordered = [
        lax.dynamic_index_in_dim(stacked, (here - i) % count, 0, False) for i in range(count)
    ]
    return jnp.concatenate(ordered, axis=0)


def project(grad_out, out_weight, chips, chip, core, before):
    span = grad_out.shape[0]
    both = 2 * out_weight.shape[1]
    other = other_core(out_weight, chips)
    core_at = core.astype(jnp.int32).reshape(1)
    rows = span // CHUNKS
    fulls = [
        lax.all_gather(grad_out[i * rows : (i + 1) * rows], "head", axis=1, tiled=True)
        for i in range(CHUNKS)
    ]
    lanes = []
    for order in orders(chips):
        hops = [0]
        for bit in order[::-1]:
            hops = hops + [hop | bit for hop in hops]
        lanes.append((order, hops))
    waiting = [[], []]

    def reduce_last(blocks):
        for lane, (order, _) in enumerate(lanes):
            keep, send = waiting[lane][-1]
            for step, bit in enumerate(order):
                arrived = across(send, bit, chips)
                if step == 0 and blocks is not None:
                    arrived = tie(arrived, *blocks)
                if step < len(order) - 1:
                    keep = keep + arrived.astype(F32)
                    size = keep.shape[0] // 2
                    send = keep[size:].astype(BF16)
                    keep = keep[:size]
            waiting[lane][-1] = (keep, arrived)

    for chunk in range(CHUNKS):
        full = tie(fulls[chunk], *before[chunk], *[w[-1][1] for w in waiting if w])
        own = [
            lax.dynamic_slice_in_dim(full, (chip ^ hop) * both, both, 1) for hop in range(chips)
        ]
        if chunk:
            reduce_last(own)
        blocks = [across(block, hop, chips) if hop else block for hop, block in enumerate(own)]
        for lane, (_, hops) in enumerate(lanes):
            send, keep = partial_sums(blocks, hops, out_weight, other, lane, core_at)
            waiting[lane].append((keep, send))
    reduce_last(None)
    ends = waiting[0] + waiting[1]
    return finish([keep for keep, _ in ends], [arrived for _, arrived in ends])


def exchange(mine, theirs, ends, chips, chip, core, reverse, fill):
    half = mine.shape[0]
    ends = lax.dynamic_slice_in_dim(ends, core * half, half, 1)
    by_chip = ends.reshape(chips, 2, half)
    own_ends = lax.dynamic_index_in_dim(by_chip, chip, 0, False)
    chip_ends = by_chip[:, 0] + by_chip[:, 1]
    index = jnp.arange(chips)[:, None]
    scale = lambda logs, value: jnp.exp(logs)[:, None, None] * value.astype(F32)

    def carry(source, target):
        before = source > target if reverse else source < target
        inside = (index > jnp.minimum(source, target)) & (index < jnp.maximum(source, target))
        between = jnp.sum(jnp.where(inside, chip_ends, 0.0), axis=0)
        return jnp.where(before, between, -jnp.inf)

    near_first = (core == 0) != reverse
    first = jnp.where(near_first, mine, theirs)
    second = jnp.where(near_first, theirs, mine)
    first_end, second_end = (own_ends[1], own_ends[0]) if reverse else (own_ends[0], own_ends[1])
    chip_state = scale(second_end, first) + second
    lanes = []
    for lane in range(2):
        heads = slice(lane * (half // 2), (lane + 1) * (half // 2))
        lanes.append((heads, {0: chip_state[heads].astype(BF16)}))
    bits = orders(chips)
    for step in range(len(bits[0])):
        last = step == len(bits[0]) - 1
        sent = []
        for order, (heads, items) in zip(bits, lanes):
            if last:
                target = chip ^ order[step]
                total = sum(scale(carry(chip ^ o, target)[heads], i) for o, i in items.items())
                sent.append({0: total.astype(BF16)})
            else:
                sent.append(dict(items))
        done = fill(step, [item for items in sent for item in items.values()])
        for order, (heads, items), going in zip(bits, lanes, sent):
            for o, item in going.items():
                items[o | order[step]] = tie(across(item, order[step], chips), *done)
    totals = []
    for order, (heads, items) in zip(bits, lanes):
        arrived = items.pop(order[-1])
        total = sum(scale(carry(chip ^ o, chip)[heads], i) for o, i in items.items())
        totals.append(total + arrived.astype(F32))
    total = jnp.concatenate(totals, axis=0)
    after = scale(first_end, total) + first
    return jnp.where(near_first, total, after), jnp.where(near_first, after, total)


def local(grad_out, out_weight, ssm_input, step_size, log_decay, b_in, c_in, skip):
    place_on_seq = lax.axis_index("seq")
    chips = lax.axis_size("seq") // 2
    chip, core = place_on_seq // 2, place_on_seq % 2
    span, heads = step_size.shape
    width = ssm_input.shape[1] // heads
    group = min(GROUP, heads // 2)
    groups = heads // group
    by_group = lambda t: t.reshape(span, groups, group).transpose(1, 0, 2)
    flat = lambda t: t.transpose(1, 0, 2).reshape(span, heads)
    mine_at = (core * (groups // 2)).astype(jnp.int32).reshape(1)
    other_at = ((1 - core) * (groups // 2)).astype(jnp.int32).reshape(1)

    upto = jnp.tril(jnp.ones((span, span), F32))
    running = jnp.dot(upto, log_decay, precision=HIGH)
    ends = lax.all_gather(running[-1], "seq")
    tail = jnp.exp(running[-1:] - running)
    rise = by_group(jnp.exp(running))
    running_g = by_group(running)
    running_t = running.T.reshape(groups, group, span)
    steps_g = by_group(step_size)
    skip_rows = jnp.broadcast_to(skip.reshape(groups, group, 1), (groups, group, width))
    b_rows, c_rows = b_in.T, c_in.T

    def span_both(values, scale, rows_t):
        to_other = span_states(values, scale, rows_t, other_at, groups // 2)
        theirs = other_core(to_other, chips)
        return span_states(values, scale, rows_t, mine_at, groups // 2), theirs

    last_sent = []

    def note(step, sent):
        last_sent[:] = sent
        return []

    mine, theirs = span_both(ssm_input, by_group(step_size * tail), b_rows)
    for_mine, for_theirs = exchange(mine, theirs, ends, chips, chip, core, False, note)
    arrived = other_core(for_theirs, chips)
    incoming = jnp.where(
        core == 0,
        jnp.concatenate([for_mine, arrived], axis=0),
        jnp.concatenate([arrived, for_mine], axis=0),
    )
    tables = (running_g, running_t, steps_g, skip_rows)
    before = [[*last_sent, *tables, rise, c_rows]] + [[incoming]] * (CHUNKS - 1)
    grad_y = project(grad_out, out_weight, chips, chip, core, before)

    few = max(1, groups // 4)
    counts = [few, groups - 2 * few, few]
    held = ()

    def fill(step, sent):
        nonlocal held
        count = counts[step] if step < len(counts) else 0
        if count:
            held = inner_part(
                ssm_input, grad_y, b_in, c_in, tie(running_g, *sent), running_t, steps_g,
                skip_rows, incoming, sum(counts[:step]), count, held, step == len(counts) - 1,
            )
        return list(held)

    mine, theirs = span_both(grad_y, rise, c_rows)
    theirs = tie(theirs, *fill(0, [mine]))
    for_mine, for_theirs = exchange(
        mine, theirs, ends, chips, chip, core, True, lambda step, sent: fill(step + 1, sent)
    )
    for_other = other_core(for_theirs, chips)
    part, cols, carries, grad_b, grad_c = held
    shared = (running_g, steps_g, cols, carries)
    grad_x, grad_b, grad_step, grad_decay = outer_part(
        ssm_input, part, b_in, incoming, for_mine, *shared, grad_b, mine_at, None
    )
    grad_x, grad_b, grad_step, grad_decay = outer_part(
        ssm_input, part, b_in, incoming, for_other, *shared, grad_b, other_at,
        (grad_x, grad_step, grad_decay),
    )
    both = sum_over_heads(jnp.stack([grad_b, grad_c], axis=1))
    return (grad_x, flat(grad_step), flat(grad_decay), both[:, 0], both[:, 1])


def solution(mesh):
    in_specs = (
        P("seq", "head"),
        P("head", "seq"),
        P("seq", "head"),
        P("seq", "head"),
        P("seq", "head"),
        P("seq", None),
        P("seq", None),
        P("head"),
    )
    out_specs = (
        P("seq", "head"),
        P("seq", "head"),
        P("seq", "head"),
        P("seq", None),
        P("seq", None),
    )
    return jax.shard_map(local, mesh=mesh, in_specs=in_specs, out_specs=out_specs, check_vma=False)
```

```python
import jax
import jax.numpy as jnp
from jax import lax
from jax.experimental import pallas as pl
from jax.experimental.pallas import tpu as pltpu
from jax.sharding import PartitionSpec as P

BF16 = jnp.bfloat16
F32 = jnp.float32
HIGH = lax.Precision.HIGHEST
CHUNKS = 2
GROUP = 8
NN = (((1,), (0,)), ((), ()))
NT = (((1,), (1,)), ((), ()))
TN = (((0,), (0,)), ((), ()))
PARAMS = pltpu.CompilerParams(vmem_limit_bytes=60 << 20)


def mm(a, b, dims):
    return lax.dot_general(a, b, dims, preferred_element_type=F32)


def halves(a):
    high = a.astype(BF16)
    return high, (a - high.astype(F32)).astype(BF16)


def mm_right(a, b):
    width = b.shape[1]
    both = mm(a, jnp.concatenate(halves(b), axis=1), NN)
    return both[:, :width] + both[:, width:]


def mm_wide(lefts, rights):
    left = [part for a in lefts for part in halves(a)]
    right = [part for b in rights for part in [b.astype(BF16)] * 2]
    return mm(jnp.concatenate(left, axis=1), jnp.concatenate(right, axis=1), NT)


def whole(*shape):
    return pl.BlockSpec(shape, lambda i, at: (0,) * len(shape))


def tie(value, *before):
    return lax.optimization_barrier((value, *before))[0]


def cost(flops, size, exps=0):
    return pl.CostEstimate(flops=flops, bytes_accessed=size, transcendentals=exps)


def states_kernel(at_ref, v_ref, scale_ref, rows_ref, out_ref):
    del at_ref
    group = scale_ref.shape[2]
    width = v_ref.shape[1] // group
    for j in range(group):
        scaled = v_ref[:, j * width : (j + 1) * width].astype(F32) * scale_ref[0, :, j : j + 1]
        out_ref[j] = mm_right(rows_ref[...], scaled)


def span_states(values, scale, rows_t, at, count):
    groups, span, group = scale.shape
    width = values.shape[1] // (groups * group)
    states = rows_t.shape[0]
    return pl.pallas_call(
        states_kernel,
        grid_spec=pltpu.PrefetchScalarGridSpec(
            num_scalar_prefetch=1,
            grid=(count,),
            in_specs=[
                pl.BlockSpec((span, group * width), lambda i, at: (0, at[0] + i)),
                pl.BlockSpec((1, span, group), lambda i, at: (at[0] + i, 0, 0)),
                whole(states, span),
            ],
            out_specs=pl.BlockSpec((group, states, width), lambda i, at: (i, 0, 0)),
        ),
        out_shape=jax.ShapeDtypeStruct((count * group, states, width), F32),
        compiler_params=PARAMS,
        cost_estimate=cost(
            4 * span * count * group * width * states,
            count * group * width * (2 * span + 4 * states),
        ),
    )(at, values, scale, rows_t)


def decay_kernel(run_ref, run_t_ref, b_ref, c_ref, decay_ref, weight_ref, cross_ref):
    group = run_ref.shape[2]
    span = run_ref.shape[1]

    @pl.when(pl.program_id(0) == 0)
    def _():
        cross_ref[...] = mm(b_ref[...], c_ref[...], NT)

    source = lax.broadcasted_iota(jnp.int32, (span, span), 0)
    target = lax.broadcasted_iota(jnp.int32, (span, span), 1)
    causal = source <= target
    for j in range(group):
        gap = run_t_ref[0, j : j + 1, :] - run_ref[0, :, j : j + 1]
        decay = jnp.exp(jnp.where(causal, gap, -jnp.inf))
        decay_ref[j] = decay
        high, low = halves(decay * cross_ref[...])
        weight_ref[j, :, :span] = high
        weight_ref[j, :, span:] = low


def decays(running, running_t, b, c):
    groups, span, group = running.shape
    states = b.shape[1]
    fixed = lambda *shape: pl.BlockSpec(shape, lambda i: (0,) * len(shape))
    return pl.pallas_call(
        decay_kernel,
        grid=(groups,),
        in_specs=[
            pl.BlockSpec((1, span, group), lambda i: (i, 0, 0)),
            pl.BlockSpec((1, group, span), lambda i: (i, 0, 0)),
            fixed(span, states),
            fixed(span, states),
        ],
        out_specs=[
            pl.BlockSpec((group, span, span), lambda i: (i, 0, 0)),
            pl.BlockSpec((group, span, 2 * span), lambda i: (i, 0, 0)),
            fixed(span, span),
        ],
        out_shape=[
            jax.ShapeDtypeStruct((groups * group, span, span), F32),
            jax.ShapeDtypeStruct((groups * group, span, 2 * span), BF16),
            jax.ShapeDtypeStruct((span, span), F32),
        ],
        compiler_params=PARAMS,
        cost_estimate=cost(
            8 * groups * group * span * span,
            8 * groups * group * span * span,
            groups * group * span * span,
        ),
    )(running, running_t, b, c)


def inner_kernel(
    first, last, at_ref, x_ref, y_ref, b_ref, c_ref, rise_ref, step_ref, skip_ref,
    state_ref, decay_ref, weight_ref, cross_ref, *rest,
):
    del at_ref
    held = rest[: 0 if first else 5]
    partial_ref, col_ref, carry_ref, mix_ref, grad_c_ref, rows = rest[len(held) :]
    group = step_ref.shape[2]
    width = x_ref.shape[1] // group

    @pl.when(pl.program_id(0) == 0)
    def _():
        mix_ref[...] = jnp.zeros_like(mix_ref) if first else held[3][...]
        grad_c_ref[...] = jnp.zeros_like(grad_c_ref) if first else held[4][...]

    lefts, rights = [], []
    for j in range(group):
        columns = slice(j * width, (j + 1) * width)
        y = y_ref[:, columns]
        x_wide = x_ref[:, columns].astype(F32)
        y_wide = y.astype(F32)
        step_col = step_ref[0, :, j : j + 1]
        stepped = jnp.concatenate(halves(x_wide * step_col), axis=1)
        pairs = decay_ref[j] * mm(stepped, jnp.concatenate([y, y], axis=1), NT)
        mix_ref[...] += pairs
        rows[j : j + 1, :] = jnp.sum(pairs * cross_ref[...], axis=0, keepdims=True)
        inner = mm(weight_ref[j], jnp.concatenate([y, y], axis=0), NN)
        col_ref[0, :, j : j + 1] = jnp.sum(x_wide * inner, axis=1, keepdims=True)
        partial_ref[:, columns] = step_col * inner + skip_ref[0, j : j + 1, :] * y_wide
        state = state_ref[j]
        scaled = y_wide * rise_ref[0, :, j : j + 1]
        lefts.append(scaled)
        rights.append(state)
        carry_ref[0, :, j : j + 1] = jnp.sum(
            scaled * mm_right(c_ref[...], state), axis=1, keepdims=True
        )
    grad_c_ref[...] += mm_wide(lefts, rights)
    carry_ref[0] += rows[...].T

    if last:

        @pl.when(pl.program_id(0) == pl.num_programs(0) - 1)
        def _():
            high, low = halves(mix_ref[...])
            mix_ref[...] = mm(high, c_ref[...], NN) + mm(low, c_ref[...], NN)
            grad_c_ref[...] += mm(high, b_ref[...], TN) + mm(low, b_ref[...], TN)


def inner_part(
    x, y, b, c, rise, steps, skip_rows, incoming, decay, weight, cross, at, count, held, last
):
    groups, span, group = steps.shape
    heads = groups * group
    width = x.shape[1] // heads
    states = b.shape[1]
    block = pl.BlockSpec((span, group * width), lambda i, at: (0, at[0] + i))
    table = pl.BlockSpec((1, span, group), lambda i, at: (at[0] + i, 0, 0))
    per_head = lambda *shape: pl.BlockSpec((group, *shape), lambda i, at: (at[0] + i, 0, 0))
    any_place = pl.BlockSpec(memory_space=pl.ANY)
    return pl.pallas_call(
        lambda *refs: inner_kernel(not held, last, *refs),
        grid_spec=pltpu.PrefetchScalarGridSpec(
            num_scalar_prefetch=1,
            grid=(count,),
            in_specs=[
                block,
                block,
                whole(span, states),
                whole(span, states),
                table,
                table,
                pl.BlockSpec((1, group, width), lambda i, at: (at[0] + i, 0, 0)),
                per_head(states, width),
                per_head(span, span),
                per_head(span, 2 * span),
                whole(span, span),
            ]
            + ([any_place] * 3 + [whole(span, states)] * 2 if held else []),
            out_specs=[block, table, table, whole(span, states), whole(span, states)],
            scratch_shapes=[pltpu.VMEM((group, span), F32)],
        ),
        out_shape=[
            jax.ShapeDtypeStruct((span, heads * width), F32),
            jax.ShapeDtypeStruct((groups, span, group), F32),
            jax.ShapeDtypeStruct((groups, span, group), F32),
            jax.ShapeDtypeStruct((span, states), F32),
            jax.ShapeDtypeStruct((span, states), F32),
        ],
        input_output_aliases={12: 0, 13: 1, 14: 2} if held else {},
        compiler_params=PARAMS,
        cost_estimate=cost(
            14 * span * count * group * width * states,
            count * group * (8 * span * width + 4 * width * states + 8 * span * span),
        ),
    )(
        jnp.full((1,), at, jnp.int32), x, y, b, c, rise, steps, skip_rows, incoming,
        decay, weight, cross, *held,
    )


def outer_kernel(
    at_ref, x_ref, part_ref, b_ref, state_ref, grad_state_ref, run_ref, step_ref,
    col_ref, carry_ref, grad_b_in_ref, *rest,
):
    del at_ref
    grad_x_ref, grad_b_ref, grad_step_ref, grad_decay_ref, late, overlap = rest[-6:]
    group = step_ref.shape[2]
    span = x_ref.shape[0]
    width = x_ref.shape[1] // group

    @pl.when(pl.program_id(0) == 0)
    def _():
        grad_b_ref[...] = grad_b_in_ref[...]

    running = run_ref[0]
    end = running[span - 1 : span, :]
    tails = jnp.exp(end - running)
    steps = step_ref[0]
    lefts, rights = [], []
    for j in range(group):
        columns = slice(j * width, (j + 1) * width)
        tail_col = tails[:, j : j + 1]
        step_col = steps[:, j : j + 1]
        grad_state = grad_state_ref[j]
        x = x_ref[:, columns].astype(F32)
        outer = mm_right(b_ref[...], grad_state) * tail_col
        late[:, j : j + 1] = jnp.sum(x * outer, axis=1, keepdims=True)
        grad_x_ref[:, columns] = (part_ref[:, columns] + step_col * outer).astype(BF16)
        lefts.append(x * (step_col * tail_col))
        rights.append(grad_state)
        shared = jnp.sum(grad_state * state_ref[j], axis=0, keepdims=True)
        overlap[:, j : j + 1] = jnp.sum(shared, axis=1, keepdims=True)

    grad_b_ref[...] += mm_wide(lefts, rights)
    grad_step = col_ref[0] + late[...]
    grad_step_ref[0] = grad_step
    change = carry_ref[0] - steps * grad_step
    last = jnp.exp(end) * overlap[...] + jnp.sum(steps * late[...], axis=0, keepdims=True)
    source = lax.broadcasted_iota(jnp.int32, (span, span), 0)
    target = lax.broadcasted_iota(jnp.int32, (span, span), 1)
    from_here = (source <= target).astype(BF16)
    high, low = halves(change)
    lowest = (change - high.astype(F32) - low.astype(F32)).astype(BF16)
    grad_decay_ref[0] = last + (
        mm(from_here, high, NN) + mm(from_here, low, NN) + mm(from_here, lowest, NN)
    )


def outer_part(x, part, b, state, grad_state, running, steps, cols, carries, grad_b, at, before):
    groups, span, group = steps.shape
    heads = groups * group
    count = grad_state.shape[0] // group
    width = x.shape[1] // heads
    states = b.shape[1]
    block = pl.BlockSpec((span, group * width), lambda i, at: (0, at[0] + i))
    table = pl.BlockSpec((1, span, group), lambda i, at: (at[0] + i, 0, 0))
    held = [] if before is None else list(before)
    return pl.pallas_call(
        outer_kernel,
        grid_spec=pltpu.PrefetchScalarGridSpec(
            num_scalar_prefetch=1,
            grid=(count,),
            in_specs=[
                block,
                block,
                whole(span, states),
                pl.BlockSpec((group, states, width), lambda i, at: (at[0] + i, 0, 0)),
                pl.BlockSpec((group, states, width), lambda i, at: (i, 0, 0)),
                table,
                table,
                table,
                table,
                whole(span, states),
            ]
            + [pl.BlockSpec(memory_space=pl.ANY)] * len(held),
            out_specs=[block, whole(span, states), table, table],
            scratch_shapes=[pltpu.VMEM((span, group), F32), pltpu.VMEM((1, group), F32)],
        ),
        out_shape=[
            jax.ShapeDtypeStruct((span, heads * width), BF16),
            jax.ShapeDtypeStruct((span, states), F32),
            jax.ShapeDtypeStruct((groups, span, group), F32),
            jax.ShapeDtypeStruct((groups, span, group), F32),
        ],
        input_output_aliases={11: 0, 12: 2, 13: 3} if held else {},
        compiler_params=PARAMS,
        cost_estimate=cost(
            8 * span * count * group * width * states,
            count * group * width * (8 * span + 8 * states),
        ),
    )(at, x, part, b, state, grad_state, running, steps, cols, carries, grad_b, *held)


def project_kernel(hops, at_ref, *refs):
    count = len(hops)
    pieces, (own_ref, other_ref, send_ref, keep_ref, left) = refs[:count], refs[count:]
    rows = pieces[0].shape[0]
    depth = own_ref.shape[1]

    @pl.when(pl.program_id(0) == 0)
    def _():
        first = pl.multiple_of(at_ref[0] * depth, depth)
        second = pl.multiple_of((1 - at_ref[0]) * depth, depth)
        for place, hop in enumerate(hops):
            left[pl.ds(place * rows, rows), :depth] = pieces[hop][:, pl.ds(first, depth)]
            left[pl.ds(place * rows, rows), depth:] = pieces[hop][:, pl.ds(second, depth)]

    total = mm(left[:, :depth], own_ref[...], NT) + mm(left[:, depth:], other_ref[...], NT)
    middle = rows * (count // 2)
    keep_ref[...] = total[:middle]
    send_ref[...] = total[middle:].astype(BF16)


def partial_sums(pieces, hops, own, other, lane, core):
    rows, both = pieces[0].shape
    depth = own.shape[1]
    half = own.shape[0] // 2
    tile = min(512, half)
    steps = half // tile
    middle = rows * (len(hops) // 2)
    weight = pl.BlockSpec((tile, depth), lambda i, at: (lane * steps + i, 0))
    return pl.pallas_call(
        lambda *refs: project_kernel(hops, *refs),
        grid_spec=pltpu.PrefetchScalarGridSpec(
            num_scalar_prefetch=1,
            grid=(steps,),
            in_specs=[whole(rows, both)] * len(hops) + [weight, weight],
            out_specs=[pl.BlockSpec((middle, tile), lambda i, at: (0, i))] * 2,
            scratch_shapes=[pltpu.VMEM((rows * len(hops), both), BF16)],
        ),
        out_shape=[
            jax.ShapeDtypeStruct((middle, half), BF16),
            jax.ShapeDtypeStruct((middle, half), F32),
        ],
        compiler_params=PARAMS,
        cost_estimate=cost(
            2 * rows * len(hops) * both * half, 2 * both * half + 6 * middle * half
        ),
    )(core, *pieces, own, other)


def finish_kernel(count, *refs):
    keeps, arrived, out_ref = refs[: 2 * count], refs[2 * count : -1], refs[-1]
    steps = pl.num_programs(0) // 2
    rows = arrived[0].shape[0]
    for lane in range(2):

        @pl.when(pl.program_id(0) // steps == lane)
        def _():
            for chunk in range(count):
                at = lane * count + chunk
                total = keeps[at][...] + arrived[at][...].astype(F32)
                out_ref[chunk * rows : (chunk + 1) * rows, :] = total.astype(BF16)


def finish(keeps, arrived):
    count = len(keeps) // 2
    rows, half = arrived[0].shape
    tile = min(1024, half)
    steps = half // tile
    place = [lambda i: (0, jnp.minimum(i, steps - 1)), lambda i: (0, jnp.maximum(i - steps, 0))]
    specs = [pl.BlockSpec((rows, tile), place[lane]) for lane in range(2) for _ in range(count)]
    return pl.pallas_call(
        lambda *refs: finish_kernel(count, *refs),
        grid=(2 * steps,),
        in_specs=specs + specs,
        out_specs=pl.BlockSpec((rows * count, tile), lambda i: (0, i)),
        out_shape=jax.ShapeDtypeStruct((rows * count, 2 * half), BF16),
        compiler_params=PARAMS,
        cost_estimate=cost(4 * rows * count * half, 16 * rows * count * half),
    )(*keeps, *arrived)


def across(value, hop, chips):
    pairs = [(2 * i + core, 2 * (i ^ hop) + core) for i in range(chips) for core in range(2)]
    return lax.ppermute(value, "seq", pairs)


def other_core(value, chips):
    return lax.ppermute(value, "seq", [(i, i ^ 1) for i in range(2 * chips)])


def orders(chips):
    bits = [1 << i for i in range(chips.bit_length() - 1)]
    return [bits, bits[::-1]]


def sum_over_heads(value):
    count = lax.axis_size("head")
    value = value.astype(BF16)
    terms = [
        lax.ppermute(value, "head", [(i, i ^ hop) for i in range(count)]) if hop else value
        for hop in range(count)
    ]
    terms = [term.astype(F32) for term in terms]
    while len(terms) > 1:
        terms = [terms[i] + terms[i + 1] for i in range(0, len(terms), 2)]
    return terms[0]


def project(grad_out, out_weight, chips, chip, core, before):
    span = grad_out.shape[0]
    both = 2 * out_weight.shape[1]
    other = other_core(out_weight, chips)
    core_at = core.astype(jnp.int32).reshape(1)
    rows = span // CHUNKS
    fulls = [
        lax.all_gather(grad_out[i * rows : (i + 1) * rows], "head", axis=1, tiled=True)
        for i in range(CHUNKS)
    ]
    lanes = []
    for order in orders(chips):
        hops = [0]
        for bit in order[::-1]:
            hops = hops + [hop | bit for hop in hops]
        lanes.append((order, hops))
    waiting = [[], []]

    def reduce_last(blocks):
        for lane, (order, _) in enumerate(lanes):
            keep, send = waiting[lane][-1]
            for step, bit in enumerate(order):
                arrived = across(send, bit, chips)
                if step == 0 and blocks is not None:
                    arrived = tie(arrived, *blocks)
                if step < len(order) - 1:
                    keep = keep + arrived.astype(F32)
                    size = keep.shape[0] // 2
                    send = keep[size:].astype(BF16)
                    keep = keep[:size] if size > rows else keep
            waiting[lane][-1] = (keep, arrived)

    for chunk in range(CHUNKS):
        full = tie(fulls[chunk], *before[chunk], *[w[-1][1] for w in waiting if w])
        own = [
            lax.dynamic_slice_in_dim(full, (chip ^ hop) * both, both, 1) for hop in range(chips)
        ]
        if chunk:
            reduce_last(own)
        blocks = [across(block, hop, chips) if hop else block for hop, block in enumerate(own)]
        for lane, (_, hops) in enumerate(lanes):
            send, keep = partial_sums(blocks, hops, out_weight, other, lane, core_at)
            waiting[lane].append((keep, send))
    reduce_last(None)
    ends = waiting[0] + waiting[1]
    return finish([keep for keep, _ in ends], [arrived for _, arrived in ends])


def exchange(mine, theirs, ends, chips, chip, core, reverse, fill):
    half = mine.shape[0]
    ends = lax.dynamic_slice_in_dim(ends, core * half, half, 1)
    by_chip = ends.reshape(chips, 2, half)
    own_ends = lax.dynamic_index_in_dim(by_chip, chip, 0, False)
    chip_ends = by_chip[:, 0] + by_chip[:, 1]
    index = jnp.arange(chips)[:, None]
    scale = lambda logs, value: jnp.exp(logs)[:, None, None] * value.astype(F32)

    def carry(source, target):
        before = source > target if reverse else source < target
        inside = (index > jnp.minimum(source, target)) & (index < jnp.maximum(source, target))
        between = jnp.sum(jnp.where(inside, chip_ends, 0.0), axis=0)
        return jnp.where(before, between, -jnp.inf)

    near_first = (core == 0) != reverse
    first = jnp.where(near_first, mine, theirs)
    second = jnp.where(near_first, theirs, mine)
    first_end, second_end = (own_ends[1], own_ends[0]) if reverse else (own_ends[0], own_ends[1])
    chip_state = scale(second_end, first) + second
    lanes = []
    for lane in range(2):
        heads = slice(lane * (half // 2), (lane + 1) * (half // 2))
        lanes.append((heads, {0: chip_state[heads].astype(BF16)}))
    bits = orders(chips)
    for step in range(len(bits[0])):
        last = step == len(bits[0]) - 1
        sent = []
        for order, (heads, items) in zip(bits, lanes):
            if last:
                target = chip ^ order[step]
                total = sum(scale(carry(chip ^ o, target)[heads], i) for o, i in items.items())
                sent.append({0: total.astype(BF16)})
            else:
                sent.append(dict(items))
        done = fill(step, [item for items in sent for item in items.values()])
        for order, (heads, items), going in zip(bits, lanes, sent):
            for o, item in going.items():
                items[o | order[step]] = across(item, order[step], chips)
        fresh = [(items, o | order[step]) for order, (_, items), going in zip(bits, lanes, sent) for o in going]
        values = lax.optimization_barrier((*[items[o] for items, o in fresh], *done))
        for (items, o), value in zip(fresh, values):
            items[o] = value
    totals = []
    for order, (heads, items) in zip(bits, lanes):
        arrived = items.pop(order[-1])
        total = sum(scale(carry(chip ^ o, chip)[heads], i) for o, i in items.items())
        totals.append(total + arrived.astype(F32))
    total = jnp.concatenate(totals, axis=0)
    after = scale(first_end, total) + first
    return jnp.where(near_first, total, after), jnp.where(near_first, after, total)


def local(grad_out, out_weight, ssm_input, step_size, log_decay, b_in, c_in, skip):
    place_on_seq = lax.axis_index("seq")
    chips = lax.axis_size("seq") // 2
    chip, core = place_on_seq // 2, place_on_seq % 2
    span, heads = step_size.shape
    width = ssm_input.shape[1] // heads
    group = min(GROUP, heads // 2)
    groups = heads // group
    by_group = lambda t: t.reshape(span, groups, group).transpose(1, 0, 2)
    flat = lambda t: t.transpose(1, 0, 2).reshape(span, heads)
    mine_at = (core * (groups // 2)).astype(jnp.int32).reshape(1)
    other_at = ((1 - core) * (groups // 2)).astype(jnp.int32).reshape(1)

    upto = jnp.tril(jnp.ones((span, span), F32))
    running = jnp.dot(upto, log_decay, precision=HIGH)
    ends = lax.all_gather(running[-1], "seq")
    tail = jnp.exp(running[-1:] - running)
    rise = by_group(jnp.exp(running))
    running_g = by_group(running)
    running_t = running.T.reshape(groups, group, span)
    steps_g = by_group(step_size)
    skip_rows = jnp.broadcast_to(skip.reshape(groups, group, 1), (groups, group, width))
    b_rows, c_rows = b_in.T, c_in.T

    def span_both(values, scale, rows_t):
        to_other = span_states(values, scale, rows_t, other_at, groups // 2)
        theirs = other_core(to_other, chips)
        return span_states(values, scale, rows_t, mine_at, groups // 2), theirs

    last_sent = []

    def note(step, sent):
        last_sent[:] = sent
        return []

    first_rows = grad_out[: span // CHUNKS]
    scale = tie(by_group(step_size * tail), first_rows)
    mine, theirs = span_both(ssm_input, scale, b_rows)
    for_mine, for_theirs = exchange(mine, theirs, ends, chips, chip, core, False, note)
    arrived = other_core(for_theirs, chips)
    incoming = jnp.where(
        core == 0,
        jnp.concatenate([for_mine, arrived], axis=0),
        jnp.concatenate([arrived, for_mine], axis=0),
    )
    decay, weight, cross = decays(tie(running_g, *last_sent), running_t, b_in, c_in)
    before = [[*last_sent, steps_g, skip_rows, rise, c_rows]] + [[incoming, cross]] * (CHUNKS - 1)
    grad_y = project(grad_out, out_weight, chips, chip, core, before)

    few = max(1, groups // 4)
    counts = [few, groups - 2 * few, few]
    held = ()

    def fill(step, sent):
        nonlocal held
        count = counts[step] if step < len(counts) else 0
        if count:
            held = inner_part(
                ssm_input, grad_y, b_in, c_in, tie(rise, *sent), steps_g, skip_rows, incoming,
                decay, weight, cross, sum(counts[:step]), count, held, step == len(counts) - 1,
            )
        return list(held)

    mine, theirs = span_both(grad_y, rise, c_rows)
    theirs = tie(theirs, *fill(0, [mine]))
    for_mine, for_theirs = exchange(
        mine, theirs, ends, chips, chip, core, True, lambda step, sent: fill(step + 1, sent)
    )
    for_other = other_core(for_theirs, chips)
    part, cols, carries, grad_b, grad_c = held
    grad_c = sum_over_heads(grad_c)
    shared = (running_g, steps_g, cols, carries)
    grad_x, grad_b, grad_step, grad_decay = outer_part(
        ssm_input, part, b_in, incoming, for_mine, *shared, grad_b, mine_at, None
    )
    grad_x, grad_b, grad_step, grad_decay = outer_part(
        ssm_input, part, b_in, incoming, for_other, *shared, grad_b, other_at,
        (grad_x, grad_step, grad_decay),
    )
    grad_b = sum_over_heads(grad_b)
    return (grad_x, flat(grad_step), flat(grad_decay), grad_b, grad_c)


def solution(mesh):
    in_specs = (
        P("seq", "head"),
        P("head", "seq"),
        P("seq", "head"),
        P("seq", "head"),
        P("seq", "head"),
        P("seq", None),
        P("seq", None),
        P("head"),
    )
    out_specs = (
        P("seq", "head"),
        P("seq", "head"),
        P("seq", "head"),
        P("seq", None),
        P("seq", None),
    )
    return jax.shard_map(local, mesh=mesh, in_specs=in_specs, out_specs=out_specs, check_vma=False)
```

```python
import jax
import jax.numpy as jnp
from jax import lax
from jax.experimental import pallas as pl
from jax.experimental.pallas import tpu as pltpu
from jax.sharding import PartitionSpec as P

BF16 = jnp.bfloat16
F32 = jnp.float32
HIGH = lax.Precision.HIGHEST
GROUP = 8
NN = (((1,), (0,)), ((), ()))
NT = (((1,), (1,)), ((), ()))
TN = (((0,), (0,)), ((), ()))
PARAMS = pltpu.CompilerParams(vmem_limit_bytes=28 << 20)


def mm(a, b, dims):
    return lax.dot_general(a, b, dims, preferred_element_type=F32)


def halves(a):
    high = a.astype(BF16)
    return high, (a - high.astype(F32)).astype(BF16)


def mm_right(a, b):
    width = b.shape[1]
    both = mm(a, jnp.concatenate(halves(b), axis=1), NN)
    return both[:, :width] + both[:, width:]


def mm_wide(lefts, rights):
    left = [part for a in lefts for part in halves(a)]
    right = [part for b in rights for part in [b.astype(BF16)] * 2]
    return mm(jnp.concatenate(left, axis=1), jnp.concatenate(right, axis=1), NT)


def whole(*shape):
    return pl.BlockSpec(shape, lambda i, at: (0,) * len(shape))


def tie(value, *before):
    return lax.optimization_barrier((value, *before))[0]


def cost(flops, size, exps=0):
    scale = 256
    return pl.CostEstimate(
        flops=flops // scale, bytes_accessed=size // scale, transcendentals=exps // scale
    )


def states_kernel(at_ref, v_ref, scale_ref, rows_ref, out_ref):
    del at_ref
    group = scale_ref.shape[2]
    width = v_ref.shape[1] // group
    for j in range(group):
        scaled = v_ref[:, j * width : (j + 1) * width].astype(F32) * scale_ref[0, :, j : j + 1]
        out_ref[j] = mm_right(rows_ref[...], scaled)


def span_states(values, scale, rows_t, at, count):
    groups, span, group = scale.shape
    width = values.shape[1] // (groups * group)
    states = rows_t.shape[0]
    return pl.pallas_call(
        states_kernel,
        grid_spec=pltpu.PrefetchScalarGridSpec(
            num_scalar_prefetch=1,
            grid=(count,),
            in_specs=[
                pl.BlockSpec((span, group * width), lambda i, at: (0, at[0] + i)),
                pl.BlockSpec((1, span, group), lambda i, at: (at[0] + i, 0, 0)),
                whole(states, span),
            ],
            out_specs=pl.BlockSpec((group, states, width), lambda i, at: (i, 0, 0)),
        ),
        out_shape=jax.ShapeDtypeStruct((count * group, states, width), F32),
        compiler_params=PARAMS,
        cost_estimate=cost(
            4 * span * count * group * width * states,
            count * group * width * (2 * span + 4 * states),
        ),
    )(at, values, scale, rows_t)


def decay_kernel(run_ref, run_t_ref, b_ref, c_ref, decay_ref, weight_ref, cross_ref):
    group = run_ref.shape[2]
    span = run_ref.shape[1]

    @pl.when(pl.program_id(0) == 0)
    def _():
        cross_ref[...] = mm(b_ref[...], c_ref[...], NT)

    source = lax.broadcasted_iota(jnp.int32, (span, span), 0)
    target = lax.broadcasted_iota(jnp.int32, (span, span), 1)
    causal = source <= target
    for j in range(group):
        gap = run_t_ref[0, j : j + 1, :] - run_ref[0, :, j : j + 1]
        decay = jnp.exp(jnp.where(causal, gap, -jnp.inf))
        decay_ref[j] = decay
        high, low = halves(decay * cross_ref[...])
        weight_ref[j, :, :span] = high
        weight_ref[j, :, span:] = low


def decays(running, running_t, b, c):
    groups, span, group = running.shape
    states = b.shape[1]
    fixed = lambda *shape: pl.BlockSpec(shape, lambda i: (0,) * len(shape))
    return pl.pallas_call(
        decay_kernel,
        grid=(groups,),
        in_specs=[
            pl.BlockSpec((1, span, group), lambda i: (i, 0, 0)),
            pl.BlockSpec((1, group, span), lambda i: (i, 0, 0)),
            fixed(span, states),
            fixed(span, states),
        ],
        out_specs=[
            pl.BlockSpec((group, span, span), lambda i: (i, 0, 0)),
            pl.BlockSpec((group, span, 2 * span), lambda i: (i, 0, 0)),
            fixed(span, span),
        ],
        out_shape=[
            jax.ShapeDtypeStruct((groups * group, span, span), F32),
            jax.ShapeDtypeStruct((groups * group, span, 2 * span), BF16),
            jax.ShapeDtypeStruct((span, span), F32),
        ],
        compiler_params=PARAMS,
        cost_estimate=cost(
            8 * groups * group * span * span,
            8 * groups * group * span * span,
            groups * group * span * span,
        ),
    )(running, running_t, b, c)


def inner_kernel(
    first, last, at_ref, x_ref, y_ref, b_ref, c_ref, rise_ref, step_ref, skip_ref,
    state_ref, decay_ref, weight_ref, cross_ref, *rest,
):
    del at_ref
    held = rest[: 0 if first else 5]
    partial_ref, col_ref, carry_ref, mix_ref, grad_c_ref, rows = rest[len(held) :]
    group = step_ref.shape[2]
    width = x_ref.shape[1] // group

    @pl.when(pl.program_id(0) == 0)
    def _():
        mix_ref[...] = jnp.zeros_like(mix_ref) if first else held[3][...]
        grad_c_ref[...] = jnp.zeros_like(grad_c_ref) if first else held[4][...]

    lefts, rights = [], []
    for j in range(group):
        columns = slice(j * width, (j + 1) * width)
        y = y_ref[:, columns]
        x_wide = x_ref[:, columns].astype(F32)
        y_wide = y.astype(F32)
        step_col = step_ref[0, :, j : j + 1]
        stepped = jnp.concatenate(halves(x_wide * step_col), axis=1)
        pairs = decay_ref[j] * mm(stepped, jnp.concatenate([y, y], axis=1), NT)
        mix_ref[...] += pairs
        rows[j : j + 1, :] = jnp.sum(pairs * cross_ref[...], axis=0, keepdims=True)
        inner = mm(weight_ref[j], jnp.concatenate([y, y], axis=0), NN)
        col_ref[0, :, j : j + 1] = jnp.sum(x_wide * inner, axis=1, keepdims=True)
        partial_ref[:, columns] = step_col * inner + skip_ref[0, j : j + 1, :] * y_wide
        state = state_ref[j]
        scaled = y_wide * rise_ref[0, :, j : j + 1]
        lefts.append(scaled)
        rights.append(state)
        carry_ref[0, :, j : j + 1] = jnp.sum(
            scaled * mm_right(c_ref[...], state), axis=1, keepdims=True
        )
    grad_c_ref[...] += mm_wide(lefts, rights)
    carry_ref[0] += rows[...].T

    if last:

        @pl.when(pl.program_id(0) == pl.num_programs(0) - 1)
        def _():
            high, low = halves(mix_ref[...])
            mix_ref[...] = mm(high, c_ref[...], NN) + mm(low, c_ref[...], NN)
            grad_c_ref[...] += mm(high, b_ref[...], TN) + mm(low, b_ref[...], TN)


def inner_part(
    x, y, b, c, rise, steps, skip_rows, incoming, decay, weight, cross, at, count, held, last
):
    groups, span, group = steps.shape
    heads = groups * group
    width = x.shape[1] // heads
    states = b.shape[1]
    block = pl.BlockSpec((span, group * width), lambda i, at: (0, at[0] + i))
    table = pl.BlockSpec((1, span, group), lambda i, at: (at[0] + i, 0, 0))
    per_head = lambda *shape: pl.BlockSpec((group, *shape), lambda i, at: (at[0] + i, 0, 0))
    any_place = pl.BlockSpec(memory_space=pl.ANY)
    return pl.pallas_call(
        lambda *refs: inner_kernel(not held, last, *refs),
        grid_spec=pltpu.PrefetchScalarGridSpec(
            num_scalar_prefetch=1,
            grid=(count,),
            in_specs=[
                block,
                block,
                whole(span, states),
                whole(span, states),
                table,
                table,
                pl.BlockSpec((1, group, width), lambda i, at: (at[0] + i, 0, 0)),
                per_head(states, width),
                per_head(span, span),
                per_head(span, 2 * span),
                whole(span, span),
            ]
            + ([any_place] * 3 + [whole(span, states)] * 2 if held else []),
            out_specs=[block, table, table, whole(span, states), whole(span, states)],
            scratch_shapes=[pltpu.VMEM((group, span), F32)],
        ),
        out_shape=[
            jax.ShapeDtypeStruct((span, heads * width), F32),
            jax.ShapeDtypeStruct((groups, span, group), F32),
            jax.ShapeDtypeStruct((groups, span, group), F32),
            jax.ShapeDtypeStruct((span, states), F32),
            jax.ShapeDtypeStruct((span, states), F32),
        ],
        input_output_aliases={12: 0, 13: 1, 14: 2} if held else {},
        compiler_params=PARAMS,
        cost_estimate=cost(
            14 * span * count * group * width * states,
            count * group * (8 * span * width + 4 * width * states + 8 * span * span),
        ),
    )(
        jnp.full((1,), at, jnp.int32), x, y, b, c, rise, steps, skip_rows, incoming,
        decay, weight, cross, *held,
    )


def outer_kernel(
    at_ref, x_ref, part_ref, b_ref, state_ref, grad_state_ref, run_ref, step_ref,
    col_ref, carry_ref, grad_b_in_ref, *rest,
):
    del at_ref
    grad_x_ref, grad_b_ref, grad_step_ref, grad_decay_ref, late, overlap = rest[-6:]
    group = step_ref.shape[2]
    span = x_ref.shape[0]
    width = x_ref.shape[1] // group

    @pl.when(pl.program_id(0) == 0)
    def _():
        grad_b_ref[...] = grad_b_in_ref[...]

    running = run_ref[0]
    end = running[span - 1 : span, :]
    tails = jnp.exp(end - running)
    steps = step_ref[0]
    lefts, rights = [], []
    for j in range(group):
        columns = slice(j * width, (j + 1) * width)
        tail_col = tails[:, j : j + 1]
        step_col = steps[:, j : j + 1]
        grad_state = grad_state_ref[j]
        x = x_ref[:, columns].astype(F32)
        outer = mm_right(b_ref[...], grad_state) * tail_col
        late[:, j : j + 1] = jnp.sum(x * outer, axis=1, keepdims=True)
        grad_x_ref[:, columns] = (part_ref[:, columns] + step_col * outer).astype(BF16)
        lefts.append(x * (step_col * tail_col))
        rights.append(grad_state)
        shared = jnp.sum(grad_state * state_ref[j], axis=0, keepdims=True)
        overlap[:, j : j + 1] = jnp.sum(shared, axis=1, keepdims=True)

    grad_b_ref[...] += mm_wide(lefts, rights)
    grad_step = col_ref[0] + late[...]
    grad_step_ref[0] = grad_step
    change = carry_ref[0] - steps * grad_step
    last = jnp.exp(end) * overlap[...] + jnp.sum(steps * late[...], axis=0, keepdims=True)
    source = lax.broadcasted_iota(jnp.int32, (span, span), 0)
    target = lax.broadcasted_iota(jnp.int32, (span, span), 1)
    from_here = (source <= target).astype(BF16)
    high, low = halves(change)
    lowest = (change - high.astype(F32) - low.astype(F32)).astype(BF16)
    grad_decay_ref[0] = last + (
        mm(from_here, high, NN) + mm(from_here, low, NN) + mm(from_here, lowest, NN)
    )


def outer_part(x, part, b, state, grad_state, running, steps, cols, carries, grad_b, at, before):
    groups, span, group = steps.shape
    heads = groups * group
    count = grad_state.shape[0] // group
    width = x.shape[1] // heads
    states = b.shape[1]
    block = pl.BlockSpec((span, group * width), lambda i, at: (0, at[0] + i))
    table = pl.BlockSpec((1, span, group), lambda i, at: (at[0] + i, 0, 0))
    held = [] if before is None else list(before)
    return pl.pallas_call(
        outer_kernel,
        grid_spec=pltpu.PrefetchScalarGridSpec(
            num_scalar_prefetch=1,
            grid=(count,),
            in_specs=[
                block,
                block,
                whole(span, states),
                pl.BlockSpec((group, states, width), lambda i, at: (at[0] + i, 0, 0)),
                pl.BlockSpec((group, states, width), lambda i, at: (i, 0, 0)),
                table,
                table,
                table,
                table,
                whole(span, states),
            ]
            + [pl.BlockSpec(memory_space=pl.ANY)] * len(held),
            out_specs=[block, whole(span, states), table, table],
            scratch_shapes=[pltpu.VMEM((span, group), F32), pltpu.VMEM((1, group), F32)],
        ),
        out_shape=[
            jax.ShapeDtypeStruct((span, heads * width), BF16),
            jax.ShapeDtypeStruct((span, states), F32),
            jax.ShapeDtypeStruct((groups, span, group), F32),
            jax.ShapeDtypeStruct((groups, span, group), F32),
        ],
        input_output_aliases={11: 0, 12: 2, 13: 3} if held else {},
        compiler_params=PARAMS,
        cost_estimate=cost(
            8 * span * count * group * width * states,
            count * group * width * (8 * span + 8 * states),
        ),
    )(at, x, part, b, state, grad_state, running, steps, cols, carries, grad_b, *held)


def project_kernel(hops, at_ref, *refs):
    count = len(hops)
    pieces, (own_ref, other_ref, send_ref, keep_ref, left) = refs[:count], refs[count:]
    rows = pieces[0].shape[0]
    depth = own_ref.shape[1]

    @pl.when(pl.program_id(0) == 0)
    def _():
        first = pl.multiple_of(at_ref[0] * depth, depth)
        second = pl.multiple_of((1 - at_ref[0]) * depth, depth)
        for place, hop in enumerate(hops):
            left[pl.ds(place * rows, rows), :depth] = pieces[hop][:, pl.ds(first, depth)]
            left[pl.ds(place * rows, rows), depth:] = pieces[hop][:, pl.ds(second, depth)]

    total = mm(left[:, :depth], own_ref[...], NT) + mm(left[:, depth:], other_ref[...], NT)
    middle = rows * (count // 2)
    keep_ref[...] = total[:middle]
    send_ref[...] = total[middle:].astype(BF16)


def partial_sums(pieces, hops, own, other, lane, core):
    rows, both = pieces[0].shape
    depth = own.shape[1]
    half = own.shape[0] // 2
    tile = min(512, half)
    steps = half // tile
    middle = rows * (len(hops) // 2)
    weight = pl.BlockSpec((tile, depth), lambda i, at: (lane * steps + i, 0))
    return pl.pallas_call(
        lambda *refs: project_kernel(hops, *refs),
        grid_spec=pltpu.PrefetchScalarGridSpec(
            num_scalar_prefetch=1,
            grid=(steps,),
            in_specs=[whole(rows, both)] * len(hops) + [weight, weight],
            out_specs=[pl.BlockSpec((middle, tile), lambda i, at: (0, i))] * 2,
            scratch_shapes=[pltpu.VMEM((rows * len(hops), both), BF16)],
        ),
        out_shape=[
            jax.ShapeDtypeStruct((middle, half), BF16),
            jax.ShapeDtypeStruct((middle, half), F32),
        ],
        compiler_params=PARAMS,
        cost_estimate=cost(
            2 * rows * len(hops) * both * half, 2 * both * half + 6 * middle * half
        ),
    )(core, *pieces, own, other)


def finish_kernel(count, *refs):
    keeps, arrived, out_ref = refs[: 2 * count], refs[2 * count : -1], refs[-1]
    steps = pl.num_programs(0) // 2
    for lane in range(2):

        @pl.when(pl.program_id(0) // steps == lane)
        def _():
            start = 0
            for chunk in range(count):
                at = lane * count + chunk
                total = keeps[at][...] + arrived[at][...].astype(F32)
                rows = total.shape[0]
                out_ref[start : start + rows, :] = total.astype(BF16)
                start += rows


def finish(keeps, arrived):
    count = len(keeps) // 2
    half = arrived[0].shape[1]
    span = sum(a.shape[0] for a in arrived) // 2
    tile = min(1024, half)
    steps = half // tile
    place = [lambda i: (0, jnp.minimum(i, steps - 1)), lambda i: (0, jnp.maximum(i - steps, 0))]
    specs = [
        pl.BlockSpec((a.shape[0], tile), place[i // count]) for i, a in enumerate(arrived)
    ]
    return pl.pallas_call(
        lambda *refs: finish_kernel(count, *refs),
        grid=(2 * steps,),
        in_specs=specs + specs,
        out_specs=pl.BlockSpec((span, tile), lambda i: (0, i)),
        out_shape=jax.ShapeDtypeStruct((span, 2 * half), BF16),
        compiler_params=PARAMS,
        cost_estimate=cost(4 * span * half, 16 * span * half),
    )(*keeps, *arrived)


def across(value, hop, chips):
    pairs = [(2 * i + core, 2 * (i ^ hop) + core) for i in range(chips) for core in range(2)]
    return lax.ppermute(value, "seq", pairs)


def other_core(value, chips):
    return lax.ppermute(value, "seq", [(i, i ^ 1) for i in range(2 * chips)])


def orders(chips):
    bits = [1 << i for i in range(chips.bit_length() - 1)]
    return [bits, bits[::-1]]


def sum_over_heads(value):
    count = lax.axis_size("head")
    value = value.astype(BF16)
    terms = [
        lax.ppermute(value, "head", [(i, i ^ hop) for i in range(count)]) if hop else value
        for hop in range(count)
    ]
    terms = [term.astype(F32) for term in terms]
    while len(terms) > 1:
        terms = [terms[i] + terms[i + 1] for i in range(0, len(terms), 2)]
    return terms[0]


def gather_halves(grad_out):
    half = grad_out.shape[0] // 2
    pieces = [grad_out[:half], grad_out[half:]]
    return pieces[0], [lax.all_gather(p, "head", axis=1, tiled=True) for p in pieces]


def blocks_of(full, start, rows, chips, chip):
    both = full.shape[1] // chips
    return [
        lax.dynamic_slice(full, (start, (chip ^ hop) * both), (rows, both)) for hop in range(chips)
    ]


def project(fulls, own, out_weight, other, chips, chip, core, before):
    core_at = core.astype(jnp.int32).reshape(1)
    lanes = []
    for order in orders(chips):
        hops = [0]
        for bit in order[::-1]:
            hops = hops + [hop | bit for hop in hops]
        lanes.append((order, hops))
    waiting = [[], []]

    def reduce(chunk, rows, after):
        for lane, (order, _) in enumerate(lanes):
            keep, send, arrived = waiting[lane][chunk]
            for step, bit in enumerate(order):
                if step:
                    arrived = across(send, bit, chips)
                elif after:
                    arrived = tie(arrived, *after)
                if step < len(order) - 1:
                    keep = keep + arrived.astype(F32)
                    size = keep.shape[0] // 2
                    send = keep[size:].astype(BF16)
                    keep = keep[:size] if size > rows else keep
            waiting[lane][chunk] = (keep, arrived)

    half = fulls[0].shape[0]
    rows = [half, half // 2, half // 2]
    count = len(rows)
    for chunk in range(count):
        blocks = [across(block, hop, chips) if hop else block for hop, block in enumerate(own)]
        if chunk == 0:
            blocks = lax.optimization_barrier((*blocks, *before))[:chips]
        if chunk == 1:
            full = tie(fulls[1], waiting[0][0][2], *own)
            own = blocks_of(full, rows[1], rows[2], chips, chip)
            blocks = lax.optimization_barrier((*blocks, *own))[:chips]
        for lane, (order, hops) in enumerate(lanes):
            send, keep = partial_sums(blocks, hops, out_weight, other, lane, core_at)
            waiting[lane].append((keep, send, across(send, order[0], chips)))
        if chunk == 0:
            full = tie(fulls[1], *[lane[0][1] for lane in waiting])
            own = blocks_of(full, 0, rows[1], chips, chip)
        if chunk == 1:
            reduce(0, rows[0], own)
    reduce(count - 2, rows[count - 2], None)
    reduce(count - 1, rows[count - 1], None)
    ends = waiting[0] + waiting[1]
    return finish([keep for keep, _ in ends], [arrived for _, arrived in ends])


def exchange(mine, theirs, ends, chips, chip, core, reverse, fill):
    half = mine.shape[0]
    ends = lax.dynamic_slice_in_dim(ends, core * half, half, 1)
    by_chip = ends.reshape(chips, 2, half)
    own_ends = lax.dynamic_index_in_dim(by_chip, chip, 0, False)
    chip_ends = by_chip[:, 0] + by_chip[:, 1]
    index = jnp.arange(chips)[:, None]
    scale = lambda logs, value: jnp.exp(logs)[:, None, None] * value.astype(F32)

    def carry(source, target):
        before = source > target if reverse else source < target
        inside = (index > jnp.minimum(source, target)) & (index < jnp.maximum(source, target))
        between = jnp.sum(jnp.where(inside, chip_ends, 0.0), axis=0)
        return jnp.where(before, between, -jnp.inf)

    near_first = (core == 0) != reverse
    first = jnp.where(near_first, mine, theirs)
    second = jnp.where(near_first, theirs, mine)
    first_end, second_end = (own_ends[1], own_ends[0]) if reverse else (own_ends[0], own_ends[1])
    chip_state = scale(second_end, first) + second
    lanes = []
    for lane in range(2):
        heads = slice(lane * (half // 2), (lane + 1) * (half // 2))
        lanes.append((heads, {0: chip_state[heads].astype(BF16)}))
    bits = orders(chips)
    for step in range(len(bits[0])):
        last = step == len(bits[0]) - 1
        sent = []
        for order, (heads, items) in zip(bits, lanes):
            if last:
                target = chip ^ order[step]
                total = sum(scale(carry(chip ^ o, target)[heads], i) for o, i in items.items())
                sent.append({0: total.astype(BF16)})
            else:
                sent.append(dict(items))
        done = fill(step, [item for items in sent for item in items.values()])
        for order, (heads, items), going in zip(bits, lanes, sent):
            for o, item in going.items():
                items[o | order[step]] = across(item, order[step], chips)
        fresh = [(items, o | order[step]) for order, (_, items), going in zip(bits, lanes, sent) for o in going]
        values = lax.optimization_barrier((*[items[o] for items, o in fresh], *done))
        for (items, o), value in zip(fresh, values):
            items[o] = value
    totals = []
    for order, (heads, items) in zip(bits, lanes):
        arrived = items.pop(order[-1])
        total = sum(scale(carry(chip ^ o, chip)[heads], i) for o, i in items.items())
        totals.append(total + arrived.astype(F32))
    total = jnp.concatenate(totals, axis=0)
    after = scale(first_end, total) + first
    return jnp.where(near_first, total, after), jnp.where(near_first, after, total)


def local(grad_out, out_weight, ssm_input, step_size, log_decay, b_in, c_in, skip):
    place_on_seq = lax.axis_index("seq")
    chips = lax.axis_size("seq") // 2
    chip, core = place_on_seq // 2, place_on_seq % 2
    span, heads = step_size.shape
    width = ssm_input.shape[1] // heads
    group = min(GROUP, heads // 2)
    groups = heads // group
    by_group = lambda t: t.reshape(span, groups, group).transpose(1, 0, 2)
    flat = lambda t: t.transpose(1, 0, 2).reshape(span, heads)
    mine_at = (core * (groups // 2)).astype(jnp.int32).reshape(1)
    other_at = ((1 - core) * (groups // 2)).astype(jnp.int32).reshape(1)

    first_rows, fulls = gather_halves(grad_out)
    log_decay, step_size, b_in, c_in, _ = lax.optimization_barrier(
        (log_decay, step_size, b_in, c_in, first_rows)
    )
    other_weight = other_core(out_weight, chips)
    upto = jnp.tril(jnp.ones((span, span), F32))
    running = jnp.dot(upto, log_decay, precision=HIGH)
    ends = lax.all_gather(running[-1], "seq")
    tail = jnp.exp(running[-1:] - running)
    rise = by_group(jnp.exp(running))
    running_g = by_group(running)
    running_t = running.T.reshape(groups, group, span)
    steps_g = by_group(step_size)
    skip_rows = jnp.broadcast_to(skip.reshape(groups, group, 1), (groups, group, width))
    b_rows, c_rows = b_in.T, c_in.T

    def span_both(values, scale, rows_t):
        to_other = span_states(values, scale, rows_t, other_at, groups // 2)
        theirs = other_core(to_other, chips)
        return span_states(values, scale, rows_t, mine_at, groups // 2), theirs

    own = []

    def first_blocks(step, sent):
        if step < chips.bit_length() - 2:
            return []
        own[:] = blocks_of(tie(fulls[0], *sent), 0, span // 2, chips, chip)
        return own

    mine, theirs = span_both(ssm_input, by_group(step_size * tail), b_rows)
    for_mine, for_theirs = exchange(
        mine, theirs, ends, chips, chip, core, False, first_blocks
    )
    arrived = other_core(for_theirs, chips)
    incoming = jnp.where(
        core == 0,
        jnp.concatenate([for_mine, arrived], axis=0),
        jnp.concatenate([arrived, for_mine], axis=0),
    )
    decay, weight, cross = decays(tie(running_g, *own), running_t, b_in, c_in)
    before = [incoming, cross, steps_g, skip_rows, rise, c_rows]
    grad_y = project(fulls, own, out_weight, other_weight, chips, chip, core, before)

    few = max(1, groups // 4)
    counts = [few, groups - 2 * few, few]
    held = ()

    def fill(step, sent):
        nonlocal held
        count = counts[step] if step < len(counts) else 0
        if count:
            held = inner_part(
                ssm_input, grad_y, b_in, c_in, tie(rise, *sent), steps_g, skip_rows, incoming,
                decay, weight, cross, sum(counts[:step]), count, held, step == len(counts) - 1,
            )
        return list(held)

    mine, theirs = span_both(grad_y, rise, c_rows)
    theirs = tie(theirs, *fill(0, [mine]))
    for_mine, for_theirs = exchange(
        mine, theirs, ends, chips, chip, core, True, lambda step, sent: fill(step + 1, sent)
    )
    for_other = other_core(for_theirs, chips)
    part, cols, carries, grad_b, grad_c = held
    grad_c = sum_over_heads(grad_c)
    shared = (running_g, steps_g, cols, carries)
    grad_x, grad_b, grad_step, grad_decay = outer_part(
        ssm_input, part, b_in, incoming, for_mine, *shared, grad_b, mine_at, None
    )
    grad_x, grad_b, grad_step, grad_decay = outer_part(
        ssm_input, part, b_in, incoming, for_other, *shared, grad_b, other_at,
        (grad_x, grad_step, grad_decay),
    )
    grad_b = sum_over_heads(grad_b)
    return (grad_x, flat(grad_step), flat(grad_decay), grad_b, grad_c)


def solution(mesh):
    in_specs = (
        P("seq", "head"),
        P("head", "seq"),
        P("seq", "head"),
        P("seq", "head"),
        P("seq", "head"),
        P("seq", None),
        P("seq", None),
        P("head"),
    )
    out_specs = (
        P("seq", "head"),
        P("seq", "head"),
        P("seq", "head"),
        P("seq", None),
        P("seq", None),
    )
    return jax.shard_map(local, mesh=mesh, in_specs=in_specs, out_specs=out_specs, check_vma=False)
```

```python
import jax
import jax.numpy as jnp
from jax import lax
from jax.experimental import pallas as pl
from jax.experimental.pallas import tpu as pltpu
from jax.sharding import PartitionSpec as P

BF16 = jnp.bfloat16
F32 = jnp.float32
HIGH = lax.Precision.HIGHEST
GROUP = 8
NN = (((1,), (0,)), ((), ()))
NT = (((1,), (1,)), ((), ()))
TN = (((0,), (0,)), ((), ()))
PARAMS = pltpu.CompilerParams(vmem_limit_bytes=24 << 20)


def mm(a, b, dims):
    return lax.dot_general(a, b, dims, preferred_element_type=F32)


def halves(a):
    high = a.astype(BF16)
    return high, (a - high.astype(F32)).astype(BF16)


def mm_right(a, b):
    width = b.shape[1]
    both = mm(a, jnp.concatenate(halves(b), axis=1), NN)
    return both[:, :width] + both[:, width:]


def mm_wide(lefts, rights):
    left = [part for a in lefts for part in halves(a)]
    right = [part for b in rights for part in [b.astype(BF16)] * 2]
    return mm(jnp.concatenate(left, axis=1), jnp.concatenate(right, axis=1), NT)


def whole(*shape):
    return pl.BlockSpec(shape, lambda i, at: (0,) * len(shape))


def tie(value, *before):
    return lax.optimization_barrier((value, *before))[0]


def cost(flops, size, exps=0):
    scale = 256
    return pl.CostEstimate(
        flops=flops // scale, bytes_accessed=size // scale, transcendentals=exps // scale
    )


def states_kernel(at_ref, v_ref, scale_ref, rows_ref, out_ref):
    del at_ref
    group = scale_ref.shape[2]
    width = v_ref.shape[1] // group
    for j in range(group):
        scaled = v_ref[:, j * width : (j + 1) * width].astype(F32) * scale_ref[0, :, j : j + 1]
        out_ref[j] = mm_right(rows_ref[...], scaled)


def span_states(values, scale, rows_t, at, count):
    groups, span, group = scale.shape
    width = values.shape[1] // (groups * group)
    states = rows_t.shape[0]
    return pl.pallas_call(
        states_kernel,
        grid_spec=pltpu.PrefetchScalarGridSpec(
            num_scalar_prefetch=1,
            grid=(count,),
            in_specs=[
                pl.BlockSpec((span, group * width), lambda i, at: (0, at[0] + i)),
                pl.BlockSpec((1, span, group), lambda i, at: (at[0] + i, 0, 0)),
                whole(states, span),
            ],
            out_specs=pl.BlockSpec((group, states, width), lambda i, at: (i, 0, 0)),
        ),
        out_shape=jax.ShapeDtypeStruct((count * group, states, width), F32),
        compiler_params=PARAMS,
        cost_estimate=cost(
            4 * span * count * group * width * states,
            count * group * width * (2 * span + 4 * states),
        ),
    )(at, values, scale, rows_t)


def decay_kernel(run_ref, run_t_ref, b_ref, c_ref, decay_ref, weight_ref, cross_ref):
    group = run_ref.shape[2]
    span = run_ref.shape[1]

    @pl.when(pl.program_id(0) == 0)
    def _():
        cross_ref[...] = mm(b_ref[...], c_ref[...], NT)

    source = lax.broadcasted_iota(jnp.int32, (span, span), 0)
    target = lax.broadcasted_iota(jnp.int32, (span, span), 1)
    causal = source <= target
    for j in range(group):
        gap = run_t_ref[0, j : j + 1, :] - run_ref[0, :, j : j + 1]
        decay = jnp.exp(jnp.where(causal, gap, -jnp.inf))
        decay_ref[j] = decay
        high, low = halves(decay * cross_ref[...])
        weight_ref[j, :, :span] = high
        weight_ref[j, :, span:] = low


def decays(running, running_t, b, c):
    groups, span, group = running.shape
    states = b.shape[1]
    fixed = lambda *shape: pl.BlockSpec(shape, lambda i: (0,) * len(shape))
    return pl.pallas_call(
        decay_kernel,
        grid=(groups,),
        in_specs=[
            pl.BlockSpec((1, span, group), lambda i: (i, 0, 0)),
            pl.BlockSpec((1, group, span), lambda i: (i, 0, 0)),
            fixed(span, states),
            fixed(span, states),
        ],
        out_specs=[
            pl.BlockSpec((group, span, span), lambda i: (i, 0, 0)),
            pl.BlockSpec((group, span, 2 * span), lambda i: (i, 0, 0)),
            fixed(span, span),
        ],
        out_shape=[
            jax.ShapeDtypeStruct((groups * group, span, span), F32),
            jax.ShapeDtypeStruct((groups * group, span, 2 * span), BF16),
            jax.ShapeDtypeStruct((span, span), F32),
        ],
        compiler_params=PARAMS,
        cost_estimate=cost(
            8 * groups * group * span * span,
            8 * groups * group * span * span,
            groups * group * span * span,
        ),
    )(running, running_t, b, c)


def inner_kernel(
    first, last, at_ref, x_ref, y_ref, b_ref, c_ref, rise_ref, step_ref, skip_ref,
    mine_ref, other_ref, decay_ref, weight_ref, cross_ref, *rest,
):
    held = rest[: 0 if first else 5]
    partial_ref, col_ref, carry_ref, mix_ref, grad_c_ref, rows = rest[len(held) :]
    group = step_ref.shape[2]
    width = x_ref.shape[1] // group

    @pl.when(pl.program_id(0) == 0)
    def _():
        mix_ref[...] = jnp.zeros_like(mix_ref) if first else held[3][...]
        grad_c_ref[...] = jnp.zeros_like(grad_c_ref) if first else held[4][...]

    is_mine = (at_ref[0] + pl.program_id(0)) // at_ref[2] == at_ref[1]
    lefts, rights = [], []
    for j in range(group):
        columns = slice(j * width, (j + 1) * width)
        y = y_ref[:, columns]
        x_wide = x_ref[:, columns].astype(F32)
        y_wide = y.astype(F32)
        step_col = step_ref[0, :, j : j + 1]
        stepped = jnp.concatenate(halves(x_wide * step_col), axis=1)
        pairs = decay_ref[j] * mm(stepped, jnp.concatenate([y, y], axis=1), NT)
        mix_ref[...] += pairs
        rows[j : j + 1, :] = jnp.sum(pairs * cross_ref[...], axis=0, keepdims=True)
        inner = mm(weight_ref[j], jnp.concatenate([y, y], axis=0), NN)
        col_ref[0, :, j : j + 1] = jnp.sum(x_wide * inner, axis=1, keepdims=True)
        partial_ref[:, columns] = step_col * inner + skip_ref[0, j : j + 1, :] * y_wide
        state = jnp.where(is_mine, mine_ref[j], other_ref[j])
        scaled = y_wide * rise_ref[0, :, j : j + 1]
        lefts.append(scaled)
        rights.append(state)
        carry_ref[0, :, j : j + 1] = jnp.sum(
            scaled * mm_right(c_ref[...], state), axis=1, keepdims=True
        )
    grad_c_ref[...] += mm_wide(lefts, rights)
    carry_ref[0] += rows[...].T

    if last:

        @pl.when(pl.program_id(0) == pl.num_programs(0) - 1)
        def _():
            high, low = halves(mix_ref[...])
            mix_ref[...] = mm(high, c_ref[...], NN) + mm(low, c_ref[...], NN)
            grad_c_ref[...] += mm(high, b_ref[...], TN) + mm(low, b_ref[...], TN)


def inner_part(
    x, y, b, c, rise, steps, skip_rows, mine, other, core, decay, weight, cross, at, count, held,
    last,
):
    groups, span, group = steps.shape
    heads = groups * group
    width = x.shape[1] // heads
    states = b.shape[1]
    block = pl.BlockSpec((span, group * width), lambda i, at: (0, at[0] + i))
    table = pl.BlockSpec((1, span, group), lambda i, at: (at[0] + i, 0, 0))
    per_head = lambda *shape: pl.BlockSpec((group, *shape), lambda i, at: (at[0] + i, 0, 0))
    any_place = pl.BlockSpec(memory_space=pl.ANY)
    half = groups // 2
    near = lambda i, at: (jnp.clip(at[0] + i - at[1] * half, 0, half - 1), 0, 0)
    far = lambda i, at: (jnp.clip(at[0] + i - (1 - at[1]) * half, 0, half - 1), 0, 0)
    at = jnp.stack([jnp.int32(at), core.astype(jnp.int32), jnp.int32(half)])
    return pl.pallas_call(
        lambda *refs: inner_kernel(not held, last, *refs),
        grid_spec=pltpu.PrefetchScalarGridSpec(
            num_scalar_prefetch=1,
            grid=(count,),
            in_specs=[
                block,
                block,
                whole(span, states),
                whole(span, states),
                table,
                table,
                pl.BlockSpec((1, group, width), lambda i, at: (at[0] + i, 0, 0)),
                pl.BlockSpec((group, states, width), near),
                pl.BlockSpec((group, states, width), far),
                per_head(span, span),
                per_head(span, 2 * span),
                whole(span, span),
            ]
            + ([any_place] * 3 + [whole(span, states)] * 2 if held else []),
            out_specs=[block, table, table, whole(span, states), whole(span, states)],
            scratch_shapes=[pltpu.VMEM((group, span), F32)],
        ),
        out_shape=[
            jax.ShapeDtypeStruct((span, heads * width), F32),
            jax.ShapeDtypeStruct((groups, span, group), F32),
            jax.ShapeDtypeStruct((groups, span, group), F32),
            jax.ShapeDtypeStruct((span, states), F32),
            jax.ShapeDtypeStruct((span, states), F32),
        ],
        input_output_aliases={13: 0, 14: 1, 15: 2} if held else {},
        compiler_params=PARAMS,
        cost_estimate=cost(
            14 * span * count * group * width * states,
            count * group * (8 * span * width + 4 * width * states + 8 * span * span),
        ),
    )(
        at, x, y, b, c, rise, steps, skip_rows, mine, other, decay, weight, cross, *held
    )


def outer_kernel(
    at_ref, x_ref, part_ref, b_ref, state_ref, grad_state_ref, run_ref, step_ref,
    col_ref, carry_ref, grad_b_in_ref, *rest,
):
    del at_ref
    grad_x_ref, grad_b_ref, grad_step_ref, grad_decay_ref, late, overlap = rest[-6:]
    group = step_ref.shape[2]
    span = x_ref.shape[0]
    width = x_ref.shape[1] // group

    @pl.when(pl.program_id(0) == 0)
    def _():
        grad_b_ref[...] = grad_b_in_ref[...]

    running = run_ref[0]
    end = running[span - 1 : span, :]
    tails = jnp.exp(end - running)
    steps = step_ref[0]
    lefts, rights = [], []
    for j in range(group):
        columns = slice(j * width, (j + 1) * width)
        tail_col = tails[:, j : j + 1]
        step_col = steps[:, j : j + 1]
        grad_state = grad_state_ref[j]
        x = x_ref[:, columns].astype(F32)
        outer = mm_right(b_ref[...], grad_state) * tail_col
        late[:, j : j + 1] = jnp.sum(x * outer, axis=1, keepdims=True)
        grad_x_ref[:, columns] = (part_ref[:, columns] + step_col * outer).astype(BF16)
        lefts.append(x * (step_col * tail_col))
        rights.append(grad_state)
        shared = jnp.sum(grad_state * state_ref[j], axis=0, keepdims=True)
        overlap[:, j : j + 1] = jnp.sum(shared, axis=1, keepdims=True)

    grad_b_ref[...] += mm_wide(lefts, rights)
    grad_step = col_ref[0] + late[...]
    grad_step_ref[0] = grad_step
    change = carry_ref[0] - steps * grad_step
    last = jnp.exp(end) * overlap[...] + jnp.sum(steps * late[...], axis=0, keepdims=True)
    source = lax.broadcasted_iota(jnp.int32, (span, span), 0)
    target = lax.broadcasted_iota(jnp.int32, (span, span), 1)
    from_here = (source <= target).astype(BF16)
    high, low = halves(change)
    lowest = (change - high.astype(F32) - low.astype(F32)).astype(BF16)
    grad_decay_ref[0] = last + (
        mm(from_here, high, NN) + mm(from_here, low, NN) + mm(from_here, lowest, NN)
    )


def outer_part(x, part, b, state, grad_state, running, steps, cols, carries, grad_b, at, before):
    groups, span, group = steps.shape
    heads = groups * group
    count = grad_state.shape[0] // group
    width = x.shape[1] // heads
    states = b.shape[1]
    block = pl.BlockSpec((span, group * width), lambda i, at: (0, at[0] + i))
    table = pl.BlockSpec((1, span, group), lambda i, at: (at[0] + i, 0, 0))
    held = [] if before is None else list(before)
    return pl.pallas_call(
        outer_kernel,
        grid_spec=pltpu.PrefetchScalarGridSpec(
            num_scalar_prefetch=1,
            grid=(count,),
            in_specs=[
                block,
                block,
                whole(span, states),
                pl.BlockSpec((group, states, width), lambda i, at: (i, 0, 0)),
                pl.BlockSpec((group, states, width), lambda i, at: (i, 0, 0)),
                table,
                table,
                table,
                table,
                whole(span, states),
            ]
            + [pl.BlockSpec(memory_space=pl.ANY)] * len(held),
            out_specs=[block, whole(span, states), table, table],
            scratch_shapes=[pltpu.VMEM((span, group), F32), pltpu.VMEM((1, group), F32)],
        ),
        out_shape=[
            jax.ShapeDtypeStruct((span, heads * width), BF16),
            jax.ShapeDtypeStruct((span, states), F32),
            jax.ShapeDtypeStruct((groups, span, group), F32),
            jax.ShapeDtypeStruct((groups, span, group), F32),
        ],
        input_output_aliases={11: 0, 12: 2, 13: 3} if held else {},
        compiler_params=PARAMS,
        cost_estimate=cost(
            8 * span * count * group * width * states,
            count * group * width * (8 * span + 8 * states),
        ),
    )(at, x, part, b, state, grad_state, running, steps, cols, carries, grad_b, *held)


def project_kernel(hops, at_ref, *refs):
    count = len(hops)
    pieces, (own_ref, other_ref, send_ref, keep_ref, left) = refs[:count], refs[count:]
    rows = pieces[0].shape[0]
    depth = own_ref.shape[1]

    @pl.when(pl.program_id(0) == 0)
    def _():
        first = pl.multiple_of(at_ref[0] * depth, depth)
        second = pl.multiple_of((1 - at_ref[0]) * depth, depth)
        for place, hop in enumerate(hops):
            left[pl.ds(place * rows, rows), :depth] = pieces[hop][:, pl.ds(first, depth)]
            left[pl.ds(place * rows, rows), depth:] = pieces[hop][:, pl.ds(second, depth)]

    total = mm(left[:, :depth], own_ref[...], NT) + mm(left[:, depth:], other_ref[...], NT)
    middle = rows * (count // 2)
    keep_ref[...] = total[:middle]
    send_ref[...] = total[middle:].astype(BF16)


def partial_sums(pieces, hops, own, other, lane, core):
    rows, both = pieces[0].shape
    depth = own.shape[1]
    half = own.shape[0] // 2
    tile = min(512, half)
    steps = half // tile
    middle = rows * (len(hops) // 2)
    weight = pl.BlockSpec((tile, depth), lambda i, at: (lane * steps + i, 0))
    return pl.pallas_call(
        lambda *refs: project_kernel(hops, *refs),
        grid_spec=pltpu.PrefetchScalarGridSpec(
            num_scalar_prefetch=1,
            grid=(steps,),
            in_specs=[whole(rows, both)] * len(hops) + [weight, weight],
            out_specs=[pl.BlockSpec((middle, tile), lambda i, at: (0, i))] * 2,
            scratch_shapes=[pltpu.VMEM((rows * len(hops), both), BF16)],
        ),
        out_shape=[
            jax.ShapeDtypeStruct((middle, half), BF16),
            jax.ShapeDtypeStruct((middle, half), F32),
        ],
        compiler_params=PARAMS,
        cost_estimate=cost(
            2 * rows * len(hops) * both * half, 2 * both * half + 6 * middle * half
        ),
    )(core, *pieces, own, other)


def finish_kernel(count, *refs):
    keeps, arrived, out_ref = refs[: 2 * count], refs[2 * count : -1], refs[-1]
    steps = pl.num_programs(0) // 2
    for lane in range(2):

        @pl.when(pl.program_id(0) // steps == lane)
        def _():
            start = 0
            for chunk in range(count):
                at = lane * count + chunk
                total = keeps[at][...] + arrived[at][...].astype(F32)
                rows = total.shape[0]
                out_ref[start : start + rows, :] = total.astype(BF16)
                start += rows


def finish(keeps, arrived):
    count = len(keeps) // 2
    half = arrived[0].shape[1]
    span = sum(a.shape[0] for a in arrived) // 2
    tile = min(1024, half)
    steps = half // tile
    place = [lambda i: (0, jnp.minimum(i, steps - 1)), lambda i: (0, jnp.maximum(i - steps, 0))]
    specs = [
        pl.BlockSpec((a.shape[0], tile), place[i // count]) for i, a in enumerate(arrived)
    ]
    return pl.pallas_call(
        lambda *refs: finish_kernel(count, *refs),
        grid=(2 * steps,),
        in_specs=specs + specs,
        out_specs=pl.BlockSpec((span, tile), lambda i: (0, i)),
        out_shape=jax.ShapeDtypeStruct((span, 2 * half), BF16),
        compiler_params=PARAMS,
        cost_estimate=cost(4 * span * half, 16 * span * half),
    )(*keeps, *arrived)


def split_kernel(keep_ref, arrived_ref, out_ref, send_ref):
    total = keep_ref[...] + arrived_ref[...].astype(F32)
    size = out_ref.shape[0]
    out_ref[...] = total[:size]
    send_ref[...] = total[size:].astype(BF16)


def add_and_split(keep, arrived):
    rows, half = keep.shape
    tile = min(1024, half)
    column = lambda size: pl.BlockSpec((size, tile), lambda i: (0, i))
    return pl.pallas_call(
        split_kernel,
        grid=(half // tile,),
        in_specs=[column(rows), column(rows)],
        out_specs=[column(rows // 2), column(rows // 2)],
        out_shape=[
            jax.ShapeDtypeStruct((rows // 2, half), F32),
            jax.ShapeDtypeStruct((rows // 2, half), BF16),
        ],
        compiler_params=PARAMS,
        cost_estimate=cost(rows * half, 9 * rows * half),
    )(keep, arrived)


def blend_kernel(count, step, at_ref, *refs):
    del at_ref
    weight_ref, terms, outs = refs[0], refs[1 : 1 + count], refs[1 + count :]
    for j in range(step):
        head = pl.program_id(0) * step + j
        values = [term[j].astype(F32) for term in terms]
        for k, out in enumerate(outs):
            total = weight_ref[k * count, head] * values[0]
            for i in range(1, count):
                total += weight_ref[k * count + i, head] * values[i]
            out[j] = total.astype(out.dtype)


def blend(terms, starts, weights, heads, dtype):
    count = len(terms)
    step = max(1, min(4, heads // 2))
    while any(start % step for start in starts):
        step //= 2
    rows, width = terms[0].shape[1:]
    specs = []
    for term, start in zip(terms, starts):
        last = term.shape[0] // step - 1
        shift = start // step
        specs.append(
            pl.BlockSpec(
                (step, rows, width),
                lambda i, at, last=last, shift=shift: (jnp.clip(i + shift, 0, last), 0, 0),
            )
        )
    out = pl.BlockSpec((step, rows, width), lambda i, at: (i, 0, 0))
    table = jnp.stack([weight for row in weights for weight in row])
    return pl.pallas_call(
        lambda *refs: blend_kernel(count, step, *refs),
        grid_spec=pltpu.PrefetchScalarGridSpec(
            num_scalar_prefetch=1,
            grid=(heads // step,),
            in_specs=[pl.BlockSpec(memory_space=pltpu.SMEM)] + specs,
            out_specs=[out] * len(weights),
        ),
        out_shape=[jax.ShapeDtypeStruct((heads, rows, width), dtype)] * len(weights),
        compiler_params=PARAMS,
        cost_estimate=cost(
            2 * count * len(weights) * heads * rows * width, 4 * count * heads * rows * width
        ),
    )(jnp.zeros((1,), jnp.int32), table, *terms)


def across(value, hop, chips):
    pairs = [(2 * i + core, 2 * (i ^ hop) + core) for i in range(chips) for core in range(2)]
    return lax.ppermute(value, "seq", pairs)


def other_core(value, chips):
    return lax.ppermute(value, "seq", [(i, i ^ 1) for i in range(2 * chips)])


def orders(chips):
    bits = [1 << i for i in range(chips.bit_length() - 1)]
    return [bits, bits[::-1]]


def sum_over_heads(value):
    count = lax.axis_size("head")
    value = value.astype(BF16)
    terms = [
        lax.ppermute(value, "head", [(i, i ^ hop) for i in range(count)]) if hop else value
        for hop in range(count)
    ]
    terms = [term.astype(F32) for term in terms]
    while len(terms) > 1:
        terms = [terms[i] + terms[i + 1] for i in range(0, len(terms), 2)]
    return terms[0]


def gather_halves(grad_out):
    half = grad_out.shape[0] // 2
    pieces = [grad_out[:half], grad_out[half:]]
    return pieces[0], [lax.all_gather(p, "head", axis=1, tiled=True) for p in pieces]


def blocks_of(full, start, rows, chips, chip):
    both = full.shape[1] // chips
    return [
        lax.dynamic_slice(full, (start, (chip ^ hop) * both), (rows, both)) for hop in range(chips)
    ]


def project(fulls, blocks, second, out_weight, other, chips, chip, core, ahead, before):
    core_at = core.astype(jnp.int32).reshape(1)
    lanes = []
    for order in orders(chips):
        hops = [0]
        for bit in order[::-1]:
            hops = hops + [hop | bit for hop in hops]
        lanes.append((order, hops))
    waiting = [[], []]

    def reduce(chunk, after):
        last = []
        for lane, (order, _) in enumerate(lanes):
            keep, send, arrived = waiting[lane][chunk]
            for step, bit in enumerate(order):
                if step:
                    arrived = across(send, bit, chips)
                elif after:
                    arrived = tie(arrived, *after)
                if step < len(order) - 1:
                    keep, send = add_and_split(keep, arrived)
            waiting[lane][chunk] = (keep, arrived)
            last.append(send)
        return last, [lane[chunk][1] for lane in waiting]

    rows = fulls[0].shape[0] // 2
    own = [None, second]
    for chunk in range(4):
        if chunk:
            blocks = [
                across(block, hop, chips) if hop else block
                for hop, block in enumerate(own[chunk])
            ]
        blocks = lax.optimization_barrier((*blocks, *ahead))[:chips]
        for lane, (order, hops) in enumerate(lanes):
            send, keep = partial_sums(blocks, hops, out_weight, other, lane, core_at)
            waiting[lane].append((keep, send, across(send, order[0], chips)))
        ahead = [lane[chunk][1] for lane in waiting]
        if chunk == 1:
            sent, first = reduce(0, ahead)
            full = tie(fulls[1], *ahead, *first, *before(sent))
            own += [blocks_of(full, i * rows, rows, chips, chip) for i in range(2)]
            ahead = reduce(1, own[2])[1]
    reduce(2, ahead)
    reduce(3, None)
    ends = waiting[0] + waiting[1]
    return finish([keep for keep, _ in ends], [arrived for _, arrived in ends])


def exchange(mine, theirs, ends, chips, chip, core, reverse):
    half = mine.shape[0]
    ends = lax.dynamic_slice_in_dim(ends, core * half, half, 1)
    by_chip = ends.reshape(chips, 2, half)
    own_ends = lax.dynamic_index_in_dim(by_chip, chip, 0, False)
    chip_ends = by_chip[:, 0] + by_chip[:, 1]
    index = jnp.arange(chips)[:, None]

    def carry(source, target):
        before = source > target if reverse else source < target
        inside = (index > jnp.minimum(source, target)) & (index < jnp.maximum(source, target))
        between = jnp.sum(jnp.where(inside, chip_ends, 0.0), axis=0)
        return jnp.exp(jnp.where(before, between, -jnp.inf))

    near_first = (core == 0) != reverse
    own_scale = jnp.exp(own_ends)
    first_scale, second_scale = own_scale[int(reverse)], own_scale[1 - int(reverse)]
    one = jnp.ones((half,), F32)
    pick_near = lambda a, b: jnp.where(near_first, a, b)
    few = half // 2
    part = [slice(0, few), slice(few, half)]
    parts = [pick_near(second_scale, one), pick_near(one, second_scale)]
    lanes = []
    for heads in part:
        weights = [[weight[heads] for weight in parts]]
        chip_state = blend([mine, theirs], [heads.start] * 2, weights, few, BF16)
        lanes.append({0: chip_state[0]})
    bits = orders(chips)
    for step in range(len(bits[0])):
        last = step == len(bits[0]) - 1
        sent = []
        for order, heads, items in zip(bits, part, lanes):
            if last:
                target = chip ^ order[step]
                weights = [[carry(chip ^ o, target)[heads] for o in items]]
                total = blend(list(items.values()), [0] * len(items), weights, few, BF16)
                sent.append({0: total[0]})
            else:
                sent.append(dict(items))
        fresh = []
        for order, items, going in zip(bits, lanes, sent):
            for o, item in going.items():
                items[o | order[step]] = across(item, order[step], chips)
                fresh.append((items, o | order[step]))
        arrived = [items[o] for items, o in fresh]
        done = yield [item for going in sent for item in going.values()], arrived
        values = lax.optimization_barrier((*arrived, *done))
        for (items, o), value in zip(fresh, values):
            items[o] = value
    terms, starts = [mine, theirs], [0, 0]
    alphas = [pick_near(one, first_scale), pick_near(first_scale, one)]
    zero = jnp.zeros((half,), F32)
    weights = [[zero, pick_near(zero, one)], [pick_near(one, zero), zero]]
    for order, heads, items in zip(bits, part, lanes):
        here = (jnp.arange(half) >= heads.start) & (jnp.arange(half) < heads.stop)
        for o, item in items.items():
            if o == 0:
                continue
            scale = one if o == order[-1] else carry(chip ^ o, chip)
            terms.append(item)
            starts.append(-heads.start)
            for row, alpha in zip(weights, alphas):
                row.append(jnp.where(here, alpha * scale, 0.0))
    return tuple(blend(terms, starts, weights, half, F32))


def run_steps(steps, work, done=None):
    for step in range(64):
        try:
            sent, _ = steps.send(done)
        except StopIteration as stop:
            return stop.value
        done = work(step, sent)


def local(grad_out, out_weight, ssm_input, step_size, log_decay, b_in, c_in, skip):
    place_on_seq = lax.axis_index("seq")
    chips = lax.axis_size("seq") // 2
    chip, core = place_on_seq // 2, place_on_seq % 2
    span, heads = step_size.shape
    width = ssm_input.shape[1] // heads
    group = min(GROUP, heads // 2)
    groups = heads // group
    by_group = lambda t: t.reshape(span, groups, group).transpose(1, 0, 2)
    flat = lambda t: t.transpose(1, 0, 2).reshape(span, heads)
    mine_at = (core * (groups // 2)).astype(jnp.int32).reshape(1)
    other_at = ((1 - core) * (groups // 2)).astype(jnp.int32).reshape(1)

    first_rows, fulls = gather_halves(grad_out)
    log_decay, step_size, b_in, c_in, _ = lax.optimization_barrier(
        (log_decay, step_size, b_in, c_in, first_rows)
    )
    other_weight = other_core(out_weight, chips)
    upto = jnp.tril(jnp.ones((span, span), F32))
    running = jnp.dot(upto, log_decay, precision=HIGH)
    ends = lax.all_gather(running[-1], "seq")
    tail = jnp.exp(running[-1:] - running)
    rise = by_group(jnp.exp(running))
    running_g = by_group(running)
    running_t = running.T.reshape(groups, group, span)
    steps_g = by_group(step_size)
    skip_rows = jnp.broadcast_to(skip.reshape(groups, group, 1), (groups, group, width))
    b_rows, c_rows = b_in.T, c_in.T

    def span_both(values, scale, rows_t):
        to_other = span_states(values, scale, rows_t, other_at, groups // 2)
        theirs = other_core(to_other, chips)
        return span_states(values, scale, rows_t, mine_at, groups // 2), theirs

    mine, theirs = span_both(ssm_input, by_group(step_size * tail), b_rows)
    forward = exchange(mine, theirs, ends, chips, chip, core, False)
    sent, raw = next(forward)
    for _ in range(chips.bit_length() - 2):
        sent, raw = forward.send([])
    full = tie(fulls[0], other_weight, *sent)
    rows = span // 4
    own = blocks_of(full, 0, rows, chips, chip)
    blocks = [across(block, hop, chips) if hop else block for hop, block in enumerate(own)]
    second = blocks_of(tie(full, *blocks[1:]), rows, rows, chips, chip)
    tables = []

    def before(done):
        in_mine, for_theirs = run_steps(forward, None, done)
        in_other = other_core(for_theirs, chips)
        tables[:] = [in_mine, in_other, *decays(tie(running_g, *done), running_t, b_in, c_in)]
        return [in_mine, tables[-1], steps_g, skip_rows, rise, c_rows]

    grad_y = project(
        fulls, blocks, second, out_weight, other_weight, chips, chip, core, raw, before
    )
    in_mine, in_other, decay, weight, cross = tables

    counts = [0, groups - groups // 2, groups // 2]
    held = ()

    def fill(step, sent):
        nonlocal held
        count = counts[step] if step < len(counts) else 0
        if count:
            held = inner_part(
                ssm_input, grad_y, b_in, c_in, tie(rise, *sent), steps_g, skip_rows, in_mine,
                in_other, core, decay, weight, cross, sum(counts[:step]), count, held, step == len(counts) - 1,
            )
        return list(held)

    mine, theirs = span_both(grad_y, rise, c_rows)
    theirs = tie(theirs, *fill(0, [mine]))
    backward = exchange(mine, theirs, ends, chips, chip, core, True)
    for_mine, for_theirs = run_steps(backward, lambda step, sent: fill(step + 1, sent))
    for_other = other_core(for_theirs, chips)
    part, cols, carries, grad_b, grad_c = held
    grad_c = sum_over_heads(grad_c)
    shared = (running_g, steps_g, cols, carries)
    grad_x, grad_b, grad_step, grad_decay = outer_part(
        ssm_input, part, b_in, in_mine, for_mine, *shared, grad_b, mine_at, None
    )
    grad_x, grad_b, grad_step, grad_decay = outer_part(
        ssm_input, part, b_in, in_other, for_other, *shared, grad_b, other_at,
        (grad_x, grad_step, grad_decay),
    )
    grad_b = sum_over_heads(grad_b)
    return (grad_x, flat(grad_step), flat(grad_decay), grad_b, grad_c)


def solution(mesh):
    in_specs = (
        P("seq", "head"),
        P("head", "seq"),
        P("seq", "head"),
        P("seq", "head"),
        P("seq", "head"),
        P("seq", None),
        P("seq", None),
        P("head"),
    )
    out_specs = (
        P("seq", "head"),
        P("seq", "head"),
        P("seq", "head"),
        P("seq", None),
        P("seq", None),
    )
    return jax.shard_map(local, mesh=mesh, in_specs=in_specs, out_specs=out_specs, check_vma=False)
```

```python
import jax
import jax.numpy as jnp
from jax import lax
from jax.experimental import pallas as pl
from jax.experimental.pallas import tpu as pltpu
from jax.sharding import PartitionSpec as P

BF16 = jnp.bfloat16
F32 = jnp.float32
HIGH = lax.Precision.HIGHEST
GROUP = 8
NN = (((1,), (0,)), ((), ()))
NT = (((1,), (1,)), ((), ()))
TN = (((0,), (0,)), ((), ()))
PARAMS = pltpu.CompilerParams(vmem_limit_bytes=48 << 20)


def mm(a, b, dims):
    return lax.dot_general(a, b, dims, preferred_element_type=F32)


def halves(a):
    high = a.astype(BF16)
    return high, (a - high.astype(F32)).astype(BF16)


def mm_right(a, b):
    width = b.shape[1]
    both = mm(a, jnp.concatenate(halves(b), axis=1), NN)
    return both[:, :width] + both[:, width:]


def mm_wide(lefts, rights):
    left = [part for a in lefts for part in halves(a)]
    right = [part for b in rights for part in [b.astype(BF16)] * 2]
    return mm(jnp.concatenate(left, axis=1), jnp.concatenate(right, axis=1), NT)


def whole(*shape):
    return pl.BlockSpec(shape, lambda i, at: (0,) * len(shape))


def tie(value, *before):
    return lax.optimization_barrier((value, *before))[0]


def cost(flops, size, exps=0):
    scale = 256
    return pl.CostEstimate(
        flops=flops // scale, bytes_accessed=size // scale, transcendentals=exps // scale
    )


def states_kernel(at_ref, v_ref, scale_ref, rows_ref, out_ref):
    del at_ref
    group = scale_ref.shape[2]
    width = v_ref.shape[1] // group
    for j in range(group):
        scaled = v_ref[:, j * width : (j + 1) * width].astype(F32) * scale_ref[0, :, j : j + 1]
        out_ref[j] = mm_right(rows_ref[...], scaled)


def span_states(values, scale, rows_t, at, count):
    groups, span, group = scale.shape
    width = values.shape[1] // (groups * group)
    states = rows_t.shape[0]
    return pl.pallas_call(
        states_kernel,
        grid_spec=pltpu.PrefetchScalarGridSpec(
            num_scalar_prefetch=1,
            grid=(count,),
            in_specs=[
                pl.BlockSpec((span, group * width), lambda i, at: (0, at[0] + i)),
                pl.BlockSpec((1, span, group), lambda i, at: (at[0] + i, 0, 0)),
                whole(states, span),
            ],
            out_specs=pl.BlockSpec((group, states, width), lambda i, at: (i, 0, 0)),
        ),
        out_shape=jax.ShapeDtypeStruct((count * group, states, width), F32),
        compiler_params=PARAMS,
        cost_estimate=cost(
            4 * span * count * group * width * states,
            count * group * width * (2 * span + 4 * states),
        ),
    )(at, values, scale, rows_t)


def decay_kernel(run_ref, run_t_ref, b_ref, c_ref, decay_ref, weight_ref, cross_ref):
    group = run_ref.shape[2]
    span = run_ref.shape[1]

    @pl.when(pl.program_id(0) == 0)
    def _():
        cross_ref[...] = mm(b_ref[...], c_ref[...], NT)

    source = lax.broadcasted_iota(jnp.int32, (span, span), 0)
    target = lax.broadcasted_iota(jnp.int32, (span, span), 1)
    causal = source <= target
    for j in range(group):
        gap = run_t_ref[0, j : j + 1, :] - run_ref[0, :, j : j + 1]
        decay = jnp.exp(jnp.where(causal, gap, -jnp.inf))
        decay_ref[j] = decay
        high, low = halves(decay * cross_ref[...])
        weight_ref[j, :, :span] = high
        weight_ref[j, :, span:] = low


def decays(running, running_t, b, c):
    groups, span, group = running.shape
    states = b.shape[1]
    fixed = lambda *shape: pl.BlockSpec(shape, lambda i: (0,) * len(shape))
    return pl.pallas_call(
        decay_kernel,
        grid=(groups,),
        in_specs=[
            pl.BlockSpec((1, span, group), lambda i: (i, 0, 0)),
            pl.BlockSpec((1, group, span), lambda i: (i, 0, 0)),
            fixed(span, states),
            fixed(span, states),
        ],
        out_specs=[
            pl.BlockSpec((group, span, span), lambda i: (i, 0, 0)),
            pl.BlockSpec((group, span, 2 * span), lambda i: (i, 0, 0)),
            fixed(span, span),
        ],
        out_shape=[
            jax.ShapeDtypeStruct((groups * group, span, span), F32),
            jax.ShapeDtypeStruct((groups * group, span, 2 * span), BF16),
            jax.ShapeDtypeStruct((span, span), F32),
        ],
        compiler_params=PARAMS,
        cost_estimate=cost(
            8 * groups * group * span * span,
            8 * groups * group * span * span,
            groups * group * span * span,
        ),
    )(running, running_t, b, c)


def inner_kernel(
    first, last, at_ref, x_ref, y_ref, b_ref, c_ref, rise_ref, step_ref, skip_ref,
    mine_ref, other_ref, decay_ref, weight_ref, cross_ref, *rest,
):
    held = rest[: 0 if first else 5]
    partial_ref, col_ref, carry_ref, mix_ref, grad_c_ref, rows = rest[len(held) :]
    group = step_ref.shape[2]
    width = x_ref.shape[1] // group

    @pl.when(pl.program_id(0) == 0)
    def _():
        mix_ref[...] = jnp.zeros_like(mix_ref) if first else held[3][...]
        grad_c_ref[...] = jnp.zeros_like(grad_c_ref) if first else held[4][...]

    is_mine = (at_ref[0] + pl.program_id(0)) // at_ref[2] == at_ref[1]
    lefts, rights = [], []
    for j in range(group):
        columns = slice(j * width, (j + 1) * width)
        y = y_ref[:, columns]
        x_wide = x_ref[:, columns].astype(F32)
        y_wide = y.astype(F32)
        step_col = step_ref[0, :, j : j + 1]
        stepped = jnp.concatenate(halves(x_wide * step_col), axis=1)
        pairs = decay_ref[j] * mm(stepped, jnp.concatenate([y, y], axis=1), NT)
        mix_ref[...] += pairs
        rows[j : j + 1, :] = jnp.sum(pairs * cross_ref[...], axis=0, keepdims=True)
        inner = mm(weight_ref[j], jnp.concatenate([y, y], axis=0), NN)
        col_ref[0, :, j : j + 1] = jnp.sum(x_wide * inner, axis=1, keepdims=True)
        partial_ref[:, columns] = step_col * inner + skip_ref[0, j : j + 1, :] * y_wide
        state = jnp.where(is_mine, mine_ref[j], other_ref[j])
        scaled = y_wide * rise_ref[0, :, j : j + 1]
        lefts.append(scaled)
        rights.append(state)
        carry_ref[0, :, j : j + 1] = jnp.sum(
            scaled * mm_right(c_ref[...], state), axis=1, keepdims=True
        )
    grad_c_ref[...] += mm_wide(lefts, rights)
    carry_ref[0] += rows[...].T

    if last:

        @pl.when(pl.program_id(0) == pl.num_programs(0) - 1)
        def _():
            high, low = halves(mix_ref[...])
            mix_ref[...] = mm(high, c_ref[...], NN) + mm(low, c_ref[...], NN)
            grad_c_ref[...] += mm(high, b_ref[...], TN) + mm(low, b_ref[...], TN)


def inner_part(
    x, y, b, c, rise, steps, skip_rows, mine, other, core, decay, weight, cross, at, count, held,
    last,
):
    groups, span, group = steps.shape
    heads = groups * group
    width = x.shape[1] // heads
    states = b.shape[1]
    block = pl.BlockSpec((span, group * width), lambda i, at: (0, at[0] + i))
    table = pl.BlockSpec((1, span, group), lambda i, at: (at[0] + i, 0, 0))
    per_head = lambda *shape: pl.BlockSpec((group, *shape), lambda i, at: (at[0] + i, 0, 0))
    any_place = pl.BlockSpec(memory_space=pl.ANY)
    half = groups // 2
    near = lambda i, at: (jnp.clip(at[0] + i - at[1] * half, 0, half - 1), 0, 0)
    far = lambda i, at: (jnp.clip(at[0] + i - (1 - at[1]) * half, 0, half - 1), 0, 0)
    at = jnp.stack([jnp.int32(at), core.astype(jnp.int32), jnp.int32(half)])
    return pl.pallas_call(
        lambda *refs: inner_kernel(not held, last, *refs),
        grid_spec=pltpu.PrefetchScalarGridSpec(
            num_scalar_prefetch=1,
            grid=(count,),
            in_specs=[
                block,
                block,
                whole(span, states),
                whole(span, states),
                table,
                table,
                pl.BlockSpec((1, group, width), lambda i, at: (at[0] + i, 0, 0)),
                pl.BlockSpec((group, states, width), near),
                pl.BlockSpec((group, states, width), far),
                per_head(span, span),
                per_head(span, 2 * span),
                whole(span, span),
            ]
            + ([any_place] * 3 + [whole(span, states)] * 2 if held else []),
            out_specs=[block, table, table, whole(span, states), whole(span, states)],
            scratch_shapes=[pltpu.VMEM((group, span), F32)],
        ),
        out_shape=[
            jax.ShapeDtypeStruct((span, heads * width), F32),
            jax.ShapeDtypeStruct((groups, span, group), F32),
            jax.ShapeDtypeStruct((groups, span, group), F32),
            jax.ShapeDtypeStruct((span, states), F32),
            jax.ShapeDtypeStruct((span, states), F32),
        ],
        input_output_aliases={13: 0, 14: 1, 15: 2} if held else {},
        compiler_params=PARAMS,
        cost_estimate=cost(
            14 * span * count * group * width * states,
            count * group * (8 * span * width + 4 * width * states + 8 * span * span),
        ),
    )(
        at, x, y, b, c, rise, steps, skip_rows, mine, other, decay, weight, cross, *held
    )


def outer_kernel(
    at_ref, x_ref, part_ref, b_ref, state_ref, grad_state_ref, run_ref, step_ref,
    col_ref, carry_ref, grad_b_in_ref, *rest,
):
    del at_ref
    grad_x_ref, grad_b_ref, grad_step_ref, grad_decay_ref, late, overlap = rest[-6:]
    group = step_ref.shape[2]
    span = x_ref.shape[0]
    width = x_ref.shape[1] // group

    @pl.when(pl.program_id(0) == 0)
    def _():
        grad_b_ref[...] = grad_b_in_ref[...]

    running = run_ref[0]
    end = running[span - 1 : span, :]
    tails = jnp.exp(end - running)
    steps = step_ref[0]
    lefts, rights = [], []
    for j in range(group):
        columns = slice(j * width, (j + 1) * width)
        tail_col = tails[:, j : j + 1]
        step_col = steps[:, j : j + 1]
        grad_state = grad_state_ref[j]
        x = x_ref[:, columns].astype(F32)
        outer = mm_right(b_ref[...], grad_state) * tail_col
        late[:, j : j + 1] = jnp.sum(x * outer, axis=1, keepdims=True)
        grad_x_ref[:, columns] = (part_ref[:, columns] + step_col * outer).astype(BF16)
        lefts.append(x * (step_col * tail_col))
        rights.append(grad_state)
        shared = jnp.sum(grad_state * state_ref[j], axis=0, keepdims=True)
        overlap[:, j : j + 1] = jnp.sum(shared, axis=1, keepdims=True)

    grad_b_ref[...] += mm_wide(lefts, rights)
    grad_step = col_ref[0] + late[...]
    grad_step_ref[0] = grad_step
    change = carry_ref[0] - steps * grad_step
    last = jnp.exp(end) * overlap[...] + jnp.sum(steps * late[...], axis=0, keepdims=True)
    source = lax.broadcasted_iota(jnp.int32, (span, span), 0)
    target = lax.broadcasted_iota(jnp.int32, (span, span), 1)
    from_here = (source <= target).astype(BF16)
    high, low = halves(change)
    lowest = (change - high.astype(F32) - low.astype(F32)).astype(BF16)
    grad_decay_ref[0] = last + (
        mm(from_here, high, NN) + mm(from_here, low, NN) + mm(from_here, lowest, NN)
    )


def outer_part(x, part, b, state, grad_state, running, steps, cols, carries, grad_b, at, before):
    groups, span, group = steps.shape
    heads = groups * group
    count = grad_state.shape[0] // group
    width = x.shape[1] // heads
    states = b.shape[1]
    block = pl.BlockSpec((span, group * width), lambda i, at: (0, at[0] + i))
    table = pl.BlockSpec((1, span, group), lambda i, at: (at[0] + i, 0, 0))
    held = [] if before is None else list(before)
    return pl.pallas_call(
        outer_kernel,
        grid_spec=pltpu.PrefetchScalarGridSpec(
            num_scalar_prefetch=1,
            grid=(count,),
            in_specs=[
                block,
                block,
                whole(span, states),
                pl.BlockSpec((group, states, width), lambda i, at: (i, 0, 0)),
                pl.BlockSpec((group, states, width), lambda i, at: (i, 0, 0)),
                table,
                table,
                table,
                table,
                whole(span, states),
            ]
            + [pl.BlockSpec(memory_space=pl.ANY)] * len(held),
            out_specs=[block, whole(span, states), table, table],
            scratch_shapes=[pltpu.VMEM((span, group), F32), pltpu.VMEM((1, group), F32)],
        ),
        out_shape=[
            jax.ShapeDtypeStruct((span, heads * width), BF16),
            jax.ShapeDtypeStruct((span, states), F32),
            jax.ShapeDtypeStruct((groups, span, group), F32),
            jax.ShapeDtypeStruct((groups, span, group), F32),
        ],
        input_output_aliases={11: 0, 12: 2, 13: 3} if held else {},
        compiler_params=PARAMS,
        cost_estimate=cost(
            8 * span * count * group * width * states,
            count * group * width * (8 * span + 8 * states),
        ),
    )(at, x, part, b, state, grad_state, running, steps, cols, carries, grad_b, *held)


def project_kernel(hops, at_ref, *refs):
    count = len(hops)
    pieces, (own_ref, other_ref, send_ref, keep_ref, left) = refs[:count], refs[count:]
    rows = pieces[0].shape[0]
    depth = own_ref.shape[1]

    @pl.when(pl.program_id(0) == 0)
    def _():
        first = pl.multiple_of(at_ref[0] * depth, depth)
        second = pl.multiple_of((1 - at_ref[0]) * depth, depth)
        for place, hop in enumerate(hops):
            left[pl.ds(place * rows, rows), :depth] = pieces[hop][:, pl.ds(first, depth)]
            left[pl.ds(place * rows, rows), depth:] = pieces[hop][:, pl.ds(second, depth)]

    total = mm(left[:, :depth], own_ref[...], NT) + mm(left[:, depth:], other_ref[...], NT)
    middle = rows * (count // 2)
    keep_ref[...] = total[:middle]
    send_ref[...] = total[middle:].astype(BF16)


def partial_sums(pieces, hops, own, other, lane, core):
    rows, both = pieces[0].shape
    depth = own.shape[1]
    half = own.shape[0] // 2
    tile = min(512, half)
    steps = half // tile
    middle = rows * (len(hops) // 2)
    weight = pl.BlockSpec((tile, depth), lambda i, at: (lane * steps + i, 0))
    return pl.pallas_call(
        lambda *refs: project_kernel(hops, *refs),
        grid_spec=pltpu.PrefetchScalarGridSpec(
            num_scalar_prefetch=1,
            grid=(steps,),
            in_specs=[whole(rows, both)] * len(hops) + [weight, weight],
            out_specs=[pl.BlockSpec((middle, tile), lambda i, at: (0, i))] * 2,
            scratch_shapes=[pltpu.VMEM((rows * len(hops), both), BF16)],
        ),
        out_shape=[
            jax.ShapeDtypeStruct((middle, half), BF16),
            jax.ShapeDtypeStruct((middle, half), F32),
        ],
        compiler_params=PARAMS,
        cost_estimate=cost(
            2 * rows * len(hops) * both * half, 2 * both * half + 6 * middle * half
        ),
    )(core, *pieces, own, other)


def finish_kernel(count, *refs):
    keeps, arrived, out_ref = refs[: 2 * count], refs[2 * count : -1], refs[-1]
    steps = pl.num_programs(0) // 2
    for lane in range(2):

        @pl.when(pl.program_id(0) // steps == lane)
        def _():
            start = 0
            for chunk in range(count):
                at = lane * count + chunk
                total = keeps[at][...] + arrived[at][...].astype(F32)
                rows = total.shape[0]
                out_ref[start : start + rows, :] = total.astype(BF16)
                start += rows


def finish(keeps, arrived):
    count = len(keeps) // 2
    half = arrived[0].shape[1]
    span = sum(a.shape[0] for a in arrived) // 2
    tile = min(1024, half)
    steps = half // tile
    place = [lambda i: (0, jnp.minimum(i, steps - 1)), lambda i: (0, jnp.maximum(i - steps, 0))]
    specs = [
        pl.BlockSpec((a.shape[0], tile), place[i // count]) for i, a in enumerate(arrived)
    ]
    return pl.pallas_call(
        lambda *refs: finish_kernel(count, *refs),
        grid=(2 * steps,),
        in_specs=specs + specs,
        out_specs=pl.BlockSpec((span, tile), lambda i: (0, i)),
        out_shape=jax.ShapeDtypeStruct((span, 2 * half), BF16),
        compiler_params=PARAMS,
        cost_estimate=cost(4 * span * half, 16 * span * half),
    )(*keeps, *arrived)


def split_kernel(keep_ref, arrived_ref, out_ref, send_ref):
    total = keep_ref[...] + arrived_ref[...].astype(F32)
    size = out_ref.shape[0]
    out_ref[...] = total[:size]
    send_ref[...] = total[size:].astype(BF16)


def add_and_split(keep, arrived):
    rows, half = keep.shape
    tile = min(1024, half)
    column = lambda size: pl.BlockSpec((size, tile), lambda i: (0, i))
    return pl.pallas_call(
        split_kernel,
        grid=(half // tile,),
        in_specs=[column(rows), column(rows)],
        out_specs=[column(rows // 2), column(rows // 2)],
        out_shape=[
            jax.ShapeDtypeStruct((rows // 2, half), F32),
            jax.ShapeDtypeStruct((rows // 2, half), BF16),
        ],
        compiler_params=PARAMS,
        cost_estimate=cost(rows * half, 9 * rows * half),
    )(keep, arrived)


def blend_kernel(count, step, at_ref, *refs):
    del at_ref
    weight_ref, terms, outs = refs[0], refs[1 : 1 + count], refs[1 + count :]
    for j in range(step):
        head = pl.program_id(0) * step + j
        values = [term[j].astype(F32) for term in terms]
        for k, out in enumerate(outs):
            total = weight_ref[k * count, head] * values[0]
            for i in range(1, count):
                total += weight_ref[k * count + i, head] * values[i]
            out[j] = total.astype(out.dtype)


def blend(terms, starts, weights, heads, dtype):
    count = len(terms)
    step = max(1, min(4, heads // 2))
    while any(start % step for start in starts):
        step //= 2
    rows, width = terms[0].shape[1:]
    specs = []
    for term, start in zip(terms, starts):
        last = term.shape[0] // step - 1
        shift = start // step
        specs.append(
            pl.BlockSpec(
                (step, rows, width),
                lambda i, at, last=last, shift=shift: (jnp.clip(i + shift, 0, last), 0, 0),
            )
        )
    out = pl.BlockSpec((step, rows, width), lambda i, at: (i, 0, 0))
    table = jnp.stack([weight for row in weights for weight in row])
    return pl.pallas_call(
        lambda *refs: blend_kernel(count, step, *refs),
        grid_spec=pltpu.PrefetchScalarGridSpec(
            num_scalar_prefetch=1,
            grid=(heads // step,),
            in_specs=[pl.BlockSpec(memory_space=pltpu.SMEM)] + specs,
            out_specs=[out] * len(weights),
        ),
        out_shape=[jax.ShapeDtypeStruct((heads, rows, width), dtype)] * len(weights),
        compiler_params=PARAMS,
        cost_estimate=cost(
            2 * count * len(weights) * heads * rows * width, 4 * count * heads * rows * width
        ),
    )(jnp.zeros((1,), jnp.int32), table, *terms)


def across(value, hop, chips):
    pairs = [(2 * i + core, 2 * (i ^ hop) + core) for i in range(chips) for core in range(2)]
    return lax.ppermute(value, "seq", pairs)


def other_core(value, chips):
    return lax.ppermute(value, "seq", [(i, i ^ 1) for i in range(2 * chips)])


def orders(chips):
    bits = [1 << i for i in range(chips.bit_length() - 1)]
    return [bits, bits[::-1]]


def sum_over_heads(value):
    count = lax.axis_size("head")
    value = value.astype(BF16)
    terms = [
        lax.ppermute(value, "head", [(i, i ^ hop) for i in range(count)]) if hop else value
        for hop in range(count)
    ]
    terms = [term.astype(F32) for term in terms]
    while len(terms) > 1:
        terms = [terms[i] + terms[i + 1] for i in range(0, len(terms), 2)]
    return terms[0]


def gather_halves(grad_out):
    half = grad_out.shape[0] // 2
    pieces = [grad_out[:half], grad_out[half:]]
    return pieces[0], [lax.all_gather(p, "head", axis=1, tiled=True) for p in pieces]


def blocks_of(full, start, rows, chips, chip):
    both = full.shape[1] // chips
    return [
        lax.dynamic_slice(full, (start, (chip ^ hop) * both), (rows, both)) for hop in range(chips)
    ]


def project(fulls, blocks, second, out_weight, other, chips, chip, core, ahead, before):
    core_at = core.astype(jnp.int32).reshape(1)
    lanes = []
    for order in orders(chips):
        hops = [0]
        for bit in order[::-1]:
            hops = hops + [hop | bit for hop in hops]
        lanes.append((order, hops))
    waiting = [[], []]

    def reduce(chunk, after):
        last = []
        for lane, (order, _) in enumerate(lanes):
            keep, send, arrived = waiting[lane][chunk]
            for step, bit in enumerate(order):
                if step:
                    arrived = across(send, bit, chips)
                elif after:
                    arrived = tie(arrived, *after)
                if step < len(order) - 1:
                    keep, send = add_and_split(keep, arrived)
            waiting[lane][chunk] = (keep, arrived)
            last.append(send)
        return last, [lane[chunk][1] for lane in waiting]

    rows = fulls[0].shape[0] // 2
    own = [None, second]
    for chunk in range(4):
        if chunk:
            blocks = [
                across(block, hop, chips) if hop else block
                for hop, block in enumerate(own[chunk])
            ]
        blocks = lax.optimization_barrier((*blocks, *ahead))[:chips]
        for lane, (order, hops) in enumerate(lanes):
            send, keep = partial_sums(blocks, hops, out_weight, other, lane, core_at)
            waiting[lane].append((keep, send, across(send, order[0], chips)))
        ahead = [lane[chunk][1] for lane in waiting]
        if chunk == 1:
            sent, first = reduce(0, ahead)
            full = tie(fulls[1], *ahead)
            own += [blocks_of(full, i * rows, rows, chips, chip) for i in range(2)]
            last = reduce(1, own[2])[1]
            ahead = [*first, *before([*sent, *own[2]]), *own[3]]
    reduce(2, [*ahead, *last])
    reduce(3, None)
    ends = waiting[0] + waiting[1]
    return finish([keep for keep, _ in ends], [arrived for _, arrived in ends])


def exchange(mine, theirs, ends, chips, chip, core, reverse):
    half = mine.shape[0]
    ends = lax.dynamic_slice_in_dim(ends, core * half, half, 1)
    by_chip = ends.reshape(chips, 2, half)
    own_ends = lax.dynamic_index_in_dim(by_chip, chip, 0, False)
    chip_ends = by_chip[:, 0] + by_chip[:, 1]
    index = jnp.arange(chips)[:, None]

    def carry(source, target):
        before = source > target if reverse else source < target
        inside = (index > jnp.minimum(source, target)) & (index < jnp.maximum(source, target))
        between = jnp.sum(jnp.where(inside, chip_ends, 0.0), axis=0)
        return jnp.exp(jnp.where(before, between, -jnp.inf))

    near_first = (core == 0) != reverse
    own_scale = jnp.exp(own_ends)
    first_scale, second_scale = own_scale[int(reverse)], own_scale[1 - int(reverse)]
    one = jnp.ones((half,), F32)
    pick_near = lambda a, b: jnp.where(near_first, a, b)
    few = half // 2
    part = [slice(0, few), slice(few, half)]
    parts = [pick_near(second_scale, one), pick_near(one, second_scale)]
    lanes = []
    for heads in part:
        weights = [[weight[heads] for weight in parts]]
        chip_state = blend([mine, theirs], [heads.start] * 2, weights, few, BF16)
        lanes.append({0: chip_state[0]})
    bits = orders(chips)
    for step in range(len(bits[0])):
        last = step == len(bits[0]) - 1
        sent = []
        for order, heads, items in zip(bits, part, lanes):
            if last:
                target = chip ^ order[step]
                weights = [[carry(chip ^ o, target)[heads] for o in items]]
                total = blend(list(items.values()), [0] * len(items), weights, few, BF16)
                sent.append({0: total[0]})
            else:
                sent.append(dict(items))
        fresh = []
        for order, items, going in zip(bits, lanes, sent):
            for o, item in going.items():
                items[o | order[step]] = across(item, order[step], chips)
                fresh.append((items, o | order[step]))
        arrived = [items[o] for items, o in fresh]
        done = yield [item for going in sent for item in going.values()], arrived
        values = lax.optimization_barrier((*arrived, *done))
        for (items, o), value in zip(fresh, values):
            items[o] = value
    terms, starts = [mine, theirs], [0, 0]
    alphas = [pick_near(one, first_scale), pick_near(first_scale, one)]
    zero = jnp.zeros((half,), F32)
    weights = [[zero, pick_near(zero, one)], [pick_near(one, zero), zero]]
    for order, heads, items in zip(bits, part, lanes):
        here = (jnp.arange(half) >= heads.start) & (jnp.arange(half) < heads.stop)
        for o, item in items.items():
            if o == 0:
                continue
            scale = one if o == order[-1] else carry(chip ^ o, chip)
            terms.append(item)
            starts.append(-heads.start)
            for row, alpha in zip(weights, alphas):
                row.append(jnp.where(here, alpha * scale, 0.0))
    return tuple(blend(terms, starts, weights, half, F32))


def run_steps(steps, work, done=None):
    for step in range(64):
        try:
            sent, _ = steps.send(done)
        except StopIteration as stop:
            return stop.value
        done = work(step, sent)


def local(grad_out, out_weight, ssm_input, step_size, log_decay, b_in, c_in, skip):
    place_on_seq = lax.axis_index("seq")
    chips = lax.axis_size("seq") // 2
    chip, core = place_on_seq // 2, place_on_seq % 2
    span, heads = step_size.shape
    width = ssm_input.shape[1] // heads
    group = min(GROUP, heads // 2)
    groups = heads // group
    by_group = lambda t: t.reshape(span, groups, group).transpose(1, 0, 2)
    flat = lambda t: t.transpose(1, 0, 2).reshape(span, heads)
    mine_at = (core * (groups // 2)).astype(jnp.int32).reshape(1)
    other_at = ((1 - core) * (groups // 2)).astype(jnp.int32).reshape(1)

    first_rows, fulls = gather_halves(grad_out)
    log_decay, step_size, b_in, c_in, _ = lax.optimization_barrier(
        (log_decay, step_size, b_in, c_in, first_rows)
    )
    other_weight = other_core(out_weight, chips)
    upto = jnp.tril(jnp.ones((span, span), F32))
    running = jnp.dot(upto, log_decay, precision=HIGH)
    ends = lax.all_gather(running[-1], "seq")
    tail = jnp.exp(running[-1:] - running)
    rise = by_group(jnp.exp(running))
    running_g = by_group(running)
    running_t = running.T.reshape(groups, group, span)
    steps_g = by_group(step_size)
    skip_rows = jnp.broadcast_to(skip.reshape(groups, group, 1), (groups, group, width))
    b_rows, c_rows = b_in.T, c_in.T

    def span_both(values, scale, rows_t):
        to_other = span_states(values, scale, rows_t, other_at, groups // 2)
        theirs = other_core(to_other, chips)
        return span_states(values, scale, rows_t, mine_at, groups // 2), theirs

    mine, theirs = span_both(ssm_input, by_group(step_size * tail), b_rows)
    forward = exchange(mine, theirs, ends, chips, chip, core, False)
    _, raw = next(forward)
    for _ in range(chips.bit_length() - 2):
        _, raw = forward.send([])
    full = tie(fulls[0], other_weight, *raw)
    rows = span // 4
    own = blocks_of(full, 0, rows, chips, chip)
    blocks = [across(block, hop, chips) if hop else block for hop, block in enumerate(own)]
    second = blocks_of(tie(full, *blocks[1:]), rows, rows, chips, chip)
    tables = []

    def before(done):
        in_mine, for_theirs = run_steps(forward, None, done)
        in_other = other_core(for_theirs, chips)
        tables[:] = [in_mine, in_other, *decays(tie(running_g, *done), running_t, b_in, c_in)]
        return [in_mine, tables[-1], steps_g, skip_rows, rise, c_rows]

    grad_y = project(
        fulls, blocks, second, out_weight, other_weight, chips, chip, core, second, before
    )
    in_mine, in_other, decay, weight, cross = tables

    counts = [0, groups - groups // 2, groups // 2]
    held = ()

    def fill(step, sent):
        nonlocal held
        count = counts[step] if step < len(counts) else 0
        if count:
            held = inner_part(
                ssm_input, grad_y, b_in, c_in, tie(rise, *sent), steps_g, skip_rows, in_mine,
                in_other, core, decay, weight, cross, sum(counts[:step]), count, held, step == len(counts) - 1,
            )
        return list(held)

    mine, theirs = span_both(grad_y, rise, c_rows)
    theirs = tie(theirs, *fill(0, [mine]))
    backward = exchange(mine, theirs, ends, chips, chip, core, True)
    for_mine, for_theirs = run_steps(backward, lambda step, sent: fill(step + 1, sent))
    for_other = other_core(for_theirs, chips)
    part, cols, carries, grad_b, grad_c = held
    grad_c = sum_over_heads(grad_c)
    shared = (running_g, steps_g, cols, carries)
    grad_x, grad_b, grad_step, grad_decay = outer_part(
        ssm_input, part, b_in, in_mine, for_mine, *shared, grad_b, mine_at, None
    )
    grad_x, grad_b, grad_step, grad_decay = outer_part(
        ssm_input, part, b_in, in_other, for_other, *shared, grad_b, other_at,
        (grad_x, grad_step, grad_decay),
    )
    grad_b = sum_over_heads(grad_b)
    return (grad_x, flat(grad_step), flat(grad_decay), grad_b, grad_c)


def solution(mesh):
    in_specs = (
        P("seq", "head"),
        P("head", "seq"),
        P("seq", "head"),
        P("seq", "head"),
        P("seq", "head"),
        P("seq", None),
        P("seq", None),
        P("head"),
    )
    out_specs = (
        P("seq", "head"),
        P("seq", "head"),
        P("seq", "head"),
        P("seq", None),
        P("seq", None),
    )
    return jax.shard_map(local, mesh=mesh, in_specs=in_specs, out_specs=out_specs, check_vma=False)
```

```python
import jax
import jax.numpy as jnp
from jax import lax
from jax.experimental import pallas as pl
from jax.experimental.pallas import tpu as pltpu
from jax.sharding import PartitionSpec as P

BF16 = jnp.bfloat16
F32 = jnp.float32
HIGH = lax.Precision.HIGHEST
GROUP = 8
NN = (((1,), (0,)), ((), ()))
NT = (((1,), (1,)), ((), ()))
TN = (((0,), (0,)), ((), ()))
PARAMS = pltpu.CompilerParams(vmem_limit_bytes=28 << 20)


def mm(a, b, dims):
    return lax.dot_general(a, b, dims, preferred_element_type=F32)


def halves(a):
    high = a.astype(BF16)
    return high, (a - high.astype(F32)).astype(BF16)


def mm_right(a, b):
    width = b.shape[1]
    both = mm(a, jnp.concatenate(halves(b), axis=1), NN)
    return both[:, :width] + both[:, width:]


def mm_wide(lefts, rights):
    left = [part for a in lefts for part in halves(a)]
    right = [part for b in rights for part in [b.astype(BF16)] * 2]
    return mm(jnp.concatenate(left, axis=1), jnp.concatenate(right, axis=1), NT)


def whole(*shape):
    return pl.BlockSpec(shape, lambda i, at: (0,) * len(shape))


def tie(value, *before):
    return lax.optimization_barrier((value, *before))[0]


def cost(flops, size, exps=0):
    scale = 256
    return pl.CostEstimate(
        flops=flops // scale, bytes_accessed=size // scale, transcendentals=exps // scale
    )


def states_kernel(at_ref, v_ref, scale_ref, rows_ref, out_ref):
    del at_ref
    group = scale_ref.shape[2]
    width = v_ref.shape[1] // group
    for j in range(group):
        scaled = v_ref[:, j * width : (j + 1) * width].astype(F32) * scale_ref[0, :, j : j + 1]
        out_ref[j] = mm_right(rows_ref[...], scaled)


def span_states(values, scale, rows_t, at, count):
    groups, span, group = scale.shape
    width = values.shape[1] // (groups * group)
    states = rows_t.shape[0]
    return pl.pallas_call(
        states_kernel,
        grid_spec=pltpu.PrefetchScalarGridSpec(
            num_scalar_prefetch=1,
            grid=(count,),
            in_specs=[
                pl.BlockSpec((span, group * width), lambda i, at: (0, at[0] + i)),
                pl.BlockSpec((1, span, group), lambda i, at: (at[0] + i, 0, 0)),
                whole(states, span),
            ],
            out_specs=pl.BlockSpec((group, states, width), lambda i, at: (i, 0, 0)),
        ),
        out_shape=jax.ShapeDtypeStruct((count * group, states, width), F32),
        compiler_params=PARAMS,
        cost_estimate=cost(
            4 * span * count * group * width * states,
            count * group * width * (2 * span + 4 * states),
        ),
    )(at, values, scale, rows_t)


def decay_kernel(run_ref, run_t_ref, b_ref, c_ref, decay_ref, weight_ref, cross_ref):
    group = run_ref.shape[2]
    span = run_ref.shape[1]

    @pl.when(pl.program_id(0) == 0)
    def _():
        cross_ref[...] = mm(b_ref[...], c_ref[...], NT)

    source = lax.broadcasted_iota(jnp.int32, (span, span), 0)
    target = lax.broadcasted_iota(jnp.int32, (span, span), 1)
    causal = source <= target
    for j in range(group):
        gap = run_t_ref[0, j : j + 1, :] - run_ref[0, :, j : j + 1]
        decay = jnp.exp(jnp.where(causal, gap, -jnp.inf))
        decay_ref[j] = decay
        high, low = halves(decay * cross_ref[...])
        weight_ref[j, :, :span] = high
        weight_ref[j, :, span:] = low


def decays(running, running_t, b, c):
    groups, span, group = running.shape
    states = b.shape[1]
    fixed = lambda *shape: pl.BlockSpec(shape, lambda i: (0,) * len(shape))
    return pl.pallas_call(
        decay_kernel,
        grid=(groups,),
        in_specs=[
            pl.BlockSpec((1, span, group), lambda i: (i, 0, 0)),
            pl.BlockSpec((1, group, span), lambda i: (i, 0, 0)),
            fixed(span, states),
            fixed(span, states),
        ],
        out_specs=[
            pl.BlockSpec((group, span, span), lambda i: (i, 0, 0)),
            pl.BlockSpec((group, span, 2 * span), lambda i: (i, 0, 0)),
            fixed(span, span),
        ],
        out_shape=[
            jax.ShapeDtypeStruct((groups * group, span, span), F32),
            jax.ShapeDtypeStruct((groups * group, span, 2 * span), BF16),
            jax.ShapeDtypeStruct((span, span), F32),
        ],
        compiler_params=pltpu.CompilerParams(vmem_limit_bytes=60 << 20),
        cost_estimate=cost(
            8 * groups * group * span * span,
            8 * groups * group * span * span,
            groups * group * span * span,
        ),
    )(running, running_t, b, c)


def inner_kernel(
    first, last, at_ref, x_ref, y_ref, b_ref, c_ref, rise_ref, step_ref, skip_ref,
    mine_ref, other_ref, decay_ref, weight_ref, cross_ref, *rest,
):
    held = rest[: 0 if first else 5]
    partial_ref, col_ref, carry_ref, mix_ref, grad_c_ref, rows = rest[len(held) :]
    group = step_ref.shape[2]
    width = x_ref.shape[1] // group

    @pl.when(pl.program_id(0) == 0)
    def _():
        mix_ref[...] = jnp.zeros_like(mix_ref) if first else held[3][...]
        grad_c_ref[...] = jnp.zeros_like(grad_c_ref) if first else held[4][...]

    is_mine = (at_ref[0] + pl.program_id(0)) // at_ref[2] == at_ref[1]
    lefts, rights = [], []
    for j in range(group):
        columns = slice(j * width, (j + 1) * width)
        y = y_ref[:, columns]
        x_wide = x_ref[:, columns].astype(F32)
        y_wide = y.astype(F32)
        step_col = step_ref[0, :, j : j + 1]
        stepped = jnp.concatenate(halves(x_wide * step_col), axis=1)
        pairs = decay_ref[j] * mm(stepped, jnp.concatenate([y, y], axis=1), NT)
        mix_ref[...] += pairs
        rows[j : j + 1, :] = jnp.sum(pairs * cross_ref[...], axis=0, keepdims=True)
        inner = mm(weight_ref[j], jnp.concatenate([y, y], axis=0), NN)
        col_ref[0, :, j : j + 1] = jnp.sum(x_wide * inner, axis=1, keepdims=True)
        partial_ref[:, columns] = step_col * inner + skip_ref[0, j : j + 1, :] * y_wide
        state = jnp.where(is_mine, mine_ref[j], other_ref[j])
        scaled = y_wide * rise_ref[0, :, j : j + 1]
        lefts.append(scaled)
        rights.append(state)
        carry_ref[0, :, j : j + 1] = jnp.sum(
            scaled * mm_right(c_ref[...], state), axis=1, keepdims=True
        )
    grad_c_ref[...] += mm_wide(lefts, rights)
    carry_ref[0] += rows[...].T

    if last:

        @pl.when(pl.program_id(0) == pl.num_programs(0) - 1)
        def _():
            high, low = halves(mix_ref[...])
            mix_ref[...] = mm(high, c_ref[...], NN) + mm(low, c_ref[...], NN)
            grad_c_ref[...] += mm(high, b_ref[...], TN) + mm(low, b_ref[...], TN)


def inner_part(
    x, y, b, c, rise, steps, skip_rows, mine, other, core, decay, weight, cross, at, count, held,
    last,
):
    groups, span, group = steps.shape
    heads = groups * group
    width = x.shape[1] // heads
    states = b.shape[1]
    block = pl.BlockSpec((span, group * width), lambda i, at: (0, at[0] + i))
    table = pl.BlockSpec((1, span, group), lambda i, at: (at[0] + i, 0, 0))
    per_head = lambda *shape: pl.BlockSpec((group, *shape), lambda i, at: (at[0] + i, 0, 0))
    any_place = pl.BlockSpec(memory_space=pl.ANY)
    half = groups // 2
    near = lambda i, at: (jnp.clip(at[0] + i - at[1] * half, 0, half - 1), 0, 0)
    far = lambda i, at: (jnp.clip(at[0] + i - (1 - at[1]) * half, 0, half - 1), 0, 0)
    at = jnp.stack([jnp.int32(at), core.astype(jnp.int32), jnp.int32(half)])
    return pl.pallas_call(
        lambda *refs: inner_kernel(not held, last, *refs),
        grid_spec=pltpu.PrefetchScalarGridSpec(
            num_scalar_prefetch=1,
            grid=(count,),
            in_specs=[
                block,
                block,
                whole(span, states),
                whole(span, states),
                table,
                table,
                pl.BlockSpec((1, group, width), lambda i, at: (at[0] + i, 0, 0)),
                pl.BlockSpec((group, states, width), near),
                pl.BlockSpec((group, states, width), far),
                per_head(span, span),
                per_head(span, 2 * span),
                whole(span, span),
            ]
            + ([any_place] * 3 + [whole(span, states)] * 2 if held else []),
            out_specs=[block, table, table, whole(span, states), whole(span, states)],
            scratch_shapes=[pltpu.VMEM((group, span), F32)],
        ),
        out_shape=[
            jax.ShapeDtypeStruct((span, heads * width), F32),
            jax.ShapeDtypeStruct((groups, span, group), F32),
            jax.ShapeDtypeStruct((groups, span, group), F32),
            jax.ShapeDtypeStruct((span, states), F32),
            jax.ShapeDtypeStruct((span, states), F32),
        ],
        input_output_aliases={13: 0, 14: 1, 15: 2} if held else {},
        compiler_params=PARAMS,
        cost_estimate=cost(
            14 * span * count * group * width * states,
            count * group * (8 * span * width + 4 * width * states + 8 * span * span),
        ),
    )(
        at, x, y, b, c, rise, steps, skip_rows, mine, other, decay, weight, cross, *held
    )


def outer_kernel(
    at_ref, x_ref, part_ref, b_ref, state_ref, grad_state_ref, run_ref, step_ref,
    col_ref, carry_ref, grad_b_in_ref, *rest,
):
    del at_ref
    grad_x_ref, grad_b_ref, grad_step_ref, grad_decay_ref, late, overlap = rest[-6:]
    group = step_ref.shape[2]
    span = x_ref.shape[0]
    width = x_ref.shape[1] // group

    @pl.when(pl.program_id(0) == 0)
    def _():
        grad_b_ref[...] = grad_b_in_ref[...]

    running = run_ref[0]
    end = running[span - 1 : span, :]
    tails = jnp.exp(end - running)
    steps = step_ref[0]
    lefts, rights = [], []
    for j in range(group):
        columns = slice(j * width, (j + 1) * width)
        tail_col = tails[:, j : j + 1]
        step_col = steps[:, j : j + 1]
        grad_state = grad_state_ref[j]
        x = x_ref[:, columns].astype(F32)
        outer = mm_right(b_ref[...], grad_state) * tail_col
        late[:, j : j + 1] = jnp.sum(x * outer, axis=1, keepdims=True)
        grad_x_ref[:, columns] = (part_ref[:, columns] + step_col * outer).astype(BF16)
        lefts.append(x * (step_col * tail_col))
        rights.append(grad_state)
        shared = jnp.sum(grad_state * state_ref[j], axis=0, keepdims=True)
        overlap[:, j : j + 1] = jnp.sum(shared, axis=1, keepdims=True)

    grad_b_ref[...] += mm_wide(lefts, rights)
    grad_step = col_ref[0] + late[...]
    grad_step_ref[0] = grad_step
    change = carry_ref[0] - steps * grad_step
    last = jnp.exp(end) * overlap[...] + jnp.sum(steps * late[...], axis=0, keepdims=True)
    source = lax.broadcasted_iota(jnp.int32, (span, span), 0)
    target = lax.broadcasted_iota(jnp.int32, (span, span), 1)
    from_here = (source <= target).astype(BF16)
    high, low = halves(change)
    lowest = (change - high.astype(F32) - low.astype(F32)).astype(BF16)
    grad_decay_ref[0] = last + (
        mm(from_here, high, NN) + mm(from_here, low, NN) + mm(from_here, lowest, NN)
    )


def outer_part(x, part, b, state, grad_state, running, steps, cols, carries, grad_b, at, before):
    groups, span, group = steps.shape
    heads = groups * group
    count = grad_state.shape[0] // group
    width = x.shape[1] // heads
    states = b.shape[1]
    block = pl.BlockSpec((span, group * width), lambda i, at: (0, at[0] + i))
    table = pl.BlockSpec((1, span, group), lambda i, at: (at[0] + i, 0, 0))
    held = [] if before is None else list(before)
    return pl.pallas_call(
        outer_kernel,
        grid_spec=pltpu.PrefetchScalarGridSpec(
            num_scalar_prefetch=1,
            grid=(count,),
            in_specs=[
                block,
                block,
                whole(span, states),
                pl.BlockSpec((group, states, width), lambda i, at: (i, 0, 0)),
                pl.BlockSpec((group, states, width), lambda i, at: (i, 0, 0)),
                table,
                table,
                table,
                table,
                whole(span, states),
            ]
            + [pl.BlockSpec(memory_space=pl.ANY)] * len(held),
            out_specs=[block, whole(span, states), table, table],
            scratch_shapes=[pltpu.VMEM((span, group), F32), pltpu.VMEM((1, group), F32)],
        ),
        out_shape=[
            jax.ShapeDtypeStruct((span, heads * width), BF16),
            jax.ShapeDtypeStruct((span, states), F32),
            jax.ShapeDtypeStruct((groups, span, group), F32),
            jax.ShapeDtypeStruct((groups, span, group), F32),
        ],
        input_output_aliases={11: 0, 12: 2, 13: 3} if held else {},
        compiler_params=PARAMS,
        cost_estimate=cost(
            8 * span * count * group * width * states,
            count * group * width * (8 * span + 8 * states),
        ),
    )(at, x, part, b, state, grad_state, running, steps, cols, carries, grad_b, *held)


def project_kernel(hops, at_ref, *refs):
    count = len(hops)
    pieces, (own_ref, other_ref, send_ref, keep_ref, left) = refs[:count], refs[count:]
    rows = pieces[0].shape[0]
    depth = own_ref.shape[1]

    @pl.when(pl.program_id(0) == 0)
    def _():
        first = pl.multiple_of(at_ref[0] * depth, depth)
        second = pl.multiple_of((1 - at_ref[0]) * depth, depth)
        for place, hop in enumerate(hops):
            left[pl.ds(place * rows, rows), :depth] = pieces[hop][:, pl.ds(first, depth)]
            left[pl.ds(place * rows, rows), depth:] = pieces[hop][:, pl.ds(second, depth)]

    total = mm(left[:, :depth], own_ref[...], NT) + mm(left[:, depth:], other_ref[...], NT)
    middle = rows * (count // 2)
    keep_ref[...] = total[:middle]
    send_ref[...] = total[middle:].astype(BF16)


def partial_sums(pieces, hops, own, other, lane, core):
    rows, both = pieces[0].shape
    depth = own.shape[1]
    half = own.shape[0] // 2
    tile = min(512, half)
    steps = half // tile
    middle = rows * (len(hops) // 2)
    weight = pl.BlockSpec((tile, depth), lambda i, at: (lane * steps + i, 0))
    return pl.pallas_call(
        lambda *refs: project_kernel(hops, *refs),
        grid_spec=pltpu.PrefetchScalarGridSpec(
            num_scalar_prefetch=1,
            grid=(steps,),
            in_specs=[whole(rows, both)] * len(hops) + [weight, weight],
            out_specs=[pl.BlockSpec((middle, tile), lambda i, at: (0, i))] * 2,
            scratch_shapes=[pltpu.VMEM((rows * len(hops), both), BF16)],
        ),
        out_shape=[
            jax.ShapeDtypeStruct((middle, half), BF16),
            jax.ShapeDtypeStruct((middle, half), F32),
        ],
        compiler_params=PARAMS,
        cost_estimate=cost(
            2 * rows * len(hops) * both * half, 2 * both * half + 6 * middle * half
        ),
    )(core, *pieces, own, other)


def finish_kernel(count, *refs):
    keeps, arrived, out_ref = refs[: 2 * count], refs[2 * count : -1], refs[-1]
    steps = pl.num_programs(0) // 2
    for lane in range(2):

        @pl.when(pl.program_id(0) // steps == lane)
        def _():
            start = 0
            for chunk in range(count):
                at = lane * count + chunk
                total = keeps[at][...] + arrived[at][...].astype(F32)
                rows = total.shape[0]
                out_ref[start : start + rows, :] = total.astype(BF16)
                start += rows


def finish(keeps, arrived):
    count = len(keeps) // 2
    half = arrived[0].shape[1]
    span = sum(a.shape[0] for a in arrived) // 2
    tile = min(1024, half)
    steps = half // tile
    place = [lambda i: (0, jnp.minimum(i, steps - 1)), lambda i: (0, jnp.maximum(i - steps, 0))]
    specs = [
        pl.BlockSpec((a.shape[0], tile), place[i // count]) for i, a in enumerate(arrived)
    ]
    return pl.pallas_call(
        lambda *refs: finish_kernel(count, *refs),
        grid=(2 * steps,),
        in_specs=specs + specs,
        out_specs=pl.BlockSpec((span, tile), lambda i: (0, i)),
        out_shape=jax.ShapeDtypeStruct((span, 2 * half), BF16),
        compiler_params=PARAMS,
        cost_estimate=cost(4 * span * half, 16 * span * half),
    )(*keeps, *arrived)


def split_kernel(keep_ref, arrived_ref, out_ref, send_ref):
    total = keep_ref[...] + arrived_ref[...].astype(F32)
    size = out_ref.shape[0]
    out_ref[...] = total[:size]
    send_ref[...] = total[size:].astype(BF16)


def add_and_split(keep, arrived):
    rows, half = keep.shape
    tile = min(1024, half)
    column = lambda size: pl.BlockSpec((size, tile), lambda i: (0, i))
    return pl.pallas_call(
        split_kernel,
        grid=(half // tile,),
        in_specs=[column(rows), column(rows)],
        out_specs=[column(rows // 2), column(rows // 2)],
        out_shape=[
            jax.ShapeDtypeStruct((rows // 2, half), F32),
            jax.ShapeDtypeStruct((rows // 2, half), BF16),
        ],
        compiler_params=PARAMS,
        cost_estimate=cost(rows * half, 9 * rows * half),
    )(keep, arrived)


def blend_kernel(count, step, at_ref, *refs):
    del at_ref
    weight_ref, terms, outs = refs[0], refs[1 : 1 + count], refs[1 + count :]
    for j in range(step):
        head = pl.program_id(0) * step + j
        values = [term[j].astype(F32) for term in terms]
        for k, out in enumerate(outs):
            total = weight_ref[k * count, head] * values[0]
            for i in range(1, count):
                total += weight_ref[k * count + i, head] * values[i]
            out[j] = total.astype(out.dtype)


def blend(terms, starts, weights, heads, dtype):
    count = len(terms)
    step = max(1, min(4, heads // 2))
    while any(start % step for start in starts):
        step //= 2
    rows, width = terms[0].shape[1:]
    specs = []
    for term, start in zip(terms, starts):
        last = term.shape[0] // step - 1
        shift = start // step
        specs.append(
            pl.BlockSpec(
                (step, rows, width),
                lambda i, at, last=last, shift=shift: (jnp.clip(i + shift, 0, last), 0, 0),
            )
        )
    out = pl.BlockSpec((step, rows, width), lambda i, at: (i, 0, 0))
    table = jnp.stack([weight for row in weights for weight in row])
    return pl.pallas_call(
        lambda *refs: blend_kernel(count, step, *refs),
        grid_spec=pltpu.PrefetchScalarGridSpec(
            num_scalar_prefetch=1,
            grid=(heads // step,),
            in_specs=[pl.BlockSpec(memory_space=pltpu.SMEM)] + specs,
            out_specs=[out] * len(weights),
        ),
        out_shape=[jax.ShapeDtypeStruct((heads, rows, width), dtype)] * len(weights),
        compiler_params=PARAMS,
        cost_estimate=cost(
            2 * count * len(weights) * heads * rows * width, 4 * count * heads * rows * width
        ),
    )(jnp.zeros((1,), jnp.int32), table, *terms)


def across(value, hop, chips):
    pairs = [(2 * i + core, 2 * (i ^ hop) + core) for i in range(chips) for core in range(2)]
    return lax.ppermute(value, "seq", pairs)


def other_core(value, chips):
    return lax.ppermute(value, "seq", [(i, i ^ 1) for i in range(2 * chips)])


def orders(chips):
    bits = [1 << i for i in range(chips.bit_length() - 1)]
    return [bits, bits[::-1]]


def sum_over_heads(value):
    count = lax.axis_size("head")
    value = value.astype(BF16)
    terms = [
        lax.ppermute(value, "head", [(i, i ^ hop) for i in range(count)]) if hop else value
        for hop in range(count)
    ]
    terms = [term.astype(F32) for term in terms]
    while len(terms) > 1:
        terms = [terms[i] + terms[i + 1] for i in range(0, len(terms), 2)]
    return terms[0]


def gather_halves(grad_out):
    half = grad_out.shape[0] // 2
    pieces = [grad_out[:half], grad_out[half:]]
    return pieces[0], [lax.all_gather(p, "head", axis=1, tiled=True) for p in pieces]


def blocks_of(full, start, rows, chips, chip):
    both = full.shape[1] // chips
    return [
        lax.dynamic_slice(full, (start, (chip ^ hop) * both), (rows, both)) for hop in range(chips)
    ]


def project(fulls, blocks, second, out_weight, other, chips, chip, core, ahead, before):
    core_at = core.astype(jnp.int32).reshape(1)
    lanes = []
    for order in orders(chips):
        hops = [0]
        for bit in order[::-1]:
            hops = hops + [hop | bit for hop in hops]
        lanes.append((order, hops))
    waiting = [[], []]

    def reduce(chunk, after):
        last = []
        for lane, (order, _) in enumerate(lanes):
            keep, send, arrived = waiting[lane][chunk]
            for step, bit in enumerate(order):
                if step:
                    arrived = across(send, bit, chips)
                elif after:
                    arrived = tie(arrived, *after)
                if step < len(order) - 1:
                    keep, send = add_and_split(keep, arrived)
            waiting[lane][chunk] = (keep, arrived)
            last.append(send)
        return last, [lane[chunk][1] for lane in waiting]

    rows = fulls[0].shape[0] // 2
    own = [None, second]
    for chunk in range(4):
        if chunk:
            blocks = [
                across(block, hop, chips) if hop else block
                for hop, block in enumerate(own[chunk])
            ]
        blocks = lax.optimization_barrier((*blocks, *ahead))[:chips]
        for lane, (order, hops) in enumerate(lanes):
            send, keep = partial_sums(blocks, hops, out_weight, other, lane, core_at)
            waiting[lane].append((keep, send, across(send, order[0], chips)))
        ahead = [lane[chunk][1] for lane in waiting]
        if chunk == 1:
            first = reduce(0, ahead)[1]
            full = tie(fulls[1], *ahead)
            own += [blocks_of(full, i * rows, rows, chips, chip) for i in range(2)]
            last = reduce(1, own[2])[1]
            ahead = [*first, *own[3]]
    sent, _ = reduce(2, [*ahead, *last])
    reduce(3, before([*ahead, *sent]))
    ends = waiting[0] + waiting[1]
    return finish([keep for keep, _ in ends], [arrived for _, arrived in ends])


def exchange(mine, theirs, ends, chips, chip, core, reverse):
    half = mine.shape[0]
    ends = lax.dynamic_slice_in_dim(ends, core * half, half, 1)
    by_chip = ends.reshape(chips, 2, half)
    own_ends = lax.dynamic_index_in_dim(by_chip, chip, 0, False)
    chip_ends = by_chip[:, 0] + by_chip[:, 1]
    index = jnp.arange(chips)[:, None]

    def carry(source, target):
        before = source > target if reverse else source < target
        inside = (index > jnp.minimum(source, target)) & (index < jnp.maximum(source, target))
        between = jnp.sum(jnp.where(inside, chip_ends, 0.0), axis=0)
        return jnp.exp(jnp.where(before, between, -jnp.inf))

    near_first = (core == 0) != reverse
    own_scale = jnp.exp(own_ends)
    first_scale, second_scale = own_scale[int(reverse)], own_scale[1 - int(reverse)]
    one = jnp.ones((half,), F32)
    pick_near = lambda a, b: jnp.where(near_first, a, b)
    few = half // 2
    part = [slice(0, few), slice(few, half)]
    parts = [pick_near(second_scale, one), pick_near(one, second_scale)]
    lanes = []
    for heads in part:
        weights = [[weight[heads] for weight in parts]]
        chip_state = blend([mine, theirs], [heads.start] * 2, weights, few, BF16)
        lanes.append({0: chip_state[0]})
    bits = orders(chips)
    for step in range(len(bits[0])):
        last = step == len(bits[0]) - 1
        sent = []
        for order, heads, items in zip(bits, part, lanes):
            if last:
                target = chip ^ order[step]
                weights = [[carry(chip ^ o, target)[heads] for o in items]]
                total = blend(list(items.values()), [0] * len(items), weights, few, BF16)
                sent.append({0: total[0]})
            else:
                sent.append(dict(items))
        fresh = []
        for order, items, going in zip(bits, lanes, sent):
            for o, item in going.items():
                items[o | order[step]] = across(item, order[step], chips)
                fresh.append((items, o | order[step]))
        arrived = [items[o] for items, o in fresh]
        done = yield [item for going in sent for item in going.values()], arrived
        values = lax.optimization_barrier((*arrived, *done))
        for (items, o), value in zip(fresh, values):
            items[o] = value
    terms, starts = [mine, theirs], [0, 0]
    alphas = [pick_near(one, first_scale), pick_near(first_scale, one)]
    zero = jnp.zeros((half,), F32)
    weights = [[zero, pick_near(zero, one)], [pick_near(one, zero), zero]]
    for order, heads, items in zip(bits, part, lanes):
        here = (jnp.arange(half) >= heads.start) & (jnp.arange(half) < heads.stop)
        for o, item in items.items():
            if o == 0:
                continue
            scale = one if o == order[-1] else carry(chip ^ o, chip)
            terms.append(item)
            starts.append(-heads.start)
            for row, alpha in zip(weights, alphas):
                row.append(jnp.where(here, alpha * scale, 0.0))
    return tuple(blend(terms, starts, weights, half, F32))


def run_steps(steps, work, done=None):
    for step in range(64):
        try:
            sent, _ = steps.send(done)
        except StopIteration as stop:
            return stop.value
        done = work(step, sent)


def local(grad_out, out_weight, ssm_input, step_size, log_decay, b_in, c_in, skip):
    place_on_seq = lax.axis_index("seq")
    chips = lax.axis_size("seq") // 2
    chip, core = place_on_seq // 2, place_on_seq % 2
    span, heads = step_size.shape
    width = ssm_input.shape[1] // heads
    group = min(GROUP, heads // 2)
    groups = heads // group
    by_group = lambda t: t.reshape(span, groups, group).transpose(1, 0, 2)
    flat = lambda t: t.transpose(1, 0, 2).reshape(span, heads)
    mine_at = (core * (groups // 2)).astype(jnp.int32).reshape(1)
    other_at = ((1 - core) * (groups // 2)).astype(jnp.int32).reshape(1)

    first_rows, fulls = gather_halves(grad_out)
    log_decay, step_size, b_in, c_in, _ = lax.optimization_barrier(
        (log_decay, step_size, b_in, c_in, first_rows)
    )
    other_weight = other_core(out_weight, chips)
    upto = jnp.tril(jnp.ones((span, span), F32))
    running = jnp.dot(upto, log_decay, precision=HIGH)
    ends = lax.all_gather(running[-1], "seq")
    tail = jnp.exp(running[-1:] - running)
    rise = by_group(jnp.exp(running))
    running_g = by_group(running)
    running_t = running.T.reshape(groups, group, span)
    steps_g = by_group(step_size)
    skip_rows = jnp.broadcast_to(skip.reshape(groups, group, 1), (groups, group, width))
    b_rows, c_rows = b_in.T, c_in.T

    def span_both(values, scale, rows_t):
        to_other = span_states(values, scale, rows_t, other_at, groups // 2)
        theirs = other_core(to_other, chips)
        return span_states(values, scale, rows_t, mine_at, groups // 2), theirs

    mine, theirs = span_both(ssm_input, by_group(step_size * tail), b_rows)
    forward = exchange(mine, theirs, ends, chips, chip, core, False)
    _, raw = next(forward)
    for _ in range(chips.bit_length() - 2):
        _, raw = forward.send([])
    full = tie(fulls[0], other_weight, *raw)
    rows = span // 4
    own = blocks_of(full, 0, rows, chips, chip)
    blocks = [across(block, hop, chips) if hop else block for hop, block in enumerate(own)]
    second = blocks_of(tie(full, *blocks[1:]), rows, rows, chips, chip)
    tables = []

    def before(done):
        in_mine, for_theirs = run_steps(forward, None, done)
        in_other = other_core(for_theirs, chips)
        tables[:] = [in_mine, in_other, *decays(tie(running_g, *done), running_t, b_in, c_in)]
        return [in_mine, tables[-1], steps_g, skip_rows, rise, c_rows]

    grad_y = project(
        fulls, blocks, second, out_weight, other_weight, chips, chip, core, second, before
    )
    in_mine, in_other, decay, weight, cross = tables

    counts = [0, groups - groups // 2, groups // 2]
    held = ()

    def fill(step, sent):
        nonlocal held
        count = counts[step] if step < len(counts) else 0
        if count:
            held = inner_part(
                ssm_input, grad_y, b_in, c_in, tie(rise, *sent), steps_g, skip_rows, in_mine,
                in_other, core, decay, weight, cross, sum(counts[:step]), count, held, step == len(counts) - 1,
            )
        return list(held)

    mine, theirs = span_both(grad_y, rise, c_rows)
    theirs = tie(theirs, *fill(0, [mine]))
    backward = exchange(mine, theirs, ends, chips, chip, core, True)
    for_mine, for_theirs = run_steps(backward, lambda step, sent: fill(step + 1, sent))
    for_other = other_core(for_theirs, chips)
    part, cols, carries, grad_b, grad_c = held
    grad_c = sum_over_heads(grad_c)
    shared = (running_g, steps_g, cols, carries)
    grad_x, grad_b, grad_step, grad_decay = outer_part(
        ssm_input, part, b_in, in_mine, for_mine, *shared, grad_b, mine_at, None
    )
    grad_x, grad_b, grad_step, grad_decay = outer_part(
        ssm_input, part, b_in, in_other, for_other, *shared, grad_b, other_at,
        (grad_x, grad_step, grad_decay),
    )
    grad_b = sum_over_heads(grad_b)
    return (grad_x, flat(grad_step), flat(grad_decay), grad_b, grad_c)


def solution(mesh):
    in_specs = (
        P("seq", "head"),
        P("head", "seq"),
        P("seq", "head"),
        P("seq", "head"),
        P("seq", "head"),
        P("seq", None),
        P("seq", None),
        P("head"),
    )
    out_specs = (
        P("seq", "head"),
        P("seq", "head"),
        P("seq", "head"),
        P("seq", None),
        P("seq", None),
    )
    return jax.shard_map(local, mesh=mesh, in_specs=in_specs, out_specs=out_specs, check_vma=False)
```

```python
import jax
import jax.numpy as jnp
from jax import lax
from jax.experimental import pallas as pl
from jax.experimental.pallas import tpu as pltpu
from jax.sharding import PartitionSpec as P

BF16 = jnp.bfloat16
F32 = jnp.float32
HIGH = lax.Precision.HIGHEST
GROUP = 8
NN = (((1,), (0,)), ((), ()))
NT = (((1,), (1,)), ((), ()))
TN = (((0,), (0,)), ((), ()))
PARAMS = pltpu.CompilerParams(vmem_limit_bytes=28 << 20)


def mm(a, b, dims):
    return lax.dot_general(a, b, dims, preferred_element_type=F32)


def halves(a):
    high = a.astype(BF16)
    return high, (a - high.astype(F32)).astype(BF16)


def mm_right(a, b):
    width = b.shape[1]
    both = mm(a, jnp.concatenate(halves(b), axis=1), NN)
    return both[:, :width] + both[:, width:]


def mm_wide(lefts, rights):
    left = [part for a in lefts for part in halves(a)]
    right = [part for b in rights for part in [b.astype(BF16)] * 2]
    return mm(jnp.concatenate(left, axis=1), jnp.concatenate(right, axis=1), NT)


def whole(*shape):
    return pl.BlockSpec(shape, lambda i, at: (0,) * len(shape))


def tie(value, *before):
    return lax.optimization_barrier((value, *before))[0]


def cost(flops, size, exps=0):
    scale = 256
    return pl.CostEstimate(
        flops=flops // scale, bytes_accessed=size // scale, transcendentals=exps // scale
    )


def states_kernel(at_ref, v_ref, scale_ref, rows_ref, out_ref):
    del at_ref
    group = scale_ref.shape[2]
    width = v_ref.shape[1] // group
    for j in range(group):
        scaled = v_ref[:, j * width : (j + 1) * width].astype(F32) * scale_ref[0, :, j : j + 1]
        out_ref[j] = mm_right(rows_ref[...], scaled)


def span_states(values, scale, rows_t, at, count):
    groups, span, group = scale.shape
    width = values.shape[1] // (groups * group)
    states = rows_t.shape[0]
    return pl.pallas_call(
        states_kernel,
        grid_spec=pltpu.PrefetchScalarGridSpec(
            num_scalar_prefetch=1,
            grid=(count,),
            in_specs=[
                pl.BlockSpec((span, group * width), lambda i, at: (0, at[0] + i)),
                pl.BlockSpec((1, span, group), lambda i, at: (at[0] + i, 0, 0)),
                whole(states, span),
            ],
            out_specs=pl.BlockSpec((group, states, width), lambda i, at: (i, 0, 0)),
        ),
        out_shape=jax.ShapeDtypeStruct((count * group, states, width), F32),
        compiler_params=PARAMS,
        cost_estimate=cost(
            4 * span * count * group * width * states,
            count * group * width * (2 * span + 4 * states),
        ),
    )(at, values, scale, rows_t)


def decay_kernel(run_ref, run_t_ref, b_ref, c_ref, decay_ref, weight_ref, cross_ref):
    group = run_ref.shape[2]
    span = run_ref.shape[1]

    @pl.when(pl.program_id(0) == 0)
    def _():
        cross_ref[...] = mm(b_ref[...], c_ref[...], NT)

    source = lax.broadcasted_iota(jnp.int32, (span, span), 0)
    target = lax.broadcasted_iota(jnp.int32, (span, span), 1)
    causal = source <= target
    for j in range(group):
        gap = run_t_ref[0, j : j + 1, :] - run_ref[0, :, j : j + 1]
        decay = jnp.exp(jnp.where(causal, gap, -jnp.inf))
        decay_ref[j] = decay
        high, low = halves(decay * cross_ref[...])
        weight_ref[j, :, :span] = high
        weight_ref[j, :, span:] = low


def decays(running, running_t, b, c):
    groups, span, group = running.shape
    states = b.shape[1]
    fixed = lambda *shape: pl.BlockSpec(shape, lambda i: (0,) * len(shape))
    return pl.pallas_call(
        decay_kernel,
        grid=(groups,),
        in_specs=[
            pl.BlockSpec((1, span, group), lambda i: (i, 0, 0)),
            pl.BlockSpec((1, group, span), lambda i: (i, 0, 0)),
            fixed(span, states),
            fixed(span, states),
        ],
        out_specs=[
            pl.BlockSpec((group, span, span), lambda i: (i, 0, 0)),
            pl.BlockSpec((group, span, 2 * span), lambda i: (i, 0, 0)),
            fixed(span, span),
        ],
        out_shape=[
            jax.ShapeDtypeStruct((groups * group, span, span), F32),
            jax.ShapeDtypeStruct((groups * group, span, 2 * span), BF16),
            jax.ShapeDtypeStruct((span, span), F32),
        ],
        compiler_params=PARAMS,
        cost_estimate=cost(
            8 * groups * group * span * span,
            8 * groups * group * span * span,
            groups * group * span * span,
        ),
    )(running, running_t, b, c)


def inner_kernel(
    first, last, at_ref, x_ref, y_ref, b_ref, c_ref, rise_ref, step_ref, skip_ref,
    state_ref, decay_ref, weight_ref, cross_ref, *rest,
):
    del at_ref
    held = rest[: 0 if first else 5]
    partial_ref, col_ref, carry_ref, mix_ref, grad_c_ref, rows = rest[len(held) :]
    group = step_ref.shape[2]
    width = x_ref.shape[1] // group

    @pl.when(pl.program_id(0) == 0)
    def _():
        mix_ref[...] = jnp.zeros_like(mix_ref) if first else held[3][...]
        grad_c_ref[...] = jnp.zeros_like(grad_c_ref) if first else held[4][...]

    lefts, rights = [], []
    for j in range(group):
        columns = slice(j * width, (j + 1) * width)
        y = y_ref[:, columns]
        x_wide = x_ref[:, columns].astype(F32)
        y_wide = y.astype(F32)
        step_col = step_ref[0, :, j : j + 1]
        stepped = jnp.concatenate(halves(x_wide * step_col), axis=1)
        pairs = decay_ref[j] * mm(stepped, jnp.concatenate([y, y], axis=1), NT)
        mix_ref[...] += pairs
        rows[j : j + 1, :] = jnp.sum(pairs * cross_ref[...], axis=0, keepdims=True)
        inner = mm(weight_ref[j], jnp.concatenate([y, y], axis=0), NN)
        col_ref[0, :, j : j + 1] = jnp.sum(x_wide * inner, axis=1, keepdims=True)
        partial_ref[:, columns] = step_col * inner + skip_ref[0, j : j + 1, :] * y_wide
        state = state_ref[j]
        scaled = y_wide * rise_ref[0, :, j : j + 1]
        lefts.append(scaled)
        rights.append(state)
        carry_ref[0, :, j : j + 1] = jnp.sum(
            scaled * mm_right(c_ref[...], state), axis=1, keepdims=True
        )
    grad_c_ref[...] += mm_wide(lefts, rights)
    carry_ref[0] += rows[...].T

    if last:

        @pl.when(pl.program_id(0) == pl.num_programs(0) - 1)
        def _():
            high, low = halves(mix_ref[...])
            mix_ref[...] = mm(high, c_ref[...], NN) + mm(low, c_ref[...], NN)
            grad_c_ref[...] += mm(high, b_ref[...], TN) + mm(low, b_ref[...], TN)


def inner_part(
    x, y, b, c, rise, steps, skip_rows, incoming, decay, weight, cross, at, count, held, last
):
    groups, span, group = steps.shape
    heads = groups * group
    width = x.shape[1] // heads
    states = b.shape[1]
    block = pl.BlockSpec((span, group * width), lambda i, at: (0, at[0] + i))
    table = pl.BlockSpec((1, span, group), lambda i, at: (at[0] + i, 0, 0))
    per_head = lambda *shape: pl.BlockSpec((group, *shape), lambda i, at: (at[0] + i, 0, 0))
    any_place = pl.BlockSpec(memory_space=pl.ANY)
    return pl.pallas_call(
        lambda *refs: inner_kernel(not held, last, *refs),
        grid_spec=pltpu.PrefetchScalarGridSpec(
            num_scalar_prefetch=1,
            grid=(count,),
            in_specs=[
                block,
                block,
                whole(span, states),
                whole(span, states),
                table,
                table,
                pl.BlockSpec((1, group, width), lambda i, at: (at[0] + i, 0, 0)),
                per_head(states, width),
                per_head(span, span),
                per_head(span, 2 * span),
                whole(span, span),
            ]
            + ([any_place] * 3 + [whole(span, states)] * 2 if held else []),
            out_specs=[block, table, table, whole(span, states), whole(span, states)],
            scratch_shapes=[pltpu.VMEM((group, span), F32)],
        ),
        out_shape=[
            jax.ShapeDtypeStruct((span, heads * width), F32),
            jax.ShapeDtypeStruct((groups, span, group), F32),
            jax.ShapeDtypeStruct((groups, span, group), F32),
            jax.ShapeDtypeStruct((span, states), F32),
            jax.ShapeDtypeStruct((span, states), F32),
        ],
        input_output_aliases={12: 0, 13: 1, 14: 2} if held else {},
        compiler_params=PARAMS,
        cost_estimate=cost(
            14 * span * count * group * width * states,
            count * group * (8 * span * width + 4 * width * states + 8 * span * span),
        ),
    )(
        jnp.full((1,), at, jnp.int32), x, y, b, c, rise, steps, skip_rows, incoming,
        decay, weight, cross, *held,
    )


def outer_kernel(
    at_ref, x_ref, part_ref, b_ref, state_ref, grad_state_ref, run_ref, step_ref,
    col_ref, carry_ref, grad_b_in_ref, *rest,
):
    del at_ref
    grad_x_ref, grad_b_ref, grad_step_ref, grad_decay_ref, late, overlap = rest[-6:]
    group = step_ref.shape[2]
    span = x_ref.shape[0]
    width = x_ref.shape[1] // group

    @pl.when(pl.program_id(0) == 0)
    def _():
        grad_b_ref[...] = grad_b_in_ref[...]

    running = run_ref[0]
    end = running[span - 1 : span, :]
    tails = jnp.exp(end - running)
    steps = step_ref[0]
    lefts, rights = [], []
    for j in range(group):
        columns = slice(j * width, (j + 1) * width)
        tail_col = tails[:, j : j + 1]
        step_col = steps[:, j : j + 1]
        grad_state = grad_state_ref[j]
        x = x_ref[:, columns].astype(F32)
        outer = mm_right(b_ref[...], grad_state) * tail_col
        late[:, j : j + 1] = jnp.sum(x * outer, axis=1, keepdims=True)
        grad_x_ref[:, columns] = (part_ref[:, columns] + step_col * outer).astype(BF16)
        lefts.append(x * (step_col * tail_col))
        rights.append(grad_state)
        shared = jnp.sum(grad_state * state_ref[j], axis=0, keepdims=True)
        overlap[:, j : j + 1] = jnp.sum(shared, axis=1, keepdims=True)

    grad_b_ref[...] += mm_wide(lefts, rights)
    grad_step = col_ref[0] + late[...]
    grad_step_ref[0] = grad_step
    change = carry_ref[0] - steps * grad_step
    last = jnp.exp(end) * overlap[...] + jnp.sum(steps * late[...], axis=0, keepdims=True)
    source = lax.broadcasted_iota(jnp.int32, (span, span), 0)
    target = lax.broadcasted_iota(jnp.int32, (span, span), 1)
    from_here = (source <= target).astype(BF16)
    high, low = halves(change)
    lowest = (change - high.astype(F32) - low.astype(F32)).astype(BF16)
    grad_decay_ref[0] = last + (
        mm(from_here, high, NN) + mm(from_here, low, NN) + mm(from_here, lowest, NN)
    )


def outer_part(x, part, b, state, grad_state, running, steps, cols, carries, grad_b, at, before):
    groups, span, group = steps.shape
    heads = groups * group
    count = grad_state.shape[0] // group
    width = x.shape[1] // heads
    states = b.shape[1]
    block = pl.BlockSpec((span, group * width), lambda i, at: (0, at[0] + i))
    table = pl.BlockSpec((1, span, group), lambda i, at: (at[0] + i, 0, 0))
    held = [] if before is None else list(before)
    return pl.pallas_call(
        outer_kernel,
        grid_spec=pltpu.PrefetchScalarGridSpec(
            num_scalar_prefetch=1,
            grid=(count,),
            in_specs=[
                block,
                block,
                whole(span, states),
                pl.BlockSpec((group, states, width), lambda i, at: (at[0] + i, 0, 0)),
                pl.BlockSpec((group, states, width), lambda i, at: (i, 0, 0)),
                table,
                table,
                table,
                table,
                whole(span, states),
            ]
            + [pl.BlockSpec(memory_space=pl.ANY)] * len(held),
            out_specs=[block, whole(span, states), table, table],
            scratch_shapes=[pltpu.VMEM((span, group), F32), pltpu.VMEM((1, group), F32)],
        ),
        out_shape=[
            jax.ShapeDtypeStruct((span, heads * width), BF16),
            jax.ShapeDtypeStruct((span, states), F32),
            jax.ShapeDtypeStruct((groups, span, group), F32),
            jax.ShapeDtypeStruct((groups, span, group), F32),
        ],
        input_output_aliases={11: 0, 12: 2, 13: 3} if held else {},
        compiler_params=PARAMS,
        cost_estimate=cost(
            8 * span * count * group * width * states,
            count * group * width * (8 * span + 8 * states),
        ),
    )(at, x, part, b, state, grad_state, running, steps, cols, carries, grad_b, *held)


def project_kernel(hops, at_ref, *refs):
    count = len(hops)
    pieces, (own_ref, other_ref, send_ref, keep_ref, left) = refs[:count], refs[count:]
    rows = pieces[0].shape[0]
    depth = own_ref.shape[1]

    @pl.when(pl.program_id(0) == 0)
    def _():
        first = pl.multiple_of(at_ref[0] * depth, depth)
        second = pl.multiple_of((1 - at_ref[0]) * depth, depth)
        for place, hop in enumerate(hops):
            left[pl.ds(place * rows, rows), :depth] = pieces[hop][:, pl.ds(first, depth)]
            left[pl.ds(place * rows, rows), depth:] = pieces[hop][:, pl.ds(second, depth)]

    total = mm(left[:, :depth], own_ref[...], NT) + mm(left[:, depth:], other_ref[...], NT)
    middle = rows * (count // 2)
    keep_ref[...] = total[:middle]
    send_ref[...] = total[middle:].astype(BF16)


def partial_sums(pieces, hops, own, other, lane, core):
    rows, both = pieces[0].shape
    depth = own.shape[1]
    half = own.shape[0] // 2
    tile = min(512, half)
    steps = half // tile
    middle = rows * (len(hops) // 2)
    weight = pl.BlockSpec((tile, depth), lambda i, at: (lane * steps + i, 0))
    return pl.pallas_call(
        lambda *refs: project_kernel(hops, *refs),
        grid_spec=pltpu.PrefetchScalarGridSpec(
            num_scalar_prefetch=1,
            grid=(steps,),
            in_specs=[whole(rows, both)] * len(hops) + [weight, weight],
            out_specs=[pl.BlockSpec((middle, tile), lambda i, at: (0, i))] * 2,
            scratch_shapes=[pltpu.VMEM((rows * len(hops), both), BF16)],
        ),
        out_shape=[
            jax.ShapeDtypeStruct((middle, half), BF16),
            jax.ShapeDtypeStruct((middle, half), F32),
        ],
        compiler_params=PARAMS,
        cost_estimate=cost(
            2 * rows * len(hops) * both * half, 2 * both * half + 6 * middle * half
        ),
    )(core, *pieces, own, other)


def finish_kernel(count, *refs):
    keeps, arrived, out_ref = refs[: 2 * count], refs[2 * count : -1], refs[-1]
    steps = pl.num_programs(0) // 2
    for lane in range(2):

        @pl.when(pl.program_id(0) // steps == lane)
        def _():
            start = 0
            for chunk in range(count):
                at = lane * count + chunk
                total = keeps[at][...] + arrived[at][...].astype(F32)
                rows = total.shape[0]
                out_ref[start : start + rows, :] = total.astype(BF16)
                start += rows


def finish(keeps, arrived):
    count = len(keeps) // 2
    half = arrived[0].shape[1]
    span = sum(a.shape[0] for a in arrived) // 2
    tile = min(1024, half)
    steps = half // tile
    place = [lambda i: (0, jnp.minimum(i, steps - 1)), lambda i: (0, jnp.maximum(i - steps, 0))]
    specs = [
        pl.BlockSpec((a.shape[0], tile), place[i // count]) for i, a in enumerate(arrived)
    ]
    return pl.pallas_call(
        lambda *refs: finish_kernel(count, *refs),
        grid=(2 * steps,),
        in_specs=specs + specs,
        out_specs=pl.BlockSpec((span, tile), lambda i: (0, i)),
        out_shape=jax.ShapeDtypeStruct((span, 2 * half), BF16),
        compiler_params=PARAMS,
        cost_estimate=cost(4 * span * half, 16 * span * half),
    )(*keeps, *arrived)


def across(value, hop, chips):
    pairs = [(2 * i + core, 2 * (i ^ hop) + core) for i in range(chips) for core in range(2)]
    return lax.ppermute(value, "seq", pairs)


def other_core(value, chips):
    return lax.ppermute(value, "seq", [(i, i ^ 1) for i in range(2 * chips)])


def orders(chips):
    bits = [1 << i for i in range(chips.bit_length() - 1)]
    return [bits, bits[::-1]]


def sum_over_heads(value):
    count = lax.axis_size("head")
    value = value.astype(BF16)
    terms = [
        lax.ppermute(value, "head", [(i, i ^ hop) for i in range(count)]) if hop else value
        for hop in range(count)
    ]
    terms = [term.astype(F32) for term in terms]
    while len(terms) > 1:
        terms = [terms[i] + terms[i + 1] for i in range(0, len(terms), 2)]
    return terms[0]


def gather_halves(grad_out):
    half = grad_out.shape[0] // 2
    pieces = [grad_out[:half], grad_out[half:]]
    return pieces[0], [lax.all_gather(p, "head", axis=1, tiled=True) for p in pieces]


def blocks_of(full, start, rows, chips, chip):
    both = full.shape[1] // chips
    return [
        lax.dynamic_slice(full, (start, (chip ^ hop) * both), (rows, both)) for hop in range(chips)
    ]


def project(fulls, own, out_weight, other, chips, chip, core, before):
    core_at = core.astype(jnp.int32).reshape(1)
    lanes = []
    for order in orders(chips):
        hops = [0]
        for bit in order[::-1]:
            hops = hops + [hop | bit for hop in hops]
        lanes.append((order, hops))
    waiting = [[], []]

    def reduce(chunk, rows, after):
        sends = []
        for lane, (order, _) in enumerate(lanes):
            keep, send, arrived = waiting[lane][chunk]
            for step, bit in enumerate(order):
                if step:
                    arrived = across(send, bit, chips)
                elif after:
                    arrived = tie(arrived, *after)
                if step < len(order) - 1:
                    keep = keep + arrived.astype(F32)
                    size = keep.shape[0] // 2
                    send = keep[size:].astype(BF16)
                    keep = keep[:size] if size > rows else keep
            waiting[lane][chunk] = (keep, arrived)
            sends.append(send)
        return sends

    half = fulls[0].shape[0]
    rows = [half, half // 2, half // 2]
    count = len(rows)
    for chunk in range(count):
        blocks = [across(block, hop, chips) if hop else block for hop, block in enumerate(own)]
        if chunk == 0:
            blocks = lax.optimization_barrier((*blocks, *before))[:chips]
        if chunk == 1:
            full = tie(fulls[1], waiting[0][0][2], *own)
            own = blocks_of(full, rows[1], rows[2], chips, chip)
            sends = reduce(0, rows[0], own)
            blocks = lax.optimization_barrier((*blocks, *own, *sends))[:chips]
        for lane, (order, hops) in enumerate(lanes):
            send, keep = partial_sums(blocks, hops, out_weight, other, lane, core_at)
            waiting[lane].append((keep, send, across(send, order[0], chips)))
        if chunk == 0:
            full = tie(fulls[1], *[lane[0][1] for lane in waiting])
            own = blocks_of(full, 0, rows[1], chips, chip)
    reduce(count - 2, rows[count - 2], None)
    reduce(count - 1, rows[count - 1], None)
    ends = waiting[0] + waiting[1]
    return finish([keep for keep, _ in ends], [arrived for _, arrived in ends])


def exchange(mine, theirs, ends, chips, chip, core, reverse, fill):
    half = mine.shape[0]
    ends = lax.dynamic_slice_in_dim(ends, core * half, half, 1)
    by_chip = ends.reshape(chips, 2, half)
    own_ends = lax.dynamic_index_in_dim(by_chip, chip, 0, False)
    chip_ends = by_chip[:, 0] + by_chip[:, 1]
    index = jnp.arange(chips)[:, None]
    scale = lambda logs, value: jnp.exp(logs)[:, None, None] * value.astype(F32)

    def carry(source, target):
        before = source > target if reverse else source < target
        inside = (index > jnp.minimum(source, target)) & (index < jnp.maximum(source, target))
        between = jnp.sum(jnp.where(inside, chip_ends, 0.0), axis=0)
        return jnp.where(before, between, -jnp.inf)

    near_first = (core == 0) != reverse
    first = jnp.where(near_first, mine, theirs)
    second = jnp.where(near_first, theirs, mine)
    first_end, second_end = (own_ends[1], own_ends[0]) if reverse else (own_ends[0], own_ends[1])
    chip_state = scale(second_end, first) + second
    lanes = []
    for lane in range(2):
        heads = slice(lane * (half // 2), (lane + 1) * (half // 2))
        lanes.append((heads, {0: chip_state[heads].astype(BF16)}))
    bits = orders(chips)
    for step in range(len(bits[0])):
        last = step == len(bits[0]) - 1
        sent = []
        for order, (heads, items) in zip(bits, lanes):
            if last:
                target = chip ^ order[step]
                total = sum(scale(carry(chip ^ o, target)[heads], i) for o, i in items.items())
                sent.append({0: total.astype(BF16)})
            else:
                sent.append(dict(items))
        done = fill(step, [item for items in sent for item in items.values()])
        for order, (heads, items), going in zip(bits, lanes, sent):
            for o, item in going.items():
                items[o | order[step]] = across(item, order[step], chips)
        fresh = [(items, o | order[step]) for order, (_, items), going in zip(bits, lanes, sent) for o in going]
        values = lax.optimization_barrier((*[items[o] for items, o in fresh], *done))
        for (items, o), value in zip(fresh, values):
            items[o] = value
    totals = []
    for order, (heads, items) in zip(bits, lanes):
        arrived = items.pop(order[-1])
        total = sum(scale(carry(chip ^ o, chip)[heads], i) for o, i in items.items())
        totals.append(total + arrived.astype(F32))
    total = jnp.concatenate(totals, axis=0)
    after = scale(first_end, total) + first
    return jnp.where(near_first, total, after), jnp.where(near_first, after, total)


def local(grad_out, out_weight, ssm_input, step_size, log_decay, b_in, c_in, skip):
    place_on_seq = lax.axis_index("seq")
    chips = lax.axis_size("seq") // 2
    chip, core = place_on_seq // 2, place_on_seq % 2
    span, heads = step_size.shape
    width = ssm_input.shape[1] // heads
    group = min(GROUP, heads // 2)
    groups = heads // group
    by_group = lambda t: t.reshape(span, groups, group).transpose(1, 0, 2)
    flat = lambda t: t.transpose(1, 0, 2).reshape(span, heads)
    mine_at = (core * (groups // 2)).astype(jnp.int32).reshape(1)
    other_at = ((1 - core) * (groups // 2)).astype(jnp.int32).reshape(1)

    first_rows, fulls = gather_halves(grad_out)
    log_decay, step_size, b_in, c_in, _ = lax.optimization_barrier(
        (log_decay, step_size, b_in, c_in, first_rows)
    )
    other_weight = other_core(out_weight, chips)
    upto = jnp.tril(jnp.ones((span, span), F32))
    running = jnp.dot(upto, log_decay, precision=HIGH)
    ends = lax.all_gather(running[-1], "seq")
    tail = jnp.exp(running[-1:] - running)
    rise = by_group(jnp.exp(running))
    running_g = by_group(running)
    running_t = running.T.reshape(groups, group, span)
    steps_g = by_group(step_size)
    skip_rows = jnp.broadcast_to(skip.reshape(groups, group, 1), (groups, group, width))
    b_rows, c_rows = b_in.T, c_in.T

    def span_both(values, scale, rows_t):
        to_other = span_states(values, scale, rows_t, other_at, groups // 2)
        theirs = other_core(to_other, chips)
        return span_states(values, scale, rows_t, mine_at, groups // 2), theirs

    own = []

    def first_blocks(step, sent):
        if step < chips.bit_length() - 2:
            return []
        own[:] = blocks_of(tie(fulls[0], *sent), 0, span // 2, chips, chip)
        return own

    mine, theirs = span_both(ssm_input, by_group(step_size * tail), b_rows)
    for_mine, for_theirs = exchange(
        mine, theirs, ends, chips, chip, core, False, first_blocks
    )
    arrived = other_core(for_theirs, chips)
    incoming = jnp.where(
        core == 0,
        jnp.concatenate([for_mine, arrived], axis=0),
        jnp.concatenate([arrived, for_mine], axis=0),
    )
    decay, weight, cross = decays(tie(running_g, *own), running_t, b_in, c_in)
    before = [incoming, cross, steps_g, skip_rows, rise, c_rows]
    grad_y = project(fulls, own, out_weight, other_weight, chips, chip, core, before)

    counts = [0, groups - groups // 2, groups // 2]
    held = ()

    def fill(step, sent):
        nonlocal held
        count = counts[step] if step < len(counts) else 0
        if count:
            held = inner_part(
                ssm_input, grad_y, b_in, c_in, tie(rise, *sent), steps_g, skip_rows, incoming,
                decay, weight, cross, sum(counts[:step]), count, held, step == len(counts) - 1,
            )
        return list(held)

    mine, theirs = span_both(grad_y, rise, c_rows)
    theirs = tie(theirs, *fill(0, [mine]))
    for_mine, for_theirs = exchange(
        mine, theirs, ends, chips, chip, core, True, lambda step, sent: fill(step + 1, sent)
    )
    for_other = other_core(for_theirs, chips)
    part, cols, carries, grad_b, grad_c = held
    grad_c = sum_over_heads(grad_c)
    shared = (running_g, steps_g, cols, carries)
    grad_x, grad_b, grad_step, grad_decay = outer_part(
        ssm_input, part, b_in, incoming, for_mine, *shared, grad_b, mine_at, None
    )
    grad_x, grad_b, grad_step, grad_decay = outer_part(
        ssm_input, part, b_in, incoming, for_other, *shared, grad_b, other_at,
        (grad_x, grad_step, grad_decay),
    )
    grad_b = sum_over_heads(grad_b)
    return (grad_x, flat(grad_step), flat(grad_decay), grad_b, grad_c)


def solution(mesh):
    in_specs = (
        P("seq", "head"),
        P("head", "seq"),
        P("seq", "head"),
        P("seq", "head"),
        P("seq", "head"),
        P("seq", None),
        P("seq", None),
        P("head"),
    )
    out_specs = (
        P("seq", "head"),
        P("seq", "head"),
        P("seq", "head"),
        P("seq", None),
        P("seq", None),
    )
    return jax.shard_map(local, mesh=mesh, in_specs=in_specs, out_specs=out_specs, check_vma=False)
```

```python
import jax
import jax.numpy as jnp
from jax import lax
from jax.experimental import pallas as pl
from jax.experimental.pallas import tpu as pltpu
from jax.sharding import PartitionSpec as P

BF16 = jnp.bfloat16
F32 = jnp.float32
HIGH = lax.Precision.HIGHEST
GROUP = 8
NN = (((1,), (0,)), ((), ()))
NT = (((1,), (1,)), ((), ()))
TN = (((0,), (0,)), ((), ()))
PARAMS = pltpu.CompilerParams(vmem_limit_bytes=28 << 20)


def mm(a, b, dims):
    return lax.dot_general(a, b, dims, preferred_element_type=F32)


def halves(a):
    high = a.astype(BF16)
    return high, (a - high.astype(F32)).astype(BF16)


def mm_right(a, b):
    width = b.shape[1]
    both = mm(a, jnp.concatenate(halves(b), axis=1), NN)
    return both[:, :width] + both[:, width:]


def mm_wide(lefts, rights):
    left = [part for a in lefts for part in halves(a)]
    right = [part for b in rights for part in [b.astype(BF16)] * 2]
    return mm(jnp.concatenate(left, axis=1), jnp.concatenate(right, axis=1), NT)


def whole(*shape):
    return pl.BlockSpec(shape, lambda i, at: (0,) * len(shape))


def tie(value, *before):
    return lax.optimization_barrier((value, *before))[0]


def cost(flops, size, exps=0):
    scale = 256
    return pl.CostEstimate(
        flops=flops // scale, bytes_accessed=size // scale, transcendentals=exps // scale
    )


def states_kernel(at_ref, v_ref, scale_ref, rows_ref, out_ref):
    del at_ref
    group = scale_ref.shape[2]
    width = v_ref.shape[1] // group
    for j in range(group):
        scaled = v_ref[:, j * width : (j + 1) * width].astype(F32) * scale_ref[0, :, j : j + 1]
        out_ref[j] = mm_right(rows_ref[...], scaled)


def span_states(values, scale, rows_t, at, count):
    groups, span, group = scale.shape
    width = values.shape[1] // (groups * group)
    states = rows_t.shape[0]
    return pl.pallas_call(
        states_kernel,
        grid_spec=pltpu.PrefetchScalarGridSpec(
            num_scalar_prefetch=1,
            grid=(count,),
            in_specs=[
                pl.BlockSpec((span, group * width), lambda i, at: (0, at[0] + i)),
                pl.BlockSpec((1, span, group), lambda i, at: (at[0] + i, 0, 0)),
                whole(states, span),
            ],
            out_specs=pl.BlockSpec((group, states, width), lambda i, at: (i, 0, 0)),
        ),
        out_shape=jax.ShapeDtypeStruct((count * group, states, width), F32),
        compiler_params=PARAMS,
        cost_estimate=cost(
            4 * span * count * group * width * states,
            count * group * width * (2 * span + 4 * states),
        ),
    )(at, values, scale, rows_t)


def decay_kernel(run_ref, run_t_ref, b_ref, c_ref, decay_ref, weight_ref, cross_ref):
    group = run_ref.shape[2]
    span = run_ref.shape[1]

    @pl.when(pl.program_id(0) == 0)
    def _():
        cross_ref[...] = mm(b_ref[...], c_ref[...], NT)

    source = lax.broadcasted_iota(jnp.int32, (span, span), 0)
    target = lax.broadcasted_iota(jnp.int32, (span, span), 1)
    causal = source <= target
    for j in range(group):
        gap = run_t_ref[0, j : j + 1, :] - run_ref[0, :, j : j + 1]
        decay = jnp.exp(jnp.where(causal, gap, -jnp.inf))
        decay_ref[j] = decay
        high, low = halves(decay * cross_ref[...])
        weight_ref[j, :, :span] = high
        weight_ref[j, :, span:] = low


def decays(running, running_t, b, c):
    groups, span, group = running.shape
    states = b.shape[1]
    fixed = lambda *shape: pl.BlockSpec(shape, lambda i: (0,) * len(shape))
    return pl.pallas_call(
        decay_kernel,
        grid=(groups,),
        in_specs=[
            pl.BlockSpec((1, span, group), lambda i: (i, 0, 0)),
            pl.BlockSpec((1, group, span), lambda i: (i, 0, 0)),
            fixed(span, states),
            fixed(span, states),
        ],
        out_specs=[
            pl.BlockSpec((group, span, span), lambda i: (i, 0, 0)),
            pl.BlockSpec((group, span, 2 * span), lambda i: (i, 0, 0)),
            fixed(span, span),
        ],
        out_shape=[
            jax.ShapeDtypeStruct((groups * group, span, span), F32),
            jax.ShapeDtypeStruct((groups * group, span, 2 * span), BF16),
            jax.ShapeDtypeStruct((span, span), F32),
        ],
        compiler_params=PARAMS,
        cost_estimate=cost(
            8 * groups * group * span * span,
            8 * groups * group * span * span,
            groups * group * span * span,
        ),
    )(running, running_t, b, c)


def inner_kernel(
    first, last, at_ref, x_ref, y_ref, b_ref, c_ref, rise_ref, step_ref, skip_ref,
    state_ref, decay_ref, weight_ref, cross_ref, *rest,
):
    del at_ref
    held = rest[: 0 if first else 5]
    partial_ref, col_ref, carry_ref, mix_ref, grad_c_ref, rows = rest[len(held) :]
    group = step_ref.shape[2]
    width = x_ref.shape[1] // group

    @pl.when(pl.program_id(0) == 0)
    def _():
        mix_ref[...] = jnp.zeros_like(mix_ref) if first else held[3][...]
        grad_c_ref[...] = jnp.zeros_like(grad_c_ref) if first else held[4][...]

    lefts, rights = [], []
    for j in range(group):
        columns = slice(j * width, (j + 1) * width)
        y = y_ref[:, columns]
        x_wide = x_ref[:, columns].astype(F32)
        y_wide = y.astype(F32)
        step_col = step_ref[0, :, j : j + 1]
        stepped = jnp.concatenate(halves(x_wide * step_col), axis=1)
        pairs = decay_ref[j] * mm(stepped, jnp.concatenate([y, y], axis=1), NT)
        mix_ref[...] += pairs
        rows[j : j + 1, :] = jnp.sum(pairs * cross_ref[...], axis=0, keepdims=True)
        inner = mm(weight_ref[j], jnp.concatenate([y, y], axis=0), NN)
        col_ref[0, :, j : j + 1] = jnp.sum(x_wide * inner, axis=1, keepdims=True)
        partial_ref[:, columns] = step_col * inner + skip_ref[0, j : j + 1, :] * y_wide
        state = state_ref[j]
        scaled = y_wide * rise_ref[0, :, j : j + 1]
        lefts.append(scaled)
        rights.append(state)
        carry_ref[0, :, j : j + 1] = jnp.sum(
            scaled * mm_right(c_ref[...], state), axis=1, keepdims=True
        )
    grad_c_ref[...] += mm_wide(lefts, rights)
    carry_ref[0] += rows[...].T

    if last:

        @pl.when(pl.program_id(0) == pl.num_programs(0) - 1)
        def _():
            high, low = halves(mix_ref[...])
            mix_ref[...] = mm(high, c_ref[...], NN) + mm(low, c_ref[...], NN)
            grad_c_ref[...] += mm(high, b_ref[...], TN) + mm(low, b_ref[...], TN)


def inner_part(
    x, y, b, c, rise, steps, skip_rows, incoming, decay, weight, cross, at, count, held, last
):
    groups, span, group = steps.shape
    heads = groups * group
    width = x.shape[1] // heads
    states = b.shape[1]
    block = pl.BlockSpec((span, group * width), lambda i, at: (0, at[0] + i))
    table = pl.BlockSpec((1, span, group), lambda i, at: (at[0] + i, 0, 0))
    per_head = lambda *shape: pl.BlockSpec((group, *shape), lambda i, at: (at[0] + i, 0, 0))
    any_place = pl.BlockSpec(memory_space=pl.ANY)
    return pl.pallas_call(
        lambda *refs: inner_kernel(not held, last, *refs),
        grid_spec=pltpu.PrefetchScalarGridSpec(
            num_scalar_prefetch=1,
            grid=(count,),
            in_specs=[
                block,
                block,
                whole(span, states),
                whole(span, states),
                table,
                table,
                pl.BlockSpec((1, group, width), lambda i, at: (at[0] + i, 0, 0)),
                per_head(states, width),
                per_head(span, span),
                per_head(span, 2 * span),
                whole(span, span),
            ]
            + ([any_place] * 3 + [whole(span, states)] * 2 if held else []),
            out_specs=[block, table, table, whole(span, states), whole(span, states)],
            scratch_shapes=[pltpu.VMEM((group, span), F32)],
        ),
        out_shape=[
            jax.ShapeDtypeStruct((span, heads * width), F32),
            jax.ShapeDtypeStruct((groups, span, group), F32),
            jax.ShapeDtypeStruct((groups, span, group), F32),
            jax.ShapeDtypeStruct((span, states), F32),
            jax.ShapeDtypeStruct((span, states), F32),
        ],
        input_output_aliases={12: 0, 13: 1, 14: 2} if held else {},
        compiler_params=PARAMS,
        cost_estimate=cost(
            14 * span * count * group * width * states,
            count * group * (8 * span * width + 4 * width * states + 8 * span * span),
        ),
    )(
        jnp.full((1,), at, jnp.int32), x, y, b, c, rise, steps, skip_rows, incoming,
        decay, weight, cross, *held,
    )


def outer_kernel(
    at_ref, x_ref, part_ref, b_ref, state_ref, grad_state_ref, run_ref, step_ref,
    col_ref, carry_ref, grad_b_in_ref, *rest,
):
    del at_ref
    grad_x_ref, grad_b_ref, grad_step_ref, grad_decay_ref, late, overlap = rest[-6:]
    group = step_ref.shape[2]
    span = x_ref.shape[0]
    width = x_ref.shape[1] // group

    @pl.when(pl.program_id(0) == 0)
    def _():
        grad_b_ref[...] = grad_b_in_ref[...]

    running = run_ref[0]
    end = running[span - 1 : span, :]
    tails = jnp.exp(end - running)
    steps = step_ref[0]
    lefts, rights = [], []
    for j in range(group):
        columns = slice(j * width, (j + 1) * width)
        tail_col = tails[:, j : j + 1]
        step_col = steps[:, j : j + 1]
        grad_state = grad_state_ref[j]
        x = x_ref[:, columns].astype(F32)
        outer = mm_right(b_ref[...], grad_state) * tail_col
        late[:, j : j + 1] = jnp.sum(x * outer, axis=1, keepdims=True)
        grad_x_ref[:, columns] = (part_ref[:, columns] + step_col * outer).astype(BF16)
        lefts.append(x * (step_col * tail_col))
        rights.append(grad_state)
        shared = jnp.sum(grad_state * state_ref[j], axis=0, keepdims=True)
        overlap[:, j : j + 1] = jnp.sum(shared, axis=1, keepdims=True)

    grad_b_ref[...] += mm_wide(lefts, rights)
    grad_step = col_ref[0] + late[...]
    grad_step_ref[0] = grad_step
    change = carry_ref[0] - steps * grad_step
    last = jnp.exp(end) * overlap[...] + jnp.sum(steps * late[...], axis=0, keepdims=True)
    source = lax.broadcasted_iota(jnp.int32, (span, span), 0)
    target = lax.broadcasted_iota(jnp.int32, (span, span), 1)
    from_here = (source <= target).astype(BF16)
    high, low = halves(change)
    lowest = (change - high.astype(F32) - low.astype(F32)).astype(BF16)
    grad_decay_ref[0] = last + (
        mm(from_here, high, NN) + mm(from_here, low, NN) + mm(from_here, lowest, NN)
    )


def outer_part(x, part, b, state, grad_state, running, steps, cols, carries, grad_b, at, before):
    groups, span, group = steps.shape
    heads = groups * group
    count = grad_state.shape[0] // group
    width = x.shape[1] // heads
    states = b.shape[1]
    block = pl.BlockSpec((span, group * width), lambda i, at: (0, at[0] + i))
    table = pl.BlockSpec((1, span, group), lambda i, at: (at[0] + i, 0, 0))
    held = [] if before is None else list(before)
    return pl.pallas_call(
        outer_kernel,
        grid_spec=pltpu.PrefetchScalarGridSpec(
            num_scalar_prefetch=1,
            grid=(count,),
            in_specs=[
                block,
                block,
                whole(span, states),
                pl.BlockSpec((group, states, width), lambda i, at: (at[0] + i, 0, 0)),
                pl.BlockSpec((group, states, width), lambda i, at: (i, 0, 0)),
                table,
                table,
                table,
                table,
                whole(span, states),
            ]
            + [pl.BlockSpec(memory_space=pl.ANY)] * len(held),
            out_specs=[block, whole(span, states), table, table],
            scratch_shapes=[pltpu.VMEM((span, group), F32), pltpu.VMEM((1, group), F32)],
        ),
        out_shape=[
            jax.ShapeDtypeStruct((span, heads * width), BF16),
            jax.ShapeDtypeStruct((span, states), F32),
            jax.ShapeDtypeStruct((groups, span, group), F32),
            jax.ShapeDtypeStruct((groups, span, group), F32),
        ],
        input_output_aliases={11: 0, 12: 2, 13: 3} if held else {},
        compiler_params=PARAMS,
        cost_estimate=cost(
            8 * span * count * group * width * states,
            count * group * width * (8 * span + 8 * states),
        ),
    )(at, x, part, b, state, grad_state, running, steps, cols, carries, grad_b, *held)


def project_kernel(hops, at_ref, *refs):
    count = len(hops)
    pieces, (own_ref, other_ref, send_ref, keep_ref, left) = refs[:count], refs[count:]
    rows = pieces[0].shape[0]
    depth = own_ref.shape[1]

    @pl.when(pl.program_id(0) == 0)
    def _():
        first = pl.multiple_of(at_ref[0] * depth, depth)
        second = pl.multiple_of((1 - at_ref[0]) * depth, depth)
        for place, hop in enumerate(hops):
            left[pl.ds(place * rows, rows), :depth] = pieces[hop][:, pl.ds(first, depth)]
            left[pl.ds(place * rows, rows), depth:] = pieces[hop][:, pl.ds(second, depth)]

    total = mm(left[:, :depth], own_ref[...], NT) + mm(left[:, depth:], other_ref[...], NT)
    middle = rows * (count // 2)
    keep_ref[...] = total[:middle]
    send_ref[...] = total[middle:].astype(BF16)


def partial_sums(pieces, hops, own, other, lane, core):
    rows, both = pieces[0].shape
    depth = own.shape[1]
    half = own.shape[0] // 2
    tile = min(512, half)
    steps = half // tile
    middle = rows * (len(hops) // 2)
    weight = pl.BlockSpec((tile, depth), lambda i, at: (lane * steps + i, 0))
    return pl.pallas_call(
        lambda *refs: project_kernel(hops, *refs),
        grid_spec=pltpu.PrefetchScalarGridSpec(
            num_scalar_prefetch=1,
            grid=(steps,),
            in_specs=[whole(rows, both)] * len(hops) + [weight, weight],
            out_specs=[pl.BlockSpec((middle, tile), lambda i, at: (0, i))] * 2,
            scratch_shapes=[pltpu.VMEM((rows * len(hops), both), BF16)],
        ),
        out_shape=[
            jax.ShapeDtypeStruct((middle, half), BF16),
            jax.ShapeDtypeStruct((middle, half), F32),
        ],
        compiler_params=PARAMS,
        cost_estimate=cost(
            2 * rows * len(hops) * both * half, 2 * both * half + 6 * middle * half
        ),
    )(core, *pieces, own, other)


def finish_kernel(count, *refs):
    keeps, arrived, out_ref = refs[: 2 * count], refs[2 * count : -1], refs[-1]
    steps = pl.num_programs(0) // 2
    for lane in range(2):

        @pl.when(pl.program_id(0) // steps == lane)
        def _():
            start = 0
            for chunk in range(count):
                at = lane * count + chunk
                total = keeps[at][...] + arrived[at][...].astype(F32)
                rows = total.shape[0]
                out_ref[start : start + rows, :] = total.astype(BF16)
                start += rows


def finish(keeps, arrived):
    count = len(keeps) // 2
    half = arrived[0].shape[1]
    span = sum(a.shape[0] for a in arrived) // 2
    tile = min(1024, half)
    steps = half // tile
    place = [lambda i: (0, jnp.minimum(i, steps - 1)), lambda i: (0, jnp.maximum(i - steps, 0))]
    specs = [
        pl.BlockSpec((a.shape[0], tile), place[i // count]) for i, a in enumerate(arrived)
    ]
    return pl.pallas_call(
        lambda *refs: finish_kernel(count, *refs),
        grid=(2 * steps,),
        in_specs=specs + specs,
        out_specs=pl.BlockSpec((span, tile), lambda i: (0, i)),
        out_shape=jax.ShapeDtypeStruct((span, 2 * half), BF16),
        compiler_params=PARAMS,
        cost_estimate=cost(4 * span * half, 16 * span * half),
    )(*keeps, *arrived)


def across(value, hop, chips):
    pairs = [(2 * i + core, 2 * (i ^ hop) + core) for i in range(chips) for core in range(2)]
    return lax.ppermute(value, "seq", pairs)


def other_core(value, chips):
    return lax.ppermute(value, "seq", [(i, i ^ 1) for i in range(2 * chips)])


def orders(chips):
    bits = [1 << i for i in range(chips.bit_length() - 1)]
    return [bits, bits[::-1]]


def sum_over_heads(value):
    count = lax.axis_size("head")
    value = value.astype(BF16)
    terms = [
        lax.ppermute(value, "head", [(i, i ^ hop) for i in range(count)]) if hop else value
        for hop in range(count)
    ]
    terms = [term.astype(F32) for term in terms]
    while len(terms) > 1:
        terms = [terms[i] + terms[i + 1] for i in range(0, len(terms), 2)]
    return terms[0]


def gather_halves(grad_out):
    half = grad_out.shape[0] // 2
    pieces = [grad_out[:half], grad_out[half:]]
    return pieces[0], [lax.all_gather(p, "head", axis=1, tiled=True) for p in pieces]


def blocks_of(full, start, rows, chips, chip):
    both = full.shape[1] // chips
    return [
        lax.dynamic_slice(full, (start, (chip ^ hop) * both), (rows, both)) for hop in range(chips)
    ]


def project(fulls, own, out_weight, other, chips, chip, core, before):
    core_at = core.astype(jnp.int32).reshape(1)
    lanes = []
    for order in orders(chips):
        hops = [0]
        for bit in order[::-1]:
            hops = hops + [hop | bit for hop in hops]
        lanes.append((order, hops))
    waiting = [[], []]

    def reduce(chunk, rows, after):
        sends = []
        for lane, (order, _) in enumerate(lanes):
            keep, send, arrived = waiting[lane][chunk]
            for step, bit in enumerate(order):
                if step:
                    arrived = across(send, bit, chips)
                elif after:
                    arrived = tie(arrived, *after, *sends)
                if step < len(order) - 1:
                    keep = keep + arrived.astype(F32)
                    size = keep.shape[0] // 2
                    send = keep[size:].astype(BF16)
                    keep = keep[:size] if size > rows else keep
            waiting[lane][chunk] = (keep, arrived)
            sends.append(send)
        return sends

    half = fulls[0].shape[0]
    rows = [half, half // 2, half // 2]
    count = len(rows)
    for chunk in range(count):
        blocks = [across(block, hop, chips) if hop else block for hop, block in enumerate(own)]
        if chunk == 0:
            blocks = lax.optimization_barrier((*blocks, *before))[:chips]
        if chunk == 1:
            full = tie(fulls[1], waiting[0][0][2], *own)
            own = blocks_of(full, rows[1], rows[2], chips, chip)
            sends = reduce(0, rows[0], own)
            blocks = lax.optimization_barrier((*blocks, *own, *sends))[:chips]
        for lane, (order, hops) in enumerate(lanes):
            send, keep = partial_sums(blocks, hops, out_weight, other, lane, core_at)
            waiting[lane].append((keep, send, across(send, order[0], chips)))
        if chunk == 0:
            full = tie(fulls[1], *[lane[0][1] for lane in waiting])
            own = blocks_of(full, 0, rows[1], chips, chip)
    reduce(count - 2, rows[count - 2], None)
    reduce(count - 1, rows[count - 1], None)
    ends = waiting[0] + waiting[1]
    return finish([keep for keep, _ in ends], [arrived for _, arrived in ends])


def exchange(mine, theirs, ends, chips, chip, core, reverse, fill):
    half = mine.shape[0]
    ends = lax.dynamic_slice_in_dim(ends, core * half, half, 1)
    by_chip = ends.reshape(chips, 2, half)
    own_ends = lax.dynamic_index_in_dim(by_chip, chip, 0, False)
    chip_ends = by_chip[:, 0] + by_chip[:, 1]
    index = jnp.arange(chips)[:, None]
    scale = lambda logs, value: jnp.exp(logs)[:, None, None] * value.astype(F32)

    def carry(source, target):
        before = source > target if reverse else source < target
        inside = (index > jnp.minimum(source, target)) & (index < jnp.maximum(source, target))
        between = jnp.sum(jnp.where(inside, chip_ends, 0.0), axis=0)
        return jnp.where(before, between, -jnp.inf)

    near_first = (core == 0) != reverse
    first = jnp.where(near_first, mine, theirs)
    second = jnp.where(near_first, theirs, mine)
    first_end, second_end = (own_ends[1], own_ends[0]) if reverse else (own_ends[0], own_ends[1])
    chip_state = scale(second_end, first) + second
    lanes = []
    for lane in range(2):
        heads = slice(lane * (half // 2), (lane + 1) * (half // 2))
        lanes.append((heads, {0: chip_state[heads].astype(BF16)}))
    bits = orders(chips)
    for step in range(len(bits[0])):
        last = step == len(bits[0]) - 1
        sent = []
        for order, (heads, items) in zip(bits, lanes):
            if last:
                target = chip ^ order[step]
                total = sum(scale(carry(chip ^ o, target)[heads], i) for o, i in items.items())
                sent.append({0: total.astype(BF16)})
            else:
                sent.append(dict(items))
        done = fill(step, [item for items in sent for item in items.values()])
        for order, (heads, items), going in zip(bits, lanes, sent):
            for o, item in going.items():
                items[o | order[step]] = across(item, order[step], chips)
        fresh = [(items, o | order[step]) for order, (_, items), going in zip(bits, lanes, sent) for o in going]
        values = lax.optimization_barrier((*[items[o] for items, o in fresh], *done))
        for (items, o), value in zip(fresh, values):
            items[o] = value
    totals = []
    for order, (heads, items) in zip(bits, lanes):
        arrived = items.pop(order[-1])
        total = sum(scale(carry(chip ^ o, chip)[heads], i) for o, i in items.items())
        totals.append(total + arrived.astype(F32))
    total = jnp.concatenate(totals, axis=0)
    after = scale(first_end, total) + first
    return jnp.where(near_first, total, after), jnp.where(near_first, after, total)


def local(grad_out, out_weight, ssm_input, step_size, log_decay, b_in, c_in, skip):
    place_on_seq = lax.axis_index("seq")
    chips = lax.axis_size("seq") // 2
    chip, core = place_on_seq // 2, place_on_seq % 2
    span, heads = step_size.shape
    width = ssm_input.shape[1] // heads
    group = min(GROUP, heads // 2)
    groups = heads // group
    by_group = lambda t: t.reshape(span, groups, group).transpose(1, 0, 2)
    flat = lambda t: t.transpose(1, 0, 2).reshape(span, heads)
    mine_at = (core * (groups // 2)).astype(jnp.int32).reshape(1)
    other_at = ((1 - core) * (groups // 2)).astype(jnp.int32).reshape(1)

    first_rows, fulls = gather_halves(grad_out)
    log_decay, step_size, b_in, c_in, _ = lax.optimization_barrier(
        (log_decay, step_size, b_in, c_in, first_rows)
    )
    other_weight = other_core(out_weight, chips)
    upto = jnp.tril(jnp.ones((span, span), F32))
    running = jnp.dot(upto, log_decay, precision=HIGH)
    ends = lax.all_gather(running[-1], "seq")
    tail = jnp.exp(running[-1:] - running)
    rise = by_group(jnp.exp(running))
    running_g = by_group(running)
    running_t = running.T.reshape(groups, group, span)
    steps_g = by_group(step_size)
    skip_rows = jnp.broadcast_to(skip.reshape(groups, group, 1), (groups, group, width))
    b_rows, c_rows = b_in.T, c_in.T

    def span_both(values, scale, rows_t):
        to_other = span_states(values, scale, rows_t, other_at, groups // 2)
        theirs = other_core(to_other, chips)
        return span_states(values, scale, rows_t, mine_at, groups // 2), theirs

    own = []

    def first_blocks(step, sent):
        if step < chips.bit_length() - 2:
            return []
        own[:] = blocks_of(tie(fulls[0], other_weight, *sent), 0, span // 2, chips, chip)
        return own

    mine, theirs = span_both(ssm_input, by_group(step_size * tail), b_rows)
    for_mine, for_theirs = exchange(
        mine, theirs, ends, chips, chip, core, False, first_blocks
    )
    arrived = other_core(for_theirs, chips)
    incoming = jnp.where(
        core == 0,
        jnp.concatenate([for_mine, arrived], axis=0),
        jnp.concatenate([arrived, for_mine], axis=0),
    )
    decay, weight, cross = decays(tie(running_g, *own), running_t, b_in, c_in)
    before = [incoming, cross, steps_g, skip_rows, rise, c_rows]
    grad_y = project(fulls, own, out_weight, other_weight, chips, chip, core, before)

    counts = [0, groups - groups // 2, groups // 2]
    held = ()

    def fill(step, sent):
        nonlocal held
        count = counts[step] if step < len(counts) else 0
        if count:
            held = inner_part(
                ssm_input, grad_y, b_in, c_in, tie(rise, *sent), steps_g, skip_rows, incoming,
                decay, weight, cross, sum(counts[:step]), count, held, step == len(counts) - 1,
            )
        return list(held)

    mine, theirs = span_both(grad_y, rise, c_rows)
    theirs = tie(theirs, *fill(0, [mine]))
    for_mine, for_theirs = exchange(
        mine, theirs, ends, chips, chip, core, True, lambda step, sent: fill(step + 1, sent)
    )
    for_other = other_core(for_theirs, chips)
    part, cols, carries, grad_b, grad_c = held
    grad_c = sum_over_heads(grad_c)
    shared = (running_g, steps_g, cols, carries)
    grad_x, grad_b, grad_step, grad_decay = outer_part(
        ssm_input, part, b_in, incoming, for_mine, *shared, grad_b, mine_at, None
    )
    grad_x, grad_b, grad_step, grad_decay = outer_part(
        ssm_input, part, b_in, incoming, for_other, *shared, grad_b, other_at,
        (grad_x, grad_step, grad_decay),
    )
    grad_b = sum_over_heads(grad_b)
    return (grad_x, flat(grad_step), flat(grad_decay), grad_b, grad_c)


def solution(mesh):
    in_specs = (
        P("seq", "head"),
        P("head", "seq"),
        P("seq", "head"),
        P("seq", "head"),
        P("seq", "head"),
        P("seq", None),
        P("seq", None),
        P("head"),
    )
    out_specs = (
        P("seq", "head"),
        P("seq", "head"),
        P("seq", "head"),
        P("seq", None),
        P("seq", None),
    )
    return jax.shard_map(local, mesh=mesh, in_specs=in_specs, out_specs=out_specs, check_vma=False)
```
